128 devices in a mesh: rep: 8 (over z, y_lo), tp: 16 (over x, y_hi, core).
Axes of the slice: x: 4, y: 4 (y_hi: 2, y_lo: 2; y = y_hi * 2 + y_lo), z: 4, core: 2. Of those that a mesh axis runs over, the one named last changes fastest.
Arguments:
- exp_hidden: bfloat16 [512, 8192], P('rep', 'tp'), may hold values from -160 to 160
- exp_pre_gain: float32 [8192], P('tp'), may hold values from 0.25 to 1.75
- exp_gate: bfloat16 [8192, 28672], P('tp', 'rep'), may hold values from -0.0625 to 0.0625
- exp_up: bfloat16 [8192, 28672], P('tp', 'rep'), may hold values from -0.0625 to 0.0625
- exp_down: bfloat16 [28672, 8192], P('rep', 'tp'), may hold values from -0.03125 to 0.03125
- exp_out_gain: float32 [8192], P('tp'), may hold values from 0.25 to 1.75
- exp_head: bfloat16 [8192, 65536], P(None, ('rep', 'tp')), may hold values from -10 to 10
- ama_hidden: bfloat16 [512, 4096], P('rep', 'tp'), may hold values from -160 to 160
- ama_out_gain: float32 [4096], P('tp'), may hold values from 0.25 to 1.75
- ama_head: bfloat16 [4096, 65536], P(None, ('rep', 'tp')), may hold values from -10 to 10
- logit_scale: float32 [512], replicated, may hold values from 0.25 to 3
- prompt_of: int32 [512], replicated, may hold values from 0 to 15
- prior_picks: int32 [16, 24], replicated, may hold values from 0 to 65535
- valid_mask: int32 [65536], P(('rep', 'tp')), may hold values 0 or 1
Outputs:
- scores: float32 [512, 65536], P(None, ('rep', 'tp'))
- beam_best: float32 [512], replicated
The draws below stay inside these ranges and needn't reach their ends.
All inputs are finite; a program needn't handle non-finite values. No bound on the sum of `valid_mask` on one device may be relied on, other than what follows from the above.
Results may differ from the reference program's by a relative error of at most 0.0034.
Values may be sent and summed in bfloat16 or wider, within the bound.
A program may use at most 128 MiB of HBM per device.

```python
import jax
import jax.numpy as jnp
from jax import lax

DE = 8192
FFE = 28672
DA = 4096
VOCAB = 65536
PICKS = 24
BEAMS = 512
PROMPTS = 16


favored_count = 16


def favored_entries(key):
    return jax.random.randint(jax.random.fold_in(key, 21), (favored_count,), 0, VOCAB)


def feature_rows(key, rows, width):
    first, second = jax.random.split(key, 2)
    values = jax.random.normal(first, (rows, width), jnp.float32)
    rising = 0.6 + 1.2 * jnp.arange(width, dtype=jnp.float32) / width
    rough = jnp.exp(jax.random.uniform(second, (width,), jnp.float32, -0.35, 0.35))
    values = values * rising[None, :] * rough[None, :]
    return jnp.clip(values, -160.0, 160.0).astype(jnp.bfloat16)


def head_columns(base_key, key, width, entries):
    first = jax.random.fold_in(key, 0)
    second = jax.random.fold_in(key, 1)
    fifth = jax.random.fold_in(key, 4)
    values = jax.random.normal(first, (width, entries), jnp.float32) / jnp.sqrt(width * 1.0)
    rising = 1.0 + jnp.arange(entries, dtype=jnp.float32) / entries
    rough = jnp.exp(jax.random.uniform(second, (entries,), jnp.float32, -0.3, 0.3))
    column_scale = rising * rough
    favored = favored_entries(base_key)
    entry_ids = jnp.arange(entries, dtype=jnp.int32)
    is_favored = jnp.any(entry_ids[:, None] == favored[None, :], axis=1)
    lift = jnp.exp(jax.random.uniform(fifth, (entries,), jnp.float32, 1.4, 1.8))
    column_scale = jnp.where(is_favored, lift * rising * rough, column_scale)
    return jnp.clip(values * column_scale[None, :], -10.0, 10.0).astype(jnp.bfloat16)


def draw_exp_hidden(key, part):
    return feature_rows(jax.random.fold_in(key, 11), BEAMS, DE)


def draw_ama_hidden(key, part):
    return feature_rows(jax.random.fold_in(key, 12), BEAMS, DA)


def draw_exp_head(key, part):
    return head_columns(key, jax.random.fold_in(key, 13), DE, VOCAB)


def draw_ama_head(key, part):
    return head_columns(key, jax.random.fold_in(key, 14), DA, VOCAB)


def draw_logit_scale(key, part):
    inner = jax.random.fold_in(key, 15)
    return jnp.exp(jax.random.uniform(inner, (BEAMS,), jnp.float32, -0.693, 0.693))


def draw_prior_picks(key, part):
    favored = favored_entries(key)
    first, second, third = jax.random.split(jax.random.fold_in(key, 22), 3)
    which = jax.random.randint(first, (PROMPTS, PICKS), 0, favored_count)
    from_favored = jnp.take(favored, which)
    anywhere = jax.random.randint(second, (PROMPTS, PICKS), 0, VOCAB)
    coin = jax.random.randint(third, (PROMPTS, PICKS), 0, 4)
    return jnp.where(coin < 3, from_favored, anywhere).astype(jnp.int32)


def with_ends(array, rng, low, high):
    index_at = [jax.random.randint(jax.random.fold_in(rng, axis), (), 0, length) for axis, length in enumerate(array.shape)]
    widest = array.shape.index(max(array.shape))
    next_to = index_at[:widest] + [(index_at[widest] + 1) % array.shape[widest]] + index_at[widest + 1:]
    return array.at[tuple(index_at)].set(low).at[tuple(next_to)].set(high)


def levels(key, dims, cuts, smallest, top_value):
    def one(axis_at, shards_of):
        draws = jax.random.uniform(jax.random.fold_in(jax.random.fold_in(key, 6), axis_at), (shards_of,), jnp.float32, smallest / len(cuts), top_value / len(cuts))
        return jnp.repeat(jnp.exp(draws), dims[axis_at] // shards_of).reshape((-1,) + (1,) * (len(dims) - axis_at - 1))

    level = one(*cuts[0])
    for cut in cuts[1:]:
        level = level * one(*cut)
    return level


def bell_draw(stream_key, dims, scale, reach, cuts=(), kind=jnp.bfloat16):
    values = scale * jax.random.normal(stream_key, dims, jnp.float32)
    if cuts:
        values = values * levels(stream_key, dims, cuts, -0.22, 0.18)
    return jnp.clip(values, -reach, reach).astype(kind)


def setup_inputs(seed: int = 0) -> dict:
    keys = jax.random.split(jax.random.key(seed), 15)
    exp_hidden = draw_exp_hidden(jax.random.fold_in(keys[14], 71), 0)
    exp_pre_gain = jnp.clip(1.0 + 0.15 * jax.random.normal(keys[1], (DE,), jnp.float32), 0.25, 1.75)
    exp_gate = bell_draw(keys[2], (DE, FFE), DE ** -0.5, 0.0625, ((0, 16), (1, 8)))
    exp_up = bell_draw(keys[3], (DE, FFE), DE ** -0.5, 0.0625, ((0, 16), (1, 8)))
    exp_down = bell_draw(keys[4], (FFE, DE), FFE ** -0.5, 0.03125, ((0, 8), (1, 16)))
    exp_out_gain = jnp.clip(1.0 + 0.15 * jax.random.normal(keys[5], (DE,), jnp.float32), 0.25, 1.75)
    exp_head = draw_exp_head(jax.random.fold_in(keys[14], 71), 0)
    ama_hidden = draw_ama_hidden(jax.random.fold_in(keys[14], 71), 0)
    ama_out_gain = jnp.clip(1.0 + 0.15 * jax.random.normal(keys[8], (DA,), jnp.float32), 0.25, 1.75)
    ama_head = draw_ama_head(jax.random.fold_in(keys[14], 71), 0)
    logit_scale = draw_logit_scale(jax.random.fold_in(keys[14], 71), 0)
    prompt_of = with_ends(jax.random.randint(keys[11], (BEAMS,), 0, PROMPTS), jax.random.fold_in(keys[11], 1), 0, PROMPTS - 1).astype(jnp.int32)
    prior_picks = draw_prior_picks(jax.random.fold_in(keys[14], 71), 0)
    valid_mask = with_ends((jax.random.randint(keys[13], (VOCAB,), 0, 8) < 7).astype(jnp.int32), jax.random.fold_in(keys[13], 1), 0, 1)
    return dict(exp_hidden=exp_hidden, exp_pre_gain=exp_pre_gain, exp_gate=exp_gate, exp_up=exp_up, exp_down=exp_down, exp_out_gain=exp_out_gain, exp_head=exp_head, ama_hidden=ama_hidden, ama_out_gain=ama_out_gain, ama_head=ama_head, logit_scale=logit_scale, prompt_of=prompt_of, prior_picks=prior_picks, valid_mask=valid_mask)


norm_epsilon = 1e-05
contrast_weight = 0.5
hamming_weight = 0.7

def normed_rows(values, gain):
    meansq = lax.optimization_barrier(jnp.mean(values * values, axis=1, keepdims=True))
    return (values * lax.rsqrt(meansq + norm_epsilon) * gain).astype(jnp.bfloat16)

def head_logp(final, head, logit_scale):
    logits = logit_scale[:, None] * jnp.dot(final, head, preferred_element_type=jnp.float32)
    largest = lax.optimization_barrier(jnp.max(logits, axis=1, keepdims=True))
    totals = lax.optimization_barrier(jnp.sum(jnp.exp(logits - largest), axis=1, keepdims=True))
    return logits - largest - jnp.log(totals)

def reference(exp_hidden, exp_pre_gain, exp_gate, exp_up, exp_down, exp_out_gain, exp_head, ama_hidden, ama_out_gain, ama_head, logit_scale, prompt_of, prior_picks, valid_mask):
    values = exp_hidden.astype(jnp.float32)
    normed = normed_rows(values, exp_pre_gain)
    gate = jnp.dot(normed, exp_gate, preferred_element_type=jnp.float32)
    up = jnp.dot(normed, exp_up, preferred_element_type=jnp.float32)
    hidden = (jax.nn.silu(gate) * up).astype(jnp.bfloat16)
    layer = values + jnp.dot(hidden, exp_down, preferred_element_type=jnp.float32)
    final_exp = normed_rows(layer, exp_out_gain)
    final_ama = normed_rows(ama_hidden.astype(jnp.float32), ama_out_gain)
    logp_exp = head_logp(final_exp, exp_head, logit_scale)
    logp_ama = head_logp(final_ama, ama_head, logit_scale)
    picks_row = jnp.take(prior_picks, prompt_of, axis=0)
    vocab_ids = jnp.arange(VOCAB, dtype=jnp.int32)

    def add_pick(index, counts):
        column = lax.dynamic_slice_in_dim(picks_row, index, 1, 1)
        return counts + (column == vocab_ids[None, :]).astype(jnp.float32)
    counts = lax.fori_loop(0, PICKS, add_pick, jnp.zeros((BEAMS, VOCAB), jnp.float32))
    valid = valid_mask.astype(jnp.float32)[None, :]
    scores = logp_exp - contrast_weight * valid * logp_ama - hamming_weight * counts
    return (scores, lax.optimization_barrier(jnp.max(scores, axis=1)))
```

```python
import functools

import jax
import jax.numpy as jnp
from jax import lax
from jax.experimental import pallas as pl
from jax.experimental.pallas import tpu as pltpu
from jax.sharding import Mesh
from jax.sharding import PartitionSpec as P

DE = 8192
DA = 4096
AXES = ("z", "l", "x", "h", "c")
REP = ("z", "l")
TP = ("x", "h", "c")
ALL = REP + TP

norm_epsilon = 1e-05
contrast_weight = 0.5
hamming_weight = 0.7
LOWEST = -3.0e38

ROWS = 512
BLOCK = 64
KDIM = 512
HALF = 1792
CHUNK = 256
CHUNKS = HALF // CHUNK
KAMA = 256
WIDE = 512
BF16 = jnp.bfloat16
F32 = jnp.float32

XH = [(d // 2, d % 2) for d in range(1, 8)]
TPO = [(d // 4, (d // 2) % 2, d % 2) for d in range(1, 16)]
ZL = [(d // 2, d % 2) for d in range(1, 8)]


def dot(a, b):
    return jnp.dot(a, b, preferred_element_type=F32)


def eye128():
    return lax.broadcasted_iota(jnp.int32, (128, 128), 0) == lax.broadcasted_iota(
        jnp.int32, (128, 128), 1
    )


def to_row(column):
    return jnp.sum(jnp.where(eye128(), jnp.broadcast_to(column, (128, 128)), 0.0), 0, keepdims=True)


def to_column(row):
    return jnp.sum(jnp.where(eye128(), jnp.broadcast_to(row, (128, 128)), 0.0), 1, keepdims=True)


def aligned(v, m):
    return pl.multiple_of(v, m)


def kernel(
    hid_in, pre_gain, gate, up, down, out_gain, head, ama_in, ama_gain, ahead,
    lscale, prompt, picks, valid,
    scores, best,
    XR, XG, W, DOWN, HEAD, AHEAD, PB, RR, HID, ACC, OB, OR, FE, FA, AIN, LE, LA,
    STS, ST, TOT, RC, SFS, SF, SGS, SG, RE, RA, CNT, SBUF, PG, OG, AG,
    s_loc, s_wl, s_ws, s_wr, s_xs, s_xr, s_bs, s_br, s_sts, s_str,
    s_rs, s_rr, s_hs, s_hr, s_cs, s_cr, s_os, s_or, s_rings, s_ringr, s_fs, s_fr,
    s_sfs, s_sfr, s_sgs, s_sgr, s_qs, s_qr,
):
    z, l, x, h, c = (lax.axis_index(a) for a in AXES)
    sib = 1 - c
    r = z * 2 + l
    b = x * 2 + h
    t = x * 4 + h * 2 + c
    y = h * 2 + l

    def remote(src, dst, ss, rs, **where):
        return pltpu.make_async_remote_copy(
            src_ref=src, dst_ref=dst, send_sem=ss, recv_sem=rs,
            device_id=where, device_id_type=pl.DeviceIdType.MESH,
        )

    sends = []

    def send(src, dst, ss, rs, **where):
        cp = remote(src, dst, ss, rs, **where)
        cp.start()
        sends.append(cp)

    def recv(dst, rs):
        remote(dst, dst, rs, rs, c=sib).wait_recv()

    def local(src, dst, sem):
        return pltpu.make_async_copy(src, dst, sem)

    def zl(d, sign):
        dz, dl = ZL[d]
        return lax.rem(z + sign * dz + 4, 4), lax.rem(l + dl, 2)

    def xh(d, sign):
        dx, dh = XH[d]
        return lax.rem(x + sign * dx + 4, 4), lax.rem(h + dh, 2)

    def tp(d, sign):
        dx, dh, dc = TPO[d]
        return lax.rem(x + sign * dx + 4, 4), lax.rem(h + dh, 2), lax.rem(c + dc, 2)

    def wcols(half, j):
        return pl.ds(aligned(half * HALF + j * CHUNK, 128), CHUNK)

    def wlocal(j, i, ref):
        return local(ref.at[:, wcols(c, j)], W.at[j, c, :, pl.ds(i * CHUNK, CHUNK)], s_wl.at[j, i])

    first = [
        local(hid_in, XR.at[r], s_loc.at[0]),
        local(pre_gain, PG, s_loc.at[1]),
        local(ama_in, AIN, s_loc.at[2]),
        local(ama_gain, AG, s_loc.at[3]),
        local(out_gain, OG, s_loc.at[4]),
    ]
    for cp in first:
        cp.start()
    for j in range(CHUNKS):
        wlocal(j, 0, gate).start()
        wlocal(j, 1, up).start()
    late = [
        local(down, DOWN, s_loc.at[5]),
        local(ahead, AHEAD, s_loc.at[6]),
        local(head, HEAD, s_loc.at[7]),
    ]

    barrier = pltpu.get_barrier_semaphore()

    def greet(**where):
        pl.semaphore_signal(barrier, inc=1, device_id=where, device_id_type=pl.DeviceIdType.MESH)

    for d in range(7):
        pz, q = zl(d, 1)
        greet(z=pz, l=q)
    for d in range(15):
        px, ph, pc = tp(d, 1)
        greet(x=px, h=ph, c=pc)
    greet(h=1 - h, l=1 - l)
    pl.semaphore_wait(barrier, 23)

    for d in range(7):
        pz, q = zl(d, 1)
        send(hid_in, XR.at[r], s_xs.at[d], s_xr.at[d], z=pz, l=q)
    for j in range(CHUNKS):
        for i, ref in enumerate((gate, up)):
            send(
                ref.at[:, wcols(sib, j)], W.at[j, c, :, pl.ds(i * CHUNK, CHUNK)],
                s_ws.at[j, i], s_wr.at[j, i], c=sib,
            )

    def ring(index, sets, places, me):
        prv, nxt = lax.rem(me + 3, 4), lax.rem(me + 1, 4)
        opp = lax.rem(me + 2, 4)
        lo, hi = pl.ds(0, 32), pl.ds(32, 32)
        full = pl.ds(0, 64)

        def start():
            mine = sets(me, full)
            send(mine, mine, s_rings.at[index, 0], s_ringr.at[index, 0], **places(nxt))
            send(mine, mine, s_rings.at[index, 1], s_ringr.at[index, 1], **places(prv))

        def pass_next():
            recv(sets(prv, full), s_ringr.at[index, 0])
            part = sets(prv, lo)
            send(part, part, s_rings.at[index, 2], s_ringr.at[index, 2], **places(nxt))

        def pass_prev():
            recv(sets(nxt, full), s_ringr.at[index, 1])
            part = sets(nxt, hi)
            send(part, part, s_rings.at[index, 3], s_ringr.at[index, 3], **places(prv))

        def finish():
            recv(sets(opp, lo), s_ringr.at[index, 2])
            recv(sets(opp, hi), s_ringr.at[index, 3])

        return start, pass_next, pass_prev, finish, (me, prv, nxt, opp)

    def y_place(p):
        return dict(h=p // 2, l=lax.rem(p, 2))

    every4, every2 = pl.ds(0, 4), pl.ds(0, 2)

    def rings_x_y_z(ref, cols, first_index):
        a = ring(first_index, lambda p, k: ref.at[p, h, c, z, l, k, cols], lambda p: dict(x=p), x)
        bb = ring(
            first_index + 1,
            lambda p, k: ref.at[every4, p // 2, c, z, lax.rem(p, 2), k, cols], y_place, y,
        )
        d = ring(
            first_index + 2,
            lambda p, k: ref.at[every4, every2, c, p, every2, k, cols], lambda p: dict(z=p), z,
        )
        return a, bb, d

    def rings_z_y_x(ref, cols, first_index):
        a = ring(first_index, lambda p, k: ref.at[x, h, c, p, l, k, cols], lambda p: dict(z=p), z)
        bb = ring(
            first_index + 1,
            lambda p, k: ref.at[x, p // 2, c, every4, lax.rem(p, 2), k, cols], y_place, y,
        )
        d = ring(
            first_index + 2,
            lambda p, k: ref.at[p, every2, c, every4, every2, k, cols], lambda p: dict(x=p), x,
        )
        return a, bb, d

    for cp in first:
        cp.wait()
    values_a = AIN[...].astype(F32)
    squares_a = jnp.sum(values_a * values_a, axis=1, keepdims=True)
    FA[x, h, c, z, l] = (values_a * AG[...]).astype(BF16)
    ama = rings_x_y_z(FA, pl.ds(0, KAMA), 0)
    ama[0][0]()

    def take_rows(rr, d):
        XG[c, rr] = (XR[rr].astype(F32) * PG[...]).astype(BF16)
        send(XG.at[c, rr], XG.at[c, rr], s_bs.at[d], s_br.at[d], c=sib)

    take_rows(r, 7)
    for cp in late:
        cp.start()
    for d in range(7):
        pz, q = zl(d, -1)
        rr = pz * 2 + q
        recv(XR.at[rr], s_xr.at[d])
        take_rows(rr, d)

    for q in range(4):
        v = XR[pl.ds(2 * q, 2)].reshape(128, KDIM).astype(F32)
        STS[q : q + 1, :] = to_row(jnp.sum(v * v, axis=1, keepdims=True))
    for d in range(15):
        px, ph, pc = tp(d, 1)
        send(STS, ST.at[d], s_sts.at[d], s_str.at[d], x=px, h=ph, c=pc)

    ama[0][1]()
    ama[0][2]()

    for d in range(7):
        pz, q = zl(d, -1)
        recv(XG.at[sib, pz * 2 + q], s_br.at[d])
    recv(XG.at[sib, r], s_br.at[7])

    def rs_copy(j, d):
        px, ph = xh(d, 1)
        rows = pl.ds(aligned((px * 2 + ph) * BLOCK, BLOCK), BLOCK)
        return remote(PB.at[j, rows, :], RR.at[j, d], s_rs.at[j, d], s_rr.at[j, d], x=px, h=ph)

    def products(j, _):
        for i, ref in enumerate((gate, up)):
            wlocal(j, i, ref).wait()
            recv(W.at[j, sib, :, pl.ds(i * CHUNK, CHUNK)], s_wr.at[j, i])

        def block(q, _):
            rows = pl.ds(aligned(q * 128, 128), 128)
            pair = pl.ds(q * 2, 2)
            p = dot(XG[0, pair].reshape(128, KDIM), W[j, 0])
            p += dot(XG[1, pair].reshape(128, KDIM), W[j, 1])
            PB[j, rows, :] = p.astype(BF16)
            return 0

        lax.fori_loop(0, 4, block, 0)
        for d in range(7):
            rs_copy(j, d).start()
        return 0

    lax.fori_loop(0, CHUNKS, products, 0)

    ama[0][3]()
    ama[1][0]()

    for d in range(15):
        recv(ST.at[d], s_str.at[d])
    tot = STS[...]
    for d in range(15):
        tot += ST[d]
    TOT[...] = tot
    col = to_column(TOT[pl.ds(x, 1), :])
    RC[...] = jnp.broadcast_to(lax.rsqrt(col / DE + norm_epsilon), (128, 128))
    factor = RC[pl.ds(aligned(h * BLOCK, BLOCK), BLOCK), :][:, 0:1]

    ids = t * WIDE + r * (16 * WIDE) + lax.broadcasted_iota(jnp.int32, (16, WIDE), 1)
    per_prompt = jnp.zeros((16, WIDE), F32)
    for k in range(24):
        per_prompt += (picks[:, k : k + 1] == ids).astype(F32)
    chosen = (lax.broadcasted_iota(jnp.int32, (16, ROWS), 0) == prompt[...]).astype(F32)
    CNT[...] = lax.dot_general(
        chosen.astype(BF16), per_prompt.astype(BF16), (((0,), (0,)), ((), ())),
        preferred_element_type=F32,
    )

    ama[1][1]()
    ama[1][2]()

    own_rows = pl.ds(aligned(b * BLOCK, BLOCK), BLOCK)

    def hid_copy(j, d):
        px, ph = xh(d, 1)
        piece = HID.at[c, j, own_rows, :]
        return remote(piece, piece, s_hs.at[j, d], s_hr.at[j, d], x=px, h=ph)

    def hidden(j, _):
        for d in range(7):
            recv(RR.at[j, d], s_rr.at[j, d])
        both = PB[j, own_rows, :].astype(F32)
        for d in range(7):
            both += RR[j, d].astype(F32)
        g = both[:, :CHUNK] * factor
        u = both[:, CHUNK:] * factor
        HID[c, j, own_rows, :] = (g / (1.0 + jnp.exp(-g)) * u).astype(BF16)
        for d in range(7):
            hid_copy(j, d).start()
        return 0

    lax.fori_loop(0, 3, hidden, 0)
    ama[1][3]()
    ama[2][0]()
    lax.fori_loop(3, CHUNKS, hidden, 0)
    ama[2][1]()
    ama[2][2]()

    late[0].wait()
    ACC[...] = jnp.zeros_like(ACC)

    def core_copy(j):
        return remote(HID.at[c, j], HID.at[c, j], s_cs.at[j], s_cr.at[j], c=sib)

    def gathered(j, _):
        for d in range(7):
            px, ph = xh(d, -1)
            rows = pl.ds(aligned((px * 2 + ph) * BLOCK, BLOCK), BLOCK)
            recv(HID.at[c, j, rows, :], s_hr.at[j, d])
        core_copy(j).start()

        def block(q, _):
            rows = pl.ds(aligned(q * 128, 128), 128)
            depth = pl.ds(aligned(c * HALF + j * CHUNK, CHUNK), CHUNK)
            ACC[rows, :] += dot(HID[c, j, rows, :], DOWN[depth, :])
            return 0

        lax.fori_loop(0, 4, block, 0)
        return 0

    def from_core(j, _):
        recv(HID.at[sib, j], s_cr.at[j])

        def block(q, _):
            rows = pl.ds(aligned(q * 128, 128), 128)
            depth = pl.ds(aligned(sib * HALF + j * CHUNK, CHUNK), CHUNK)
            ACC[rows, :] += dot(HID[sib, j, rows, :], DOWN[depth, :])
            return 0

        lax.fori_loop(0, 4, block, 0)
        return 0

    def step(j, _):
        gathered(j, 0)
        from_core(j - 1, 0)
        return 0

    gathered(0, 0)
    lax.fori_loop(1, CHUNKS, step, 0)
    from_core(CHUNKS - 1, 0)

    for q in range(8):
        OB[q] = ACC[q * BLOCK : (q + 1) * BLOCK, :].astype(BF16)
    for d in range(7):
        pz, q = zl(d, 1)
        send(OB.at[pz * 2 + q], OR.at[d], s_os.at[d], s_or.at[d], z=pz, l=q)
    layer = XR[r].astype(F32) + ACC[pl.ds(aligned(r * BLOCK, BLOCK), BLOCK), :]
    for d in range(7):
        recv(OR.at[d], s_or.at[d])
        layer += OR[d].astype(F32)
    FE[x, h, c, z, l] = (layer * OG[...]).astype(BF16)

    low, high = pl.ds(0, 256), pl.ds(256, 256)
    one = rings_x_y_z(FE, low, 3)
    two = rings_z_y_x(FE, high, 6)
    one[0][0]()
    two[0][0]()

    squares = jnp.concatenate([jnp.sum(layer * layer, axis=1, keepdims=True), squares_a], axis=0)
    SFS[...] = jnp.broadcast_to(to_row(squares), (8, 128))
    for d in range(15):
        px, ph, pc = tp(d, 1)
        send(SFS, SF.at[t], s_sfs.at[d], s_sfr.at[d], x=px, h=ph, c=pc)

    for g in (one[0], two[0]):
        g[1]()
        g[2]()
    for g, n in ((one[0], one[1]), (two[0], two[1])):
        g[3]()
        n[0]()

    def totals():
        SF[t] = SFS[...]
        for d in range(15):
            px, ph, pc = tp(d, -1)
            recv(SF.at[px * 4 + ph * 2 + pc], s_sfr.at[d])
        total = SF[0]
        for d in range(1, 16):
            total += SF[d]
        SGS[...] = total
        for d in range(7):
            pz, q = zl(d, 1)
            send(SGS, SG.at[r], s_sgs.at[d], s_sgr.at[d], z=pz, l=q)

    for g in (one[1], two[1]):
        g[1]()
        g[2]()
    totals()

    def over(ref, cols, index, n):
        def go(where):
            send(where, where, s_fs.at[index, n], s_fr.at[index, n], c=sib)
        return go

    def a_set(ref, cc, p, cols):
        return ref.at[every4, every2, cc, p, every2, pl.ds(0, 64), cols]

    def b_set(ref, cc, p, cols):
        return ref.at[p, every2, cc, every4, every2, pl.ds(0, 64), cols]

    def to_core(ref, maker, p, cols, index, n):
        s = maker(ref, c, p, cols)
        send(s, s, s_fs.at[index, n], s_fr.at[index, n], c=sib)

    def from_other(ref, maker, p, cols, index, n):
        recv(maker(ref, sib, p, cols), s_fr.at[index, n])

    one[1][3]()
    one[2][0]()
    two[1][3]()
    two[2][0]()

    ama_cols = pl.ds(0, KAMA)
    ama[2][3]()
    a_places = ama[2][4]
    for n in range(4):
        to_core(FA, a_set, a_places[n], ama_cols, 0, n)
    to_core(FE, a_set, z, low, 1, 0)
    to_core(FE, b_set, x, high, 2, 0)

    late[1].wait()
    late[2].wait()
    for n in range(4):
        from_other(FA, a_set, a_places[n], ama_cols, 0, n)

    def ama_block(q, _):
        def one_t(k, acc):
            xx, hh, cc = k // 4, lax.rem(k // 2, 2), lax.rem(k, 2)
            v = FA[xx, hh, cc, q].reshape(128, KAMA)
            return acc + dot(v, AHEAD[pl.ds(aligned(k * KAMA, KAMA), KAMA), :])

        rows = pl.ds(aligned(q * 128, 128), 128)
        LA[rows, :] = lax.fori_loop(0, 16, one_t, jnp.zeros((128, WIDE), F32))
        return 0

    lax.fori_loop(0, 4, ama_block, 0)

    LE[...] = jnp.zeros_like(LE)

    def use_a(p):
        def one_t(k, acc):
            xx, hh, cc = k // 4, lax.rem(k // 2, 2), lax.rem(k, 2)
            v = FE[xx, hh, cc, p, :, :, 0:256].reshape(128, 256)
            return acc + dot(v, HEAD[pl.ds(aligned(k * KDIM, KDIM), 256), :])

        rows = pl.ds(aligned(p * 128, 128), 128)
        LE[rows, :] += lax.fori_loop(0, 16, one_t, jnp.zeros((128, WIDE), F32))

    def use_b(p):
        def block(q, _):
            def one_t(k, acc):
                hh, cc = k // 2, lax.rem(k, 2)
                v = FE[p, hh, cc, q, :, :, 256:512].reshape(128, 256)
                first_row = (p * 4 + k) * KDIM + 256
                return acc + dot(v, HEAD[pl.ds(aligned(first_row, 256), 256), :])

            rows = pl.ds(aligned(q * 128, 128), 128)
            LE[rows, :] += lax.fori_loop(0, 4, one_t, jnp.zeros((128, WIDE), F32))
            return 0

        lax.fori_loop(0, 4, block, 0)

    za, xb = one[2][4], two[2][4]
    one[2][1]()
    to_core(FE, a_set, za[1], low, 1, 1)
    two[2][1]()
    to_core(FE, b_set, xb[1], high, 2, 1)
    one[2][2]()
    to_core(FE, a_set, za[2], low, 1, 2)
    two[2][2]()
    to_core(FE, b_set, xb[2], high, 2, 2)
    for n in range(3):
        from_other(FE, a_set, za[n], low, 1, n)
        use_a(za[n])
        from_other(FE, b_set, xb[n], high, 2, n)
        use_b(xb[n])

    SG[r] = SGS[...]
    for d in range(7):
        pz, q = zl(d, -1)
        recv(SG.at[pz * 2 + q], s_sgr.at[d])
    for q in range(4):
        ls = to_column(lscale[q : q + 1, :])
        for n in range(2):
            col = to_column(SG[2 * q + n, 0:1, :])
            k = n * BLOCK
            rows = slice(q * 128 + k, q * 128 + k + BLOCK)
            fe = lax.rsqrt(col[:BLOCK] / DE + norm_epsilon) * ls[k : k + BLOCK]
            fa = lax.rsqrt(col[BLOCK:] / DA + norm_epsilon) * ls[k : k + BLOCK]
            RE[rows, :] = jnp.broadcast_to(fe, (BLOCK, 128))
            RA[rows, :] = jnp.broadcast_to(fa, (BLOCK, 128))

    one[2][3]()
    to_core(FE, a_set, za[3], low, 1, 3)
    two[2][3]()
    to_core(FE, b_set, xb[3], high, 2, 3)
    from_other(FE, a_set, za[3], low, 1, 3)
    use_a(za[3])
    from_other(FE, b_set, xb[3], high, 2, 3)
    use_b(xb[3])

    vmask = valid[...].astype(F32)
    half_valid = contrast_weight * vmask
    for q in range(4):
        rows = slice(q * 128, (q + 1) * 128)
        le = LE[rows, :] * RE[rows, 0:1]
        la = LA[rows, :] * RA[rows, 0:1]
        LE[rows, :] = le
        LA[rows, :] = la
        me = jnp.max(le, axis=1, keepdims=True)
        ma = jnp.max(la, axis=1, keepdims=True)
        se = jnp.sum(jnp.exp(le - me), axis=1, keepdims=True)
        sa = jnp.sum(jnp.exp(la - ma), axis=1, keepdims=True)
        raw = le - half_valid * la - hamming_weight * CNT[rows, :]
        used = jnp.broadcast_to(vmask, raw.shape) > 0.5
        m1 = jnp.max(jnp.where(used, raw, LOWEST), axis=1, keepdims=True)
        m0 = jnp.max(jnp.where(used, LOWEST, raw), axis=1, keepdims=True)
        lines = [to_row(v) for v in (me, se, ma, sa, m1, m0, me, me)]
        SBUF[0, c, :, rows] = jnp.concatenate(lines, axis=0)

    def merge(parts):
        me = functools.reduce(jnp.maximum, [p[0:1] for p in parts])
        ma = functools.reduce(jnp.maximum, [p[2:3] for p in parts])
        se = sum(p[1:2] * jnp.exp(p[0:1] - me) for p in parts)
        sa = sum(p[3:4] * jnp.exp(p[2:3] - ma) for p in parts)
        m1 = functools.reduce(jnp.maximum, [p[4:5] for p in parts])
        m0 = functools.reduce(jnp.maximum, [p[5:6] for p in parts])
        return jnp.concatenate([me, se, ma, sa, m1, m0, me, me], axis=0)

    mine = SBUF.at[0, c]
    send(mine, mine, s_qs.at[0, 0], s_qr.at[0, 0], c=sib)
    recv(SBUF.at[0, sib], s_qr.at[0, 0])
    merged = merge([SBUF[0, 0], SBUF[0, 1]])
    for phase, (me, place) in enumerate(
        ((x, lambda p: dict(x=p)), (y, y_place), (z, lambda p: dict(z=p))), start=1
    ):
        SBUF[phase, me] = merged
        mine = SBUF.at[phase, me]
        for d in range(1, 4):
            send(mine, mine, s_qs.at[phase, d], s_qr.at[phase, d], **place(lax.rem(me + d, 4)))
        for d in range(1, 4):
            recv(SBUF.at[phase, lax.rem(me + 4 - d, 4)], s_qr.at[phase, d])
        merged = merge([SBUF[phase, k] for k in range(4)])

    le_all = jnp.log(merged[1:2])
    la_all = jnp.log(merged[3:4])
    shift_e = merged[0:1] + le_all
    shift_a = merged[2:3] + la_all
    best[...] = jnp.maximum(
        merged[4:5] - shift_e + contrast_weight * shift_a, merged[5:6] - shift_e
    )
    for q in range(4):
        rows = slice(q * 128, (q + 1) * 128)
        ce, ca = to_column(merged[0:1, rows]), to_column(merged[2:3, rows])
        de, da = to_column(le_all[:, rows]), to_column(la_all[:, rows])
        pe = LE[rows, :] - ce - de
        pa = LA[rows, :] - ca - da
        scores[rows, :] = pe - half_valid * pa - hamming_weight * CNT[rows, :]

    for cp in sends:
        cp.wait_send()

    def drain(j, _):
        for d in range(7):
            rs_copy(j, d).wait_send()
            hid_copy(j, d).wait_send()
        core_copy(j).wait_send()
        return 0

    lax.fori_loop(0, CHUNKS, drain, 0)


def body(
    exp_hidden, exp_pre_gain, exp_gate, exp_up, exp_down, exp_out_gain, exp_head,
    ama_hidden, ama_out_gain, ama_head, logit_scale, prompt_of, prior_picks, valid_mask,
):
    hbm = pl.BlockSpec(memory_space=pl.ANY)
    vmem = pl.BlockSpec(memory_space=pltpu.VMEM)
    dma = pltpu.SemaphoreType.DMA
    scratch = [
        pltpu.VMEM((8, BLOCK, KDIM), BF16),
        pltpu.VMEM((2, 8, BLOCK, KDIM), BF16),
        pltpu.VMEM((CHUNKS, 2, KDIM, 2 * CHUNK), BF16),
        pltpu.VMEM((2 * HALF, KDIM), BF16),
        pltpu.VMEM((DE, WIDE), BF16),
        pltpu.VMEM((DA, WIDE), BF16),
        pltpu.VMEM((CHUNKS, ROWS, 2 * CHUNK), BF16),
        pltpu.VMEM((CHUNKS, 7, BLOCK, 2 * CHUNK), BF16),
        pltpu.VMEM((2, CHUNKS, ROWS, CHUNK), BF16),
        pltpu.VMEM((ROWS, KDIM), F32),
        pltpu.VMEM((8, BLOCK, KDIM), BF16),
        pltpu.VMEM((7, BLOCK, KDIM), BF16),
        pltpu.VMEM((4, 2, 2, 4, 2, BLOCK, KDIM), BF16),
        pltpu.VMEM((4, 2, 2, 4, 2, BLOCK, KAMA), BF16),
        pltpu.VMEM((BLOCK, KAMA), BF16),
        pltpu.VMEM((ROWS, WIDE), F32),
        pltpu.VMEM((ROWS, WIDE), F32),
        pltpu.VMEM((8, 128), F32),
        pltpu.VMEM((15, 8, 128), F32),
        pltpu.VMEM((8, 128), F32),
        pltpu.VMEM((128, 128), F32),
        pltpu.VMEM((8, 128), F32),
        pltpu.VMEM((16, 8, 128), F32),
        pltpu.VMEM((8, 128), F32),
        pltpu.VMEM((8, 8, 128), F32),
        pltpu.VMEM((ROWS, 128), F32),
        pltpu.VMEM((ROWS, 128), F32),
        pltpu.VMEM((ROWS, WIDE), F32),
        pltpu.VMEM((4, 4, 8, ROWS), F32),
        pltpu.VMEM((1, KDIM), F32),
        pltpu.VMEM((1, KDIM), F32),
        pltpu.VMEM((1, KAMA), F32),
        dma((8,)), dma((CHUNKS, 2)), dma((CHUNKS, 2)), dma((CHUNKS, 2)),
        dma((7,)), dma((7,)), dma((8,)), dma((8,)), dma((15,)), dma((15,)),
        dma((CHUNKS, 7)), dma((CHUNKS, 7)), dma((CHUNKS, 7)), dma((CHUNKS, 7)),
        dma((CHUNKS,)), dma((CHUNKS,)), dma((7,)), dma((7,)),
        dma((9, 4)), dma((9, 4)), dma((3, 4)), dma((3, 4)),
        dma((15,)), dma((15,)), dma((7,)), dma((7,)), dma((4, 4)), dma((4, 4)),
    ]
    scores, best = pl.pallas_call(
        kernel,
        out_shape=(
            jax.ShapeDtypeStruct((ROWS, WIDE), F32),
            jax.ShapeDtypeStruct((1, ROWS), F32),
        ),
        in_specs=[hbm] * 10 + [vmem] * 4,
        out_specs=(vmem, vmem),
        scratch_shapes=scratch,
        compiler_params=pltpu.CompilerParams(
            collective_id=0, has_side_effects=True, vmem_limit_bytes=63 * 1024 * 1024
        ),
        cost_estimate=pl.CostEstimate(
            flops=12_000_000_000, bytes_accessed=25_000_000, transcendentals=600_000
        ),
    )(
        exp_hidden, exp_pre_gain.reshape(1, KDIM), exp_gate, exp_up, exp_down,
        exp_out_gain.reshape(1, KDIM), exp_head, ama_hidden, ama_out_gain.reshape(1, KAMA),
        ama_head, logit_scale.reshape(4, 128), prompt_of.reshape(1, ROWS), prior_picks,
        valid_mask.reshape(1, WIDE),
    )
    return scores, best.reshape(ROWS)


def solution(mesh):
    torus = Mesh(mesh.devices.reshape(4, 2, 4, 2, 2), AXES)
    in_specs = (
        P(REP, TP), P(TP), P(TP, REP), P(TP, REP), P(REP, TP), P(TP), P(None, ALL),
        P(REP, TP), P(TP), P(None, ALL), P(), P(), P(), P(ALL),
    )
    out_specs = (P(None, ALL), P())
    return jax.shard_map(body, mesh=torus, in_specs=in_specs, out_specs=out_specs, check_vma=False)
```

```python
import functools

import jax
import jax.numpy as jnp
from jax import lax
from jax.experimental import pallas as pl
from jax.experimental.pallas import tpu as pltpu
from jax.sharding import Mesh
from jax.sharding import PartitionSpec as P

DE = 8192
DA = 4096
AXES = ("z", "l", "x", "h", "c")
REP = ("z", "l")
TP = ("x", "h", "c")
ALL = REP + TP

norm_epsilon = 1e-05
contrast_weight = 0.5
hamming_weight = 0.7
LOWEST = -3.0e38

ROWS = 512
BLOCK = 64
KDIM = 512
HALF = 1792
CHUNK = 256
CHUNKS = HALF // CHUNK
KAMA = 256
WIDE = 512
BF16 = jnp.bfloat16
F32 = jnp.float32

XH = [(d // 2, d % 2) for d in range(1, 8)]
TPO = [(d // 4, (d // 2) % 2, d % 2) for d in range(1, 16)]
ZL = [(d // 2, d % 2) for d in range(1, 8)]


def dot(a, b):
    return jnp.dot(a, b, preferred_element_type=F32)


def eye128():
    return lax.broadcasted_iota(jnp.int32, (128, 128), 0) == lax.broadcasted_iota(
        jnp.int32, (128, 128), 1
    )


def to_row(column):
    return jnp.sum(jnp.where(eye128(), jnp.broadcast_to(column, (128, 128)), 0.0), 0, keepdims=True)


def to_column(row):
    return jnp.sum(jnp.where(eye128(), jnp.broadcast_to(row, (128, 128)), 0.0), 1, keepdims=True)


def aligned(v, m):
    return pl.multiple_of(v, m)


def kernel(
    hid_in, pre_gain, gate, up, down, out_gain, head, ama_in, ama_gain, ahead,
    lscale, prompt, picks, valid,
    raw_out, stats_out,
    XR, XG, W, DOWN, HEADA, HEADB, AHEAD, PB, RR, HID, ACC, OB, OR, FE, FA, AIN, LE, LA,
    STS, ST, FS, FR, SFS, SF, SGS, SG, RE, CNT, SBUF, PG, OG, AG,
    s_loc, s_wl, s_ws, s_wr, s_xs, s_xr, s_bs, s_br, s_sts, s_str, s_frs, s_frr,
    s_rs, s_rr, s_hs, s_hr, s_cs, s_cr, s_os, s_or, s_rings, s_ringr, s_fs, s_fr,
    s_sfs, s_sfr, s_sgs, s_sgr, s_qs, s_qr, s_out,
):
    z, l, x, h, c = (lax.axis_index(a) for a in AXES)
    sib = 1 - c
    r = z * 2 + l
    b = x * 2 + h
    t = x * 4 + h * 2 + c
    y = h * 2 + l

    def remote(src, dst, ss, rs, **where):
        return pltpu.make_async_remote_copy(
            src_ref=src, dst_ref=dst, send_sem=ss, recv_sem=rs,
            device_id=where, device_id_type=pl.DeviceIdType.MESH,
        )

    sends = []

    def send(src, dst, ss, rs, **where):
        cp = remote(src, dst, ss, rs, **where)
        cp.start()
        sends.append(cp)

    def recv(dst, rs):
        remote(dst, dst, rs, rs, c=sib).wait_recv()

    def local(src, dst, sem):
        return pltpu.make_async_copy(src, dst, sem)

    def zl(d, sign):
        dz, dl = ZL[d]
        return lax.rem(z + sign * dz + 4, 4), lax.rem(l + dl, 2)

    def xh(d, sign):
        dx, dh = XH[d]
        return lax.rem(x + sign * dx + 4, 4), lax.rem(h + dh, 2)

    def tp(d, sign):
        dx, dh, dc = TPO[d]
        return lax.rem(x + sign * dx + 4, 4), lax.rem(h + dh, 2), lax.rem(c + dc, 2)

    def wcols(half, j):
        return pl.ds(aligned(half * HALF + j * CHUNK, 128), CHUNK)

    def wpart(j, core, i):
        rows = pl.ds(aligned(core * KDIM, KDIM), KDIM)
        return W.at[j, rows, pl.ds(i * CHUNK, CHUNK)]

    def wlocal(j, i, ref):
        return local(ref.at[:, wcols(c, j)], wpart(j, c, i), s_wl.at[j, i])

    first = [
        local(hid_in, XR.at[r], s_loc.at[0]),
        local(pre_gain, PG, s_loc.at[1]),
        local(ama_in, AIN, s_loc.at[2]),
        local(ama_gain, AG, s_loc.at[3]),
        local(out_gain, OG, s_loc.at[4]),
    ]
    for cp in first:
        cp.start()
    for j in range(CHUNKS):
        wlocal(j, 0, gate).start()
        wlocal(j, 1, up).start()
    late = [
        local(down, DOWN, s_loc.at[5]),
        local(ahead, AHEAD, s_loc.at[6]),
        local(head.at[:, pl.ds(0, 256), :], HEADA, s_loc.at[7]),
        local(head.at[:, pl.ds(256, 256), :], HEADB, s_loc.at[8]),
    ]

    barrier = pltpu.get_barrier_semaphore()

    def greet(**where):
        pl.semaphore_signal(barrier, inc=1, device_id=where, device_id_type=pl.DeviceIdType.MESH)

    for d in range(7):
        pz, q = zl(d, 1)
        greet(z=pz, l=q)
    for d in range(15):
        px, ph, pc = tp(d, 1)
        greet(x=px, h=ph, c=pc)
    greet(h=1 - h, l=1 - l)
    pl.semaphore_wait(barrier, 23)

    for d in range(7):
        pz, q = zl(d, 1)
        send(hid_in, XR.at[r], s_xs.at[d], s_xr.at[d], z=pz, l=q)
    for j in range(CHUNKS):
        for i, ref in enumerate((gate, up)):
            send(
                ref.at[:, wcols(sib, j)], wpart(j, c, i),
                s_ws.at[j, i], s_wr.at[j, i], c=sib,
            )

    def ring(index, sets, places, me):
        prv, nxt = lax.rem(me + 3, 4), lax.rem(me + 1, 4)
        opp = lax.rem(me + 2, 4)
        lo, hi = pl.ds(0, 32), pl.ds(32, 32)
        full = pl.ds(0, 64)

        def start():
            mine = sets(me, full)
            send(mine, mine, s_rings.at[index, 0], s_ringr.at[index, 0], **places(nxt))
            send(mine, mine, s_rings.at[index, 1], s_ringr.at[index, 1], **places(prv))

        def pass_next():
            recv(sets(prv, full), s_ringr.at[index, 0])
            part = sets(prv, lo)
            send(part, part, s_rings.at[index, 2], s_ringr.at[index, 2], **places(nxt))

        def pass_prev():
            recv(sets(nxt, full), s_ringr.at[index, 1])
            part = sets(nxt, hi)
            send(part, part, s_rings.at[index, 3], s_ringr.at[index, 3], **places(prv))

        def finish():
            recv(sets(opp, lo), s_ringr.at[index, 2])
            recv(sets(opp, hi), s_ringr.at[index, 3])

        return start, pass_next, pass_prev, finish, (me, prv, nxt, opp)

    def y_place(p):
        return dict(h=p // 2, l=lax.rem(p, 2))

    every4, every2 = pl.ds(0, 4), pl.ds(0, 2)

    def rings_x_y_z(ref, cols, first_index, split=False):
        a = ring(first_index, lambda p, k: ref.at[p, h, c, z, l, k, cols], lambda p: dict(x=p), x)
        bb = ring(
            first_index + 1,
            lambda p, k: ref.at[every4, p // 2, c, z, lax.rem(p, 2), k, cols], y_place, y,
        )
        if split:
            def d(yy, n):
                return ring(
                    first_index + 6 + n,
                    lambda p, k: ref.at[every4, yy // 2, c, p, lax.rem(yy, 2), k, cols],
                    lambda p: dict(z=p), z,
                )
        else:
            d = ring(
                first_index + 2,
                lambda p, k: ref.at[every4, every2, c, p, every2, k, cols], lambda p: dict(z=p), z,
            )
        return a, bb, d

    def rings_z_y_x(ref, cols, first_index):
        a = ring(first_index, lambda p, k: ref.at[x, h, c, p, l, k, cols], lambda p: dict(z=p), z)
        bb = ring(
            first_index + 1,
            lambda p, k: ref.at[x, p // 2, c, every4, lax.rem(p, 2), k, cols], y_place, y,
        )

        def d(yy, n):
            return ring(
                first_index + 6 + n,
                lambda p, k: ref.at[p, yy // 2, c, every4, lax.rem(yy, 2), k, cols],
                lambda p: dict(x=p), x,
            )

        return a, bb, d

    def a_set(ref, cc, p, cols):
        return ref.at[every4, every2, cc, p, every2, pl.ds(0, 64), cols]

    def b_set(ref, cc, p, cols):
        return ref.at[p, every2, cc, every4, every2, pl.ds(0, 64), cols]

    def to_core(ref, maker, p, cols, index, n):
        s = maker(ref, c, p, cols)
        send(s, s, s_fs.at[index, n], s_fr.at[index, n], c=sib)

    def from_other(ref, maker, p, cols, index, n):
        recv(maker(ref, sib, p, cols), s_fr.at[index, n])

    for cp in first:
        cp.wait()
    values_x = XR[r].astype(F32)
    values_a = AIN[...].astype(F32)
    squares = jnp.concatenate(
        [jnp.sum(v * v, axis=1, keepdims=True) for v in (values_x, values_a)], axis=0
    )
    STS[...] = jnp.broadcast_to(to_row(squares), (8, 128))
    for d in range(15):
        px, ph, pc = tp(d, 1)
        send(STS, ST.at[d], s_sts.at[d], s_str.at[0], x=px, h=ph, c=pc)
    recv(ST, s_str.at[0])
    total = STS[...]
    for d in range(15):
        total += ST[d]
    lane = lax.broadcasted_iota(jnp.int32, (8, 128), 1)
    means = jnp.where(lane < BLOCK, total / DE, total / DA)
    FS[...] = lax.rsqrt(means + norm_epsilon)
    for d in range(7):
        pz, q = zl(d, 1)
        send(FS, FR.at[d], s_frs.at[d], s_frr.at[0], z=pz, l=q)
    own_factors = to_column(FS[0:1, :])

    FA[x, h, c, z, l] = (values_a * own_factors[BLOCK:] * AG[...]).astype(BF16)
    ama = rings_x_y_z(FA, pl.ds(0, KAMA), 0)
    ama[0][0]()

    def take_rows(rr, d, factors):
        XG[c, rr] = (XR[rr].astype(F32) * factors[:BLOCK] * PG[...]).astype(BF16)
        send(XG.at[c, rr], XG.at[c, rr], s_bs.at[d], s_br.at[d], c=sib)

    take_rows(r, 7, own_factors)
    for cp in late:
        cp.start()
    recv(FR, s_frr.at[0])
    for d in range(7):
        pz, q = zl(d, -1)
        rr = pz * 2 + q
        recv(XR.at[rr], s_xr.at[d])
        take_rows(rr, d, to_column(FR[d, 0:1, :]))

    ama[0][1]()
    ama[0][2]()

    for d in range(7):
        pz, q = zl(d, -1)
        recv(XG.at[sib, pz * 2 + q], s_br.at[d])
    recv(XG.at[sib, r], s_br.at[7])

    def rs_copy(j, d):
        px, ph = xh(d, 1)
        rows = pl.ds(aligned((px * 2 + ph) * BLOCK, BLOCK), BLOCK)
        return remote(PB.at[j, rows, :], RR.at[j, d], s_rs.at[j], s_rr.at[j], x=px, h=ph)

    def products(j, _):
        for i, ref in enumerate((gate, up)):
            wlocal(j, i, ref).wait()
            recv(wpart(j, sib, i), s_wr.at[j, i])

        def block(q, _):
            rows = pl.ds(aligned(q * 256, 256), 256)
            quad = pl.ds(q * 4, 4)
            lhs = jnp.concatenate([XG[k, quad].reshape(256, KDIM) for k in range(2)], axis=1)
            PB[j, rows, :] = dot(lhs, W[j]).astype(BF16)
            return 0

        lax.fori_loop(0, 2, block, 0)
        for d in range(7):
            rs_copy(j, d).start()
        return 0

    lax.fori_loop(0, CHUNKS, products, 0)

    ama[0][3]()
    ama[1][0]()

    ids = t * WIDE + r * (16 * WIDE) + lax.broadcasted_iota(jnp.int32, (16, WIDE), 1)
    per_prompt = jnp.zeros((16, WIDE), F32)
    for k in range(24):
        per_prompt += (picks[:, k : k + 1] == ids).astype(F32)
    chosen = (lax.broadcasted_iota(jnp.int32, (16, ROWS), 0) == prompt[...]).astype(F32)
    CNT[...] = lax.dot_general(
        chosen.astype(BF16), per_prompt.astype(BF16), (((0,), (0,)), ((), ())),
        preferred_element_type=F32,
    )

    ama[1][1]()
    ama[1][2]()
    ama[1][3]()
    ama[2][0]()

    own_rows = pl.ds(aligned(b * BLOCK, BLOCK), BLOCK)

    def hid_copy(j, d):
        px, ph = xh(d, 1)
        piece = HID.at[c, j, own_rows, :]
        return remote(piece, piece, s_hs.at[j], s_hr.at[j], x=px, h=ph)

    def hidden(j, _):
        recv(RR.at[j], s_rr.at[j])
        both = PB[j, own_rows, :].astype(F32)
        for d in range(7):
            both += RR[j, d].astype(F32)
        g = both[:, :CHUNK]
        u = both[:, CHUNK:]
        HID[c, j, own_rows, :] = (g / (1.0 + jnp.exp(-g)) * u).astype(BF16)
        for d in range(7):
            hid_copy(j, d).start()
        return 0

    lax.fori_loop(0, 3, hidden, 0)
    ama[2][1]()
    ama[2][2]()
    lax.fori_loop(3, 5, hidden, 0)
    ama[2][3]()
    a_places = ama[2][4]
    ama_cols = pl.ds(0, KAMA)
    for n in range(4):
        to_core(FA, a_set, a_places[n], ama_cols, 0, n)
    lax.fori_loop(5, CHUNKS, hidden, 0)

    late[1].wait()
    for n in range(4):
        from_other(FA, a_set, a_places[n], ama_cols, 0, n)

    def ama_block(q, _):
        rows = pl.ds(aligned(q * 256, 256), 256)
        LA[rows, :] = jnp.zeros((256, WIDE), F32)

        def part(k, _):
            lhs = jnp.concatenate(
                [FA[k, n // 2, n % 2, pl.ds(q * 2, 2)].reshape(256, KAMA) for n in range(4)], axis=1
            )
            LA[rows, :] += dot(lhs, AHEAD[pl.ds(aligned(k * 4 * KAMA, 4 * KAMA), 4 * KAMA), :])
            return 0

        lax.fori_loop(0, 4, part, 0)
        return 0

    lax.fori_loop(0, 2, ama_block, 0)

    late[0].wait()
    ACC[...] = jnp.zeros_like(ACC)

    def core_copy(j):
        return remote(HID.at[c, j], HID.at[c, j], s_cs.at[j], s_cr.at[j], c=sib)

    def gathered(j, _):
        recv(HID.at[c, j, pl.ds(0, 7 * BLOCK), :], s_hr.at[j])
        core_copy(j).start()

        def block(q, _):
            rows = pl.ds(aligned(q * 256, 256), 256)
            depth = pl.ds(aligned(c * HALF + j * CHUNK, CHUNK), CHUNK)
            ACC[rows, :] += dot(HID[c, j, rows, :], DOWN[depth, :])
            return 0

        lax.fori_loop(0, 2, block, 0)
        return 0

    def from_core(j, _):
        recv(HID.at[sib, j], s_cr.at[j])

        def block(q, _):
            rows = pl.ds(aligned(q * 256, 256), 256)
            depth = pl.ds(aligned(sib * HALF + j * CHUNK, CHUNK), CHUNK)
            ACC[rows, :] += dot(HID[sib, j, rows, :], DOWN[depth, :])
            return 0

        lax.fori_loop(0, 2, block, 0)
        return 0

    def step(j, _):
        gathered(j, 0)
        from_core(j - 1, 0)
        return 0

    gathered(0, 0)
    lax.fori_loop(1, CHUNKS, step, 0)
    from_core(CHUNKS - 1, 0)

    for q in range(8):
        OB[q] = ACC[q * BLOCK : (q + 1) * BLOCK, :].astype(BF16)
    for d in range(7):
        pz, q = zl(d, 1)
        send(OB.at[pz * 2 + q], OR.at[d], s_os.at[d], s_or.at[0], z=pz, l=q)
    layer = values_x + ACC[pl.ds(aligned(r * BLOCK, BLOCK), BLOCK), :]
    recv(OR, s_or.at[0])
    for d in range(7):
        layer += OR[d].astype(F32)
    FE[x, h, c, z, l] = (layer * OG[...]).astype(BF16)

    low, high = pl.ds(0, 256), pl.ds(256, 256)
    one = rings_x_y_z(FE, low, 3, split=True)
    two = rings_z_y_x(FE, high, 7)
    one[0][0]()
    two[0][0]()

    squares = jnp.sum(layer * layer, axis=1, keepdims=True)
    squares = jnp.concatenate([squares, squares], axis=0)
    SFS[...] = jnp.broadcast_to(to_row(squares), (8, 128))
    for d in range(15):
        px, ph, pc = tp(d, 1)
        send(SFS, SF.at[d], s_sfs.at[d], s_sfr.at[0], x=px, h=ph, c=pc)

    for g in (one[0], two[0]):
        g[1]()
        g[2]()
    y_order = one[1][4]
    last_one = [one[2](p, n) for n, p in enumerate(y_order)]
    last_two = [two[2](p, n) for n, p in enumerate(y_order)]
    for g, n, e in ((one[0], one[1], last_one), (two[0], two[1], last_two)):
        g[3]()
        n[0]()
        e[0][0]()
    for k in (1, 2):
        for n, e in ((one[1], last_one), (two[1], last_two)):
            n[k]()
            e[k][0]()

    recv(SF, s_sfr.at[0])
    total = SFS[...]
    for d in range(15):
        total += SF[d]
    SGS[...] = total
    for d in range(7):
        pz, q = zl(d, 1)
        send(SGS, SG.at[d], s_sgs.at[d], s_sgr.at[0], z=pz, l=q)

    for n, e in ((one[1], last_one), (two[1], last_two)):
        n[3]()
        e[3][0]()
    to_core(FE, a_set, z, low, 1, 0)
    to_core(FE, b_set, x, high, 2, 0)
    late[2].wait()
    late[3].wait()
    LE[...] = jnp.zeros_like(LE)

    def use_a(p):
        def part(k, _):
            lhs = jnp.concatenate(
                [FE[k, n // 2, n % 2, p, :, :, 0:256].reshape(128, 256) for n in range(4)], axis=1
            )
            rows = pl.ds(aligned(p * 128, 128), 128)
            LE[rows, :] += dot(lhs, HEADA[pl.ds(k * 4, 4)].reshape(1024, WIDE))
            return 0

        lax.fori_loop(0, 4, part, 0)

    def use_b(p):
        def part(q, _):
            pair = pl.ds(q * 2, 2)
            lhs = jnp.concatenate(
                [FE[p, n // 2, n % 2, pair, :, :, 256:512].reshape(256, 256) for n in range(4)], axis=1
            )
            rows = pl.ds(aligned(q * 256, 256), 256)
            LE[rows, :] += dot(lhs, HEADB[pl.ds(p * 4, 4)].reshape(1024, WIDE))
            return 0

        lax.fori_loop(0, 2, part, 0)

    za, xb = last_one[0][4], last_two[0][4]
    for n in range(4):
        for e in (last_one, last_two):
            e[n][1]()
            e[n][2]()
    for n in (1, 2):
        to_core(FE, a_set, za[n], low, 1, n)
        to_core(FE, b_set, xb[n], high, 2, n)
    for n in range(3):
        from_other(FE, a_set, za[n], low, 1, n)
        use_a(za[n])
        from_other(FE, b_set, xb[n], high, 2, n)
        use_b(xb[n])

    recv(SG, s_sgr.at[0])
    for q in range(4):
        ls = to_column(lscale[q : q + 1, :])
        RE[1, pl.ds(q * 128, 128), :] = jnp.broadcast_to(ls, (128, 128))

    def row_factors(rr, line):
        rows = pl.ds(aligned(rr * BLOCK, BLOCK), BLOCK)
        col = lax.rsqrt(to_column(line)[:BLOCK] / DE + norm_epsilon)
        RE[0, rows, :] = col * RE[1, rows, :]

    row_factors(r, SGS[0:1, :])
    for d in range(7):
        pz, q = zl(d, -1)
        row_factors(pz * 2 + q, SG[d, 0:1, :])

    for n in range(4):
        for e in (last_one, last_two):
            e[n][3]()
    to_core(FE, a_set, za[3], low, 1, 3)
    to_core(FE, b_set, xb[3], high, 2, 3)
    from_other(FE, a_set, za[3], low, 1, 3)
    use_a(za[3])
    from_other(FE, b_set, xb[3], high, 2, 3)
    use_b(xb[3])

    vmask = valid[...].astype(F32)
    half_valid = contrast_weight * vmask
    for q in range(4):
        rows = pl.ds(q * 128, 128)
        le = LE[rows, :] * RE[0, rows, 0:1]
        la = LA[rows, :] * RE[1, rows, 0:1]
        me = jnp.max(le, axis=1, keepdims=True)
        ma = jnp.max(la, axis=1, keepdims=True)
        se = jnp.sum(jnp.exp(le - me), axis=1, keepdims=True)
        sa = jnp.sum(jnp.exp(la - ma), axis=1, keepdims=True)
        raw = le - half_valid * la - hamming_weight * CNT[rows, :]
        LE[rows, :] = raw
        local(LE.at[rows], raw_out.at[rows], s_out.at[q]).start()
        used = jnp.broadcast_to(vmask, raw.shape) > 0.5
        m1 = jnp.max(jnp.where(used, raw, LOWEST), axis=1, keepdims=True)
        m0 = jnp.max(jnp.where(used, LOWEST, raw), axis=1, keepdims=True)
        lines = [to_row(v) for v in (me, se, ma, sa, m1, m0, me, me)]
        SBUF[0, c, :, rows] = jnp.concatenate(lines, axis=0)

    def merge(parts):
        me = functools.reduce(jnp.maximum, [p[0:1] for p in parts])
        ma = functools.reduce(jnp.maximum, [p[2:3] for p in parts])
        se = sum(p[1:2] * jnp.exp(p[0:1] - me) for p in parts)
        sa = sum(p[3:4] * jnp.exp(p[2:3] - ma) for p in parts)
        m1 = functools.reduce(jnp.maximum, [p[4:5] for p in parts])
        m0 = functools.reduce(jnp.maximum, [p[5:6] for p in parts])
        return jnp.concatenate([me, se, ma, sa, m1, m0, me, me], axis=0)

    mine = SBUF.at[0, c]
    send(mine, mine, s_qs.at[0, 0], s_qr.at[0, 0], c=sib)
    recv(SBUF.at[0, sib], s_qr.at[0, 0])
    merged = merge([SBUF[0, 0], SBUF[0, 1]])
    for phase, (me, place) in enumerate(
        ((x, lambda p: dict(x=p)), (y, y_place), (z, lambda p: dict(z=p))), start=1
    ):
        SBUF[phase, me] = merged
        mine = SBUF.at[phase, me]
        for d in range(1, 4):
            send(mine, mine, s_qs.at[phase, d], s_qr.at[phase, d], **place(lax.rem(me + d, 4)))
        for d in range(1, 4):
            recv(SBUF.at[phase, lax.rem(me + 4 - d, 4)], s_qr.at[phase, d])
        merged = merge([SBUF[phase, k] for k in range(4)])

    stats_out[...] = merged
    for q in range(4):
        rows = pl.ds(q * 128, 128)
        local(LE.at[rows], raw_out.at[rows], s_out.at[q]).wait()

    for cp in sends:
        cp.wait_send()

    def drain(j, _):
        sent = RR.at[j]
        remote(sent, sent, s_rs.at[j], s_rr.at[j], c=sib).wait_send()
        sent = HID.at[c, j, pl.ds(0, 7 * BLOCK), :]
        remote(sent, sent, s_hs.at[j], s_hr.at[j], c=sib).wait_send()
        core_copy(j).wait_send()
        return 0

    lax.fori_loop(0, CHUNKS, drain, 0)


def finish(raw, stats, valid, scores, best):
    shift_e = stats[0:1, :] + jnp.log(stats[1:2, :])
    shift_a = stats[2:3, :] + jnp.log(stats[3:4, :])
    best[...] = jnp.maximum(
        stats[4:5, :] - shift_e + contrast_weight * shift_a, stats[5:6, :] - shift_e
    )
    half_valid = contrast_weight * valid[...].astype(F32)
    for q in range(4):
        rows = slice(q * 128, (q + 1) * 128)
        back = half_valid * to_column(shift_a[:, rows]) - to_column(shift_e[:, rows])
        scores[rows, :] = raw[rows, :] + back


def body(
    exp_hidden, exp_pre_gain, exp_gate, exp_up, exp_down, exp_out_gain, exp_head,
    ama_hidden, ama_out_gain, ama_head, logit_scale, prompt_of, prior_picks, valid_mask,
):
    hbm = pl.BlockSpec(memory_space=pl.ANY)
    vmem = pl.BlockSpec(memory_space=pltpu.VMEM)
    dma = pltpu.SemaphoreType.DMA
    scratch = [
        pltpu.VMEM((8, BLOCK, KDIM), BF16),
        pltpu.VMEM((2, 8, BLOCK, KDIM), BF16),
        pltpu.VMEM((CHUNKS, 2 * KDIM, 2 * CHUNK), BF16),
        pltpu.VMEM((2 * HALF, KDIM), BF16),
        pltpu.VMEM((16, 256, WIDE), BF16),
        pltpu.VMEM((16, 256, WIDE), BF16),
        pltpu.VMEM((DA, WIDE), BF16),
        pltpu.VMEM((CHUNKS, ROWS, 2 * CHUNK), BF16),
        pltpu.VMEM((CHUNKS, 7, BLOCK, 2 * CHUNK), BF16),
        pltpu.VMEM((2, CHUNKS, ROWS, CHUNK), BF16),
        pltpu.VMEM((ROWS, KDIM), F32),
        pltpu.VMEM((8, BLOCK, KDIM), BF16),
        pltpu.VMEM((7, BLOCK, KDIM), BF16),
        pltpu.VMEM((4, 2, 2, 4, 2, BLOCK, KDIM), BF16),
        pltpu.VMEM((4, 2, 2, 4, 2, BLOCK, KAMA), BF16),
        pltpu.VMEM((BLOCK, KAMA), BF16),
        pltpu.VMEM((ROWS, WIDE), F32),
        pltpu.VMEM((ROWS, WIDE), F32),
        pltpu.VMEM((8, 128), F32),
        pltpu.VMEM((15, 8, 128), F32),
        pltpu.VMEM((8, 128), F32),
        pltpu.VMEM((7, 8, 128), F32),
        pltpu.VMEM((8, 128), F32),
        pltpu.VMEM((15, 8, 128), F32),
        pltpu.VMEM((8, 128), F32),
        pltpu.VMEM((7, 8, 128), F32),
        pltpu.VMEM((2, ROWS, 128), F32),
        pltpu.VMEM((ROWS, WIDE), F32),
        pltpu.VMEM((4, 4, 8, ROWS), F32),
        pltpu.VMEM((1, KDIM), F32),
        pltpu.VMEM((1, KDIM), F32),
        pltpu.VMEM((1, KAMA), F32),
        dma((9,)), dma((CHUNKS, 2)), dma((CHUNKS, 2)), dma((CHUNKS, 2)),
        dma((7,)), dma((7,)), dma((8,)), dma((8,)), dma((15,)), dma((1,)), dma((7,)), dma((1,)),
        dma((CHUNKS,)), dma((CHUNKS,)), dma((CHUNKS,)), dma((CHUNKS,)),
        dma((CHUNKS,)), dma((CHUNKS,)), dma((7,)), dma((1,)),
        dma((17, 4)), dma((17, 4)), dma((3, 4)), dma((3, 4)),
        dma((15,)), dma((1,)), dma((7,)), dma((1,)), dma((4, 4)), dma((4, 4)), dma((4,)),
    ]
    raw, stats = pl.pallas_call(
        kernel,
        out_shape=(
            jax.ShapeDtypeStruct((ROWS, WIDE), F32),
            jax.ShapeDtypeStruct((8, ROWS), F32),
        ),
        in_specs=[hbm] * 10 + [vmem] * 4,
        out_specs=(hbm, vmem),
        scratch_shapes=scratch,
        compiler_params=pltpu.CompilerParams(
            collective_id=0, has_side_effects=True, vmem_limit_bytes=63 * 1024 * 1024
        ),
        cost_estimate=pl.CostEstimate(
            flops=12_000_000_000, bytes_accessed=25_000_000, transcendentals=600_000
        ),
    )(
        exp_hidden, exp_pre_gain.reshape(1, KDIM), exp_gate, exp_up, exp_down,
        exp_out_gain.reshape(1, KDIM), exp_head.reshape(16, KDIM, WIDE), ama_hidden, ama_out_gain.reshape(1, KAMA),
        ama_head, logit_scale.reshape(4, 128), prompt_of.reshape(1, ROWS), prior_picks,
        valid_mask.reshape(1, WIDE),
    )
    scores, best = pl.pallas_call(
        finish,
        out_shape=(
            jax.ShapeDtypeStruct((ROWS, WIDE), F32),
            jax.ShapeDtypeStruct((1, ROWS), F32),
        ),
        in_specs=[vmem] * 3,
        out_specs=(vmem, vmem),
    )(raw, stats, valid_mask.reshape(1, WIDE))
    return scores, best.reshape(ROWS)


def solution(mesh):
    torus = Mesh(mesh.devices.reshape(4, 2, 4, 2, 2), AXES)
    in_specs = (
        P(REP, TP), P(TP), P(TP, REP), P(TP, REP), P(REP, TP), P(TP), P(None, ALL),
        P(REP, TP), P(TP), P(None, ALL), P(), P(), P(), P(ALL),
    )
    out_specs = (P(None, ALL), P())
    return jax.shard_map(body, mesh=torus, in_specs=in_specs, out_specs=out_specs, check_vma=False)
```

```python
import functools

import jax
import jax.numpy as jnp
from jax import lax
from jax.experimental import pallas as pl
from jax.experimental.pallas import tpu as pltpu
from jax.sharding import Mesh
from jax.sharding import PartitionSpec as P

DE = 8192
DA = 4096
AXES = ("z", "l", "x", "h", "c")
REP = ("z", "l")
TP = ("x", "h", "c")
ALL = REP + TP

norm_epsilon = 1e-05
contrast_weight = 0.5
hamming_weight = 0.7
LOWEST = -3.0e38

ROWS = 512
BLOCK = 64
KDIM = 512
HALF = 1792
CHUNK = 256
CHUNKS = HALF // CHUNK
XFIRST = 4
YFIRST = CHUNKS - XFIRST
KAMA = 256
WIDE = 512
BF16 = jnp.bfloat16
F32 = jnp.float32

XH = [(d // 2, d % 2) for d in range(1, 8)]
TPO = [(d // 4, (d // 2) % 2, d % 2) for d in range(1, 16)]
ZL = [(d // 2, d % 2) for d in range(1, 8)]


def dot(a, b):
    return jnp.dot(a, b, preferred_element_type=F32)


def eye128():
    return lax.broadcasted_iota(jnp.int32, (128, 128), 0) == lax.broadcasted_iota(
        jnp.int32, (128, 128), 1
    )


def to_row(column):
    return jnp.sum(jnp.where(eye128(), jnp.broadcast_to(column, (128, 128)), 0.0), 0, keepdims=True)


def to_column(row):
    return jnp.sum(jnp.where(eye128(), jnp.broadcast_to(row, (128, 128)), 0.0), 1, keepdims=True)


def aligned(v, m):
    return pl.multiple_of(v, m)


def kernel(
    hid_in, pre_gain, gate, up, down, out_gain, head, ama_in, ama_gain, ahead,
    lscale, prompt, picks, valid,
    raw_out, stats_out,
    XR, XG, W, DOWN, HEADA, HEADB, AHEAD, PB, M1, SR, T, HS, HR, YR, HID, ACC, OB, OR, FE, FA, AIN, LE, LA,
    STS, ST, FS, FR, SFS, SF, SGS, SG, RE, CNT, SBUF, PG, OG, AG,
    s_loc, s_wl, s_ws, s_wr, s_xs, s_xr, s_bs, s_br, s_sts, s_str, s_frs, s_frr,
    s_rs, s_rr, s_hs, s_hr, s_cs, s_cr, s_os, s_or, s_rings, s_ringr, s_fs, s_fr,
    s_sfs, s_sfr, s_sgs, s_sgr, s_qs, s_qr, s_out,
):
    z, l, x, h, c = (lax.axis_index(a) for a in AXES)
    sib = 1 - c
    r = z * 2 + l
    b = x * 2 + h
    t = x * 4 + h * 2 + c
    y = h * 2 + l
    xp, xn, xo = lax.rem(x + 3, 4), lax.rem(x + 1, 4), lax.rem(x + 2, 4)

    def remote(src, dst, ss, rs, **where):
        return pltpu.make_async_remote_copy(
            src_ref=src, dst_ref=dst, send_sem=ss, recv_sem=rs,
            device_id=where, device_id_type=pl.DeviceIdType.MESH,
        )

    sends = []

    def send(src, dst, ss, rs, **where):
        cp = remote(src, dst, ss, rs, **where)
        cp.start()
        sends.append(cp)

    later = []

    def send_set(region, ss, rs, where):
        remote(region(), region(), ss, rs, **where()).start()
        later.append(lambda: remote(region(), region(), ss, rs, **where()).wait_send())

    def go(src, dst, ss, rs, **where):
        remote(src, dst, ss, rs, **where).start()

    def recv(dst, rs):
        remote(dst, dst, rs, rs, c=sib).wait_recv()

    def local(src, dst, sem):
        return pltpu.make_async_copy(src, dst, sem)

    def zl(d, sign):
        dz, dl = ZL[d]
        return lax.rem(z + sign * dz + 4, 4), lax.rem(l + dl, 2)

    def xh(d, sign):
        dx, dh = XH[d]
        return lax.rem(x + sign * dx + 4, 4), lax.rem(h + dh, 2)

    def tp(d, sign):
        dx, dh, dc = TPO[d]
        return lax.rem(x + sign * dx + 4, 4), lax.rem(h + dh, 2), lax.rem(c + dc, 2)

    def wcols(half, j):
        return pl.ds(aligned(half * HALF + j * CHUNK, 128), CHUNK)

    def wpart(j, core, i):
        rows = pl.ds(aligned(core * KDIM, KDIM), KDIM)
        return W.at[j, rows, pl.ds(i * CHUNK, CHUNK)]

    def wlocal(j, i, ref):
        return local(ref.at[:, wcols(c, j)], wpart(j, c, i), s_wl.at[j, i])

    first = [
        local(hid_in, XR.at[r], s_loc.at[0]),
        local(pre_gain, PG, s_loc.at[1]),
        local(ama_in, AIN, s_loc.at[2]),
        local(ama_gain, AG, s_loc.at[3]),
        local(out_gain, OG, s_loc.at[4]),
    ]
    for cp in first:
        cp.start()
    for j in (0, 4, 1, 5, 2, 6, 3):
        wlocal(j, 0, gate).start()
        wlocal(j, 1, up).start()
    late = [
        local(down, DOWN, s_loc.at[5]),
        local(ahead, AHEAD, s_loc.at[6]),
        local(head.at[:, pl.ds(0, 256), :], HEADA, s_loc.at[7]),
        local(head.at[:, pl.ds(256, 256), :], HEADB, s_loc.at[8]),
    ]

    barrier = pltpu.get_barrier_semaphore()

    def greet(**where):
        pl.semaphore_signal(barrier, inc=1, device_id=where, device_id_type=pl.DeviceIdType.MESH)

    for d in range(7):
        pz, q = zl(d, 1)
        greet(z=pz, l=q)
    for d in range(15):
        px, ph, pc = tp(d, 1)
        greet(x=px, h=ph, c=pc)
    greet(h=1 - h, l=1 - l)
    pl.semaphore_wait(barrier, 23)

    for d in range(7):
        pz, q = zl(d, 1)
        send(hid_in, XR.at[r], s_xs.at[d], s_xr.at[d], z=pz, l=q)
    for j in (0, 4, 1, 5, 2, 6, 3):
        for i, ref in enumerate((gate, up)):
            send(
                ref.at[:, wcols(sib, j)], wpart(j, c, i),
                s_ws.at[j, i], s_wr.at[j, i], c=sib,
            )

    def ring(index, sets, places, me):
        prv, nxt = lax.rem(me + 3, 4), lax.rem(me + 1, 4)
        opp = lax.rem(me + 2, 4)
        lo, hi = pl.ds(0, 32), pl.ds(32, 32)
        full = pl.ds(0, 64)

        def pass_on(p, rows, q, n):
            send_set(
                lambda: sets(p, rows), s_rings.at[index, n], s_ringr.at[index, n], lambda: places(q)
            )

        def start():
            pass_on(me, full, nxt, 0)
            pass_on(me, full, prv, 1)

        def pass_next():
            recv(sets(prv, full), s_ringr.at[index, 0])
            pass_on(prv, lo, nxt, 2)

        def pass_prev():
            recv(sets(nxt, full), s_ringr.at[index, 1])
            pass_on(nxt, hi, prv, 3)

        def finish():
            recv(sets(opp, lo), s_ringr.at[index, 2])
            recv(sets(opp, hi), s_ringr.at[index, 3])

        return start, pass_next, pass_prev, finish, (me, prv, nxt, opp)

    def y_place(p):
        return dict(h=lax.div(p, 2), l=lax.rem(p, 2))

    every4, every2 = pl.ds(0, 4), pl.ds(0, 2)

    def rings_x_y_z(ref, cols, first_index, split=False):
        a = ring(first_index, lambda p, k: ref.at[p, h, c, z, l, k, cols], lambda p: dict(x=p), x)
        bb = ring(
            first_index + 1,
            lambda p, k: ref.at[every4, lax.div(p, 2), c, z, lax.rem(p, 2), k, cols], y_place, y,
        )
        if split:
            def d(yy, n):
                return ring(
                    first_index + 6 + n,
                    lambda p, k: ref.at[every4, lax.div(yy, 2), c, p, lax.rem(yy, 2), k, cols],
                    lambda p: dict(z=p), z,
                )
        else:
            d = ring(
                first_index + 2,
                lambda p, k: ref.at[every4, every2, c, p, every2, k, cols], lambda p: dict(z=p), z,
            )
        return a, bb, d

    def rings_z_y_x(ref, cols, first_index):
        a = ring(first_index, lambda p, k: ref.at[x, h, c, p, l, k, cols], lambda p: dict(z=p), z)
        bb = ring(
            first_index + 1,
            lambda p, k: ref.at[x, lax.div(p, 2), c, every4, lax.rem(p, 2), k, cols], y_place, y,
        )

        def d(yy, n):
            return ring(
                first_index + 6 + n,
                lambda p, k: ref.at[p, lax.div(yy, 2), c, every4, lax.rem(yy, 2), k, cols],
                lambda p: dict(x=p), x,
            )

        return a, bb, d

    def a_set(ref, cc, p, cols):
        return ref.at[every4, every2, cc, p, every2, pl.ds(0, 64), cols]

    def b_set(ref, cc, p, cols):
        return ref.at[p, every2, cc, every4, every2, pl.ds(0, 64), cols]

    def to_core(ref, maker, p, cols, index, n):
        send_set(
            lambda: maker(ref, c, p, cols), s_fs.at[index, n], s_fr.at[index, n], lambda: dict(c=sib)
        )

    def from_other(ref, maker, p, cols, index, n):
        recv(maker(ref, sib, p, cols), s_fr.at[index, n])

    for cp in first:
        cp.wait()
    values_x = XR[r].astype(F32)
    values_a = AIN[...].astype(F32)
    squares = jnp.concatenate(
        [jnp.sum(v * v, axis=1, keepdims=True) for v in (values_x, values_a)], axis=0
    )
    STS[...] = jnp.broadcast_to(to_row(squares), (8, 128))
    for d in range(15):
        px, ph, pc = tp(d, 1)
        send(STS, ST.at[d], s_sts.at[d], s_str.at[0], x=px, h=ph, c=pc)
    recv(ST, s_str.at[0])
    total = STS[...]
    for d in range(15):
        total += ST[d]
    lane = lax.broadcasted_iota(jnp.int32, (8, 128), 1)
    means = jnp.where(lane < BLOCK, total / DE, total / DA)
    FS[...] = lax.rsqrt(means + norm_epsilon)
    for d in range(7):
        pz, q = zl(d, 1)
        send(FS, FR.at[d], s_frs.at[d], s_frr.at[0], z=pz, l=q)
    own_factors = to_column(FS[0:1, :])

    FA[x, h, c, z, l] = (values_a * own_factors[BLOCK:] * AG[...]).astype(BF16)
    ama = rings_x_y_z(FA, pl.ds(0, KAMA), 0)
    ama[0][0]()

    def take_rows(rr, d, factors):
        XG[c, rr] = (XR[rr].astype(F32) * factors[:BLOCK] * PG[...]).astype(BF16)
        send(XG.at[c, rr], XG.at[c, rr], s_bs.at[d], s_br.at[d], c=sib)

    take_rows(r, 7, own_factors)
    for cp in late:
        cp.start()
    recv(FR, s_frr.at[0])
    for d in range(7):
        pz, q = zl(d, -1)
        rr = pz * 2 + q
        recv(XR.at[rr], s_xr.at[d])
        take_rows(rr, d, to_column(FR[d, 0:1, :]))

    ama[0][1]()
    ama[0][2]()

    for d in range(7):
        pz, q = zl(d, -1)
        recv(XG.at[sib, pz * 2 + q], s_br.at[d])
    recv(XG.at[sib, r], s_br.at[7])

    gates, ups = pl.ds(0, CHUNK), pl.ds(CHUNK, CHUNK)

    def piece(j, p, cols, xfirst):
        return PB.at[j, p, :, :, cols] if xfirst else YR.at[j - XFIRST, p, :, cols]

    def slot(ref, j, n, xfirst):
        return ref.at[j, n] if xfirst else ref.at[j, n, 0]

    def slots(ref, j, xfirst):
        return ref.at[j] if xfirst else ref.at[j, :, 0]

    def first_sends(j, xfirst):
        for p, cols, ref, n, k, to in (
            (xo, gates, M1, 0, 0, xn), (xo, ups, M1, 1, 0, xp),
            (xn, ups, SR, 0, 1, xn), (xp, gates, SR, 1, 1, xp),
        ):
            go(piece(j, p, cols, xfirst), slot(ref, j, n, xfirst), s_rs.at[j, 0], s_rr.at[j, k], x=to)

    def product(j):
        for i, ref in enumerate((gate, up)):
            wlocal(j, i, ref).wait()
            recv(wpart(j, sib, i), s_wr.at[j, i])

        def block(q, _):
            quad = pl.ds(q * 4, 4)
            lhs = jnp.concatenate([XG[k, quad].reshape(256, KDIM) for k in range(2)], axis=1)
            PB[j, pl.ds(q * 2, 2)] = dot(lhs, W[j]).astype(BF16).reshape(2, 2, BLOCK, 2 * CHUNK)
            return 0

        lax.fori_loop(0, 2, block, 0)

    def products(i, _):
        product(i)
        first_sends(i, True)

        @pl.when(i < YFIRST)
        def _():
            j = i + XFIRST
            product(j)
            go(PB.at[j, :, 1 - h], YR.at[i], s_rs.at[j, 2], s_rr.at[j, 2], h=1 - h)

        return 0

    lax.fori_loop(0, XFIRST, products, 0)

    ama[0][3]()
    ama[1][0]()

    ids = t * WIDE + r * (16 * WIDE) + lax.broadcasted_iota(jnp.int32, (16, WIDE), 1)
    per_prompt = jnp.zeros((16, WIDE), F32)
    for k in range(24):
        per_prompt += (picks[:, k : k + 1] == ids).astype(F32)
    chosen = (lax.broadcasted_iota(jnp.int32, (16, ROWS), 0) == prompt[...]).astype(F32)
    CNT[...] = lax.dot_general(
        chosen.astype(BF16), per_prompt.astype(BF16), (((0,), (0,)), ((), ())),
        preferred_element_type=F32,
    )

    ama[1][1]()
    ama[1][2]()
    ama[1][3]()
    ama[2][0]()

    def add_and_pass(j, xfirst):
        recv(slots(M1, j, xfirst), s_rr.at[j, 0])
        for n, p, cols in ((0, xn, gates), (1, xp, ups)):
            ref = slot(M1, j, n, xfirst)
            ref[...] = (ref[...].astype(F32) + piece(j, p, cols, xfirst)[...].astype(F32)).astype(BF16)
            go(ref, slot(SR, j, n + 2, xfirst), s_rs.at[j, 1], s_rr.at[j, 1], x=p)

    def ring_sums(j, xfirst):
        recv(slots(SR, j, xfirst), s_rr.at[j, 1])
        terms = [slot(SR, j, n, xfirst)[...].astype(F32) for n in range(4)]
        g = piece(j, x, gates, xfirst)[...].astype(F32) + terms[1] + terms[2]
        u = piece(j, x, ups, xfirst)[...].astype(F32) + terms[0] + terms[3]
        return g, u

    def put_hidden(j, g, u):
        HID[c, j, x, h] = (g / (1.0 + jnp.exp(-g)) * u).astype(BF16)

    def around(j, own):
        go(own, own, s_hs.at[j, 1], s_hr.at[j, 1], x=xn)
        go(own, own, s_hs.at[j, 1], s_hr.at[j, 2], x=xp)

    def halves_on(j, blocks):
        for p, q, n, first_row in ((xp, xn, 1, 0), (xn, xp, 2, 32)):
            recv(blocks(p, pl.ds(0, BLOCK)), s_hr.at[j, n])
            part = blocks(p, pl.ds(first_row, 32))
            go(part, part, s_hs.at[j, 2], s_hr.at[j, 3], x=q)

    def core_copy(j):
        return remote(HID.at[c, j], HID.at[c, j], s_cs.at[j], s_cr.at[j], c=sib)

    def use_chunk(j):
        recv(HID.at[sib, j], s_cr.at[j])

        def block(q, _):
            rows = pl.ds(aligned(q * 256, 256), 256)
            pair = pl.ds(q * 2, 2)
            lhs = jnp.concatenate([HID[k, j, pair].reshape(256, CHUNK) for k in range(2)], axis=1)
            rhs = jnp.concatenate(
                [DOWN[pl.ds(aligned(k * HALF + j * CHUNK, CHUNK), CHUNK), :] for k in range(2)], axis=0
            )
            ACC[rows, :] += dot(lhs, rhs)
            return 0

        lax.fori_loop(0, 2, block, 0)

    def x0(j):
        add_and_pass(j, True)

    def x1(j):
        g, u = ring_sums(j, True)
        T[j, :, :, gates] = g
        T[j, :, :, ups] = u
        HS[j] = T[j, 1 - h].astype(BF16)
        go(HS.at[j], HR.at[j], s_rs.at[j, 2], s_rr.at[j, 2], h=1 - h)

    def x2(j):
        recv(HR.at[j], s_rr.at[j, 2])
        both = T[j, h] + HR[j].astype(F32)
        put_hidden(j, both[:, :CHUNK], both[:, CHUNK:])
        own = HID.at[c, j, x, h]
        go(own, own, s_hs.at[j, 0], s_hr.at[j, 0], h=1 - h)

    def x3(j):
        recv(HID.at[c, j, x, 1 - h], s_hr.at[j, 0])
        around(j, HID.at[c, j, x])

    def x4(j):
        halves_on(j, lambda p, rows: HID.at[c, j, p, :, rows])

    def x5(j):
        recv(HID.at[c, j, xo], s_hr.at[j, 3])
        core_copy(j).start()

    def y0(i):
        j = i + XFIRST
        recv(YR.at[i], s_rr.at[j, 2])
        YR[i] = (YR[i].astype(F32) + PB[j, :, h].astype(F32)).astype(BF16)
        first_sends(j, False)

    def y1(i):
        add_and_pass(i + XFIRST, False)

    def y2(i):
        j = i + XFIRST
        g, u = ring_sums(j, False)
        put_hidden(j, g, u)
        around(j, HID.at[c, j, x, h])

    def y3(i):
        j = i + XFIRST
        halves_on(j, lambda p, rows: HID.at[c, j, p, h, rows])

    def y4(i):
        j = i + XFIRST
        recv(HID.at[c, j, xo, h], s_hr.at[j, 3])
        got = HID.at[c, j, :, h]
        go(got, got, s_hs.at[j, 0], s_hr.at[j, 0], h=1 - h)

    def y5(i):
        j = i + XFIRST
        recv(HID.at[c, j, :, 1 - h], s_hr.at[j, 0])
        core_copy(j).start()

    def y6(i):
        use_chunk(i + XFIRST)

    xstages = (x0, x1, x2, x3, x4, x5, use_chunk)
    ystages = (y0, y1, y2, y3, y4, y5, y6)
    ACC[...] = jnp.zeros_like(ACC)
    late[0].wait()
    a_places = ama[2][4]
    ama_cols = pl.ds(0, KAMA)

    def stages(n, _):
        for k in reversed(range(7)):
            for many, steps in ((YFIRST, ystages), (XFIRST, xstages)):
                pl.when((n - k >= 0) & (n - k < many))(functools.partial(steps[k], n - k))

        return 0

    lax.fori_loop(0, 5, stages, 0)
    ama[2][1]()
    ama[2][2]()
    lax.fori_loop(5, 8, stages, 0)
    ama[2][3]()
    for k in range(4):
        to_core(FA, a_set, a_places[k], ama_cols, 0, k)
    lax.fori_loop(8, XFIRST + 6, stages, 0)

    late[1].wait()
    for n in range(4):
        from_other(FA, a_set, a_places[n], ama_cols, 0, n)

    def ama_block(q, _):
        rows = pl.ds(aligned(q * 256, 256), 256)
        LA[rows, :] = jnp.zeros((256, WIDE), F32)

        def part(k, _):
            lhs = jnp.concatenate(
                [FA[k, n // 2, n % 2, pl.ds(q * 2, 2)].reshape(256, KAMA) for n in range(4)], axis=1
            )
            LA[rows, :] += dot(lhs, AHEAD[pl.ds(aligned(k * 4 * KAMA, 4 * KAMA), 4 * KAMA), :])
            return 0

        lax.fori_loop(0, 4, part, 0)
        return 0

    lax.fori_loop(0, 2, ama_block, 0)

    for q in range(8):
        OB[q] = ACC[q * BLOCK : (q + 1) * BLOCK, :].astype(BF16)
    for d in range(7):
        pz, q = zl(d, 1)
        send(OB.at[pz * 2 + q], OR.at[d], s_os.at[d], s_or.at[0], z=pz, l=q)
    layer = values_x + ACC[pl.ds(aligned(r * BLOCK, BLOCK), BLOCK), :]
    recv(OR, s_or.at[0])
    for d in range(7):
        layer += OR[d].astype(F32)
    FE[x, h, c, z, l] = (layer * OG[...]).astype(BF16)

    low, high = pl.ds(0, 256), pl.ds(256, 256)
    one = rings_x_y_z(FE, low, 3, split=True)
    two = rings_z_y_x(FE, high, 7)
    one[0][0]()
    two[0][0]()

    squares = jnp.sum(layer * layer, axis=1, keepdims=True)
    squares = jnp.concatenate([squares, squares], axis=0)
    SFS[...] = jnp.broadcast_to(to_row(squares), (8, 128))
    for d in range(15):
        px, ph, pc = tp(d, 1)
        send(SFS, SF.at[d], s_sfs.at[d], s_sfr.at[0], x=px, h=ph, c=pc)

    for g in (one[0], two[0]):
        g[1]()
        g[2]()
    y_order = one[1][4]
    last_one = [one[2](p, n) for n, p in enumerate(y_order)]
    last_two = [two[2](p, n) for n, p in enumerate(y_order)]
    for g, n, e in ((one[0], one[1], last_one), (two[0], two[1], last_two)):
        g[3]()
        n[0]()
        e[0][0]()
    for k in (1, 2):
        for n, e in ((one[1], last_one), (two[1], last_two)):
            n[k]()
            e[k][0]()

    recv(SF, s_sfr.at[0])
    total = SFS[...]
    for d in range(15):
        total += SF[d]
    SGS[...] = total
    for d in range(7):
        pz, q = zl(d, 1)
        send(SGS, SG.at[d], s_sgs.at[d], s_sgr.at[0], z=pz, l=q)

    for n, e in ((one[1], last_one), (two[1], last_two)):
        n[3]()
        e[3][0]()
    to_core(FE, a_set, z, low, 1, 0)
    to_core(FE, b_set, x, high, 2, 0)
    late[2].wait()
    late[3].wait()
    LE[...] = jnp.zeros_like(LE)

    def use_a(p):
        def part(k, _):
            lhs = jnp.concatenate(
                [FE[k, n // 2, n % 2, p, :, :, 0:256].reshape(128, 256) for n in range(4)], axis=1
            )
            rows = pl.ds(aligned(p * 128, 128), 128)
            LE[rows, :] += dot(lhs, HEADA[pl.ds(k * 4, 4)].reshape(1024, WIDE))
            return 0

        lax.fori_loop(0, 4, part, 0)

    def use_b(p):
        def part(q, _):
            pair = pl.ds(q * 2, 2)
            lhs = jnp.concatenate(
                [FE[p, n // 2, n % 2, pair, :, :, 256:512].reshape(256, 256) for n in range(4)], axis=1
            )
            rows = pl.ds(aligned(q * 256, 256), 256)
            LE[rows, :] += dot(lhs, HEADB[pl.ds(p * 4, 4)].reshape(1024, WIDE))
            return 0

        lax.fori_loop(0, 2, part, 0)

    za, xb = last_one[0][4], last_two[0][4]
    for n in range(4):
        for e in (last_one, last_two):
            e[n][1]()
            e[n][2]()
    for n in (1, 2):
        to_core(FE, a_set, za[n], low, 1, n)
        to_core(FE, b_set, xb[n], high, 2, n)
    for n in range(3):
        from_other(FE, a_set, za[n], low, 1, n)
        use_a(za[n])
        from_other(FE, b_set, xb[n], high, 2, n)
        use_b(xb[n])

    recv(SG, s_sgr.at[0])
    for q in range(4):
        ls = to_column(lscale[q : q + 1, :])
        RE[1, pl.ds(q * 128, 128), :] = jnp.broadcast_to(ls, (128, 128))

    def row_factors(rr, line):
        rows = pl.ds(aligned(rr * BLOCK, BLOCK), BLOCK)
        col = lax.rsqrt(to_column(line)[:BLOCK] / DE + norm_epsilon)
        RE[0, rows, :] = col * RE[1, rows, :]

    row_factors(r, SGS[0:1, :])
    for d in range(7):
        pz, q = zl(d, -1)
        row_factors(pz * 2 + q, SG[d, 0:1, :])

    for n in range(4):
        for e in (last_one, last_two):
            e[n][3]()
    to_core(FE, a_set, za[3], low, 1, 3)
    to_core(FE, b_set, xb[3], high, 2, 3)
    from_other(FE, a_set, za[3], low, 1, 3)
    use_a(za[3])
    from_other(FE, b_set, xb[3], high, 2, 3)
    use_b(xb[3])

    vmask = valid[...].astype(F32)
    half_valid = contrast_weight * vmask
    for q in range(4):
        rows = pl.ds(q * 128, 128)
        le = LE[rows, :] * RE[0, rows, 0:1]
        la = LA[rows, :] * RE[1, rows, 0:1]
        me = jnp.max(le, axis=1, keepdims=True)
        ma = jnp.max(la, axis=1, keepdims=True)
        se = jnp.sum(jnp.exp(le - me), axis=1, keepdims=True)
        sa = jnp.sum(jnp.exp(la - ma), axis=1, keepdims=True)
        raw = le - half_valid * la - hamming_weight * CNT[rows, :]
        LE[rows, :] = raw
        local(LE.at[rows], raw_out.at[rows], s_out.at[q]).start()
        used = jnp.broadcast_to(vmask, raw.shape) > 0.5
        m1 = jnp.max(jnp.where(used, raw, LOWEST), axis=1, keepdims=True)
        m0 = jnp.max(jnp.where(used, LOWEST, raw), axis=1, keepdims=True)
        lines = [to_row(v) for v in (me, se, ma, sa, m1, m0, me, me)]
        SBUF[0, c, :, rows] = jnp.concatenate(lines, axis=0)

    def merge(parts):
        me = functools.reduce(jnp.maximum, [p[0:1] for p in parts])
        ma = functools.reduce(jnp.maximum, [p[2:3] for p in parts])
        se = sum(p[1:2] * jnp.exp(p[0:1] - me) for p in parts)
        sa = sum(p[3:4] * jnp.exp(p[2:3] - ma) for p in parts)
        m1 = functools.reduce(jnp.maximum, [p[4:5] for p in parts])
        m0 = functools.reduce(jnp.maximum, [p[5:6] for p in parts])
        return jnp.concatenate([me, se, ma, sa, m1, m0, me, me], axis=0)

    mine = SBUF.at[0, c]
    send(mine, mine, s_qs.at[0, 0], s_qr.at[0, 0], c=sib)
    recv(SBUF.at[0, sib], s_qr.at[0, 0])
    merged = merge([SBUF[0, 0], SBUF[0, 1]])
    for phase, (me, place) in enumerate(
        ((x, lambda p: dict(x=p)), (y, y_place), (z, lambda p: dict(z=p))), start=1
    ):
        SBUF[phase, me] = merged
        mine = SBUF.at[phase, me]
        for d in range(1, 4):
            send(mine, mine, s_qs.at[phase, d], s_qr.at[phase, d], **place(lax.rem(me + d, 4)))
        for d in range(1, 4):
            recv(SBUF.at[phase, lax.rem(me + 4 - d, 4)], s_qr.at[phase, d])
        merged = merge([SBUF[phase, k] for k in range(4)])

    stats_out[...] = merged
    for q in range(4):
        rows = pl.ds(q * 128, 128)
        local(LE.at[rows], raw_out.at[rows], s_out.at[q]).wait()

    for cp in sends:
        cp.wait_send()
    for wait in later:
        wait()

    def drain(j, _):
        def sent(region, sem):
            remote(region, region, sem, sem, c=sib).wait_send()

        @pl.when(j < XFIRST)
        def _():
            sent(SR.at[j], s_rs.at[j, 0])
            sent(M1.at[j], s_rs.at[j, 1])
            sent(HR.at[j], s_rs.at[j, 2])
            sent(HID.at[c, j, x, h], s_hs.at[j, 0])
            sent(HID.at[c, j, pl.ds(0, 2)], s_hs.at[j, 1])
            sent(HID.at[c, j, x], s_hs.at[j, 2])

        @pl.when(j >= XFIRST)
        def _():
            sent(SR.at[j, :, 0], s_rs.at[j, 0])
            sent(M1.at[j, :, 0], s_rs.at[j, 1])
            sent(YR.at[j - XFIRST], s_rs.at[j, 2])
            sent(HID.at[c, j, :, h], s_hs.at[j, 0])
            sent(HID.at[c, j, x], s_hs.at[j, 1])
            sent(HID.at[c, j, x, h], s_hs.at[j, 2])

        core_copy(j).wait_send()
        return 0

    lax.fori_loop(0, CHUNKS, drain, 0)


def finish(raw, stats, valid, scores, best):
    shift_e = stats[0:1, :] + jnp.log(stats[1:2, :])
    shift_a = stats[2:3, :] + jnp.log(stats[3:4, :])
    best[...] = jnp.maximum(
        stats[4:5, :] - shift_e + contrast_weight * shift_a, stats[5:6, :] - shift_e
    )
    half_valid = contrast_weight * valid[...].astype(F32)
    for q in range(4):
        rows = slice(q * 128, (q + 1) * 128)
        back = half_valid * to_column(shift_a[:, rows]) - to_column(shift_e[:, rows])
        scores[rows, :] = raw[rows, :] + back


def body(
    exp_hidden, exp_pre_gain, exp_gate, exp_up, exp_down, exp_out_gain, exp_head,
    ama_hidden, ama_out_gain, ama_head, logit_scale, prompt_of, prior_picks, valid_mask,
):
    hbm = pl.BlockSpec(memory_space=pl.ANY)
    vmem = pl.BlockSpec(memory_space=pltpu.VMEM)
    dma = pltpu.SemaphoreType.DMA
    scratch = [
        pltpu.VMEM((8, BLOCK, KDIM), BF16),
        pltpu.VMEM((2, 8, BLOCK, KDIM), BF16),
        pltpu.VMEM((CHUNKS, 2 * KDIM, 2 * CHUNK), BF16),
        pltpu.VMEM((2 * HALF, KDIM), BF16),
        pltpu.VMEM((16, 256, WIDE), BF16),
        pltpu.VMEM((16, 256, WIDE), BF16),
        pltpu.VMEM((DA, WIDE), BF16),
        pltpu.VMEM((CHUNKS, 4, 2, BLOCK, 2 * CHUNK), BF16),
        pltpu.VMEM((CHUNKS, 2, 2, BLOCK, CHUNK), BF16),
        pltpu.VMEM((CHUNKS, 4, 2, BLOCK, CHUNK), BF16),
        pltpu.VMEM((XFIRST, 2, BLOCK, 2 * CHUNK), F32),
        pltpu.VMEM((XFIRST, BLOCK, 2 * CHUNK), BF16),
        pltpu.VMEM((XFIRST, BLOCK, 2 * CHUNK), BF16),
        pltpu.VMEM((YFIRST, 4, BLOCK, 2 * CHUNK), BF16),
        pltpu.VMEM((2, CHUNKS, 4, 2, BLOCK, CHUNK), BF16),
        pltpu.VMEM((ROWS, KDIM), F32),
        pltpu.VMEM((8, BLOCK, KDIM), BF16),
        pltpu.VMEM((7, BLOCK, KDIM), BF16),
        pltpu.VMEM((4, 2, 2, 4, 2, BLOCK, KDIM), BF16),
        pltpu.VMEM((4, 2, 2, 4, 2, BLOCK, KAMA), BF16),
        pltpu.VMEM((BLOCK, KAMA), BF16),
        pltpu.VMEM((ROWS, WIDE), F32),
        pltpu.VMEM((ROWS, WIDE), F32),
        pltpu.VMEM((8, 128), F32),
        pltpu.VMEM((15, 8, 128), F32),
        pltpu.VMEM((8, 128), F32),
        pltpu.VMEM((7, 8, 128), F32),
        pltpu.VMEM((8, 128), F32),
        pltpu.VMEM((15, 8, 128), F32),
        pltpu.VMEM((8, 128), F32),
        pltpu.VMEM((7, 8, 128), F32),
        pltpu.VMEM((2, ROWS, 128), F32),
        pltpu.VMEM((ROWS, WIDE), F32),
        pltpu.VMEM((4, 4, 8, ROWS), F32),
        pltpu.VMEM((1, KDIM), F32),
        pltpu.VMEM((1, KDIM), F32),
        pltpu.VMEM((1, KAMA), F32),
        dma((9,)), dma((CHUNKS, 2)), dma((CHUNKS, 2)), dma((CHUNKS, 2)),
        dma((7,)), dma((7,)), dma((8,)), dma((8,)), dma((15,)), dma((1,)), dma((7,)), dma((1,)),
        dma((CHUNKS, 3)), dma((CHUNKS, 3)), dma((CHUNKS, 3)), dma((CHUNKS, 4)),
        dma((CHUNKS,)), dma((CHUNKS,)), dma((7,)), dma((1,)),
        dma((17, 4)), dma((17, 4)), dma((3, 4)), dma((3, 4)),
        dma((15,)), dma((1,)), dma((7,)), dma((1,)), dma((4, 4)), dma((4, 4)), dma((4,)),
    ]
    raw, stats = pl.pallas_call(
        kernel,
        out_shape=(
            jax.ShapeDtypeStruct((ROWS, WIDE), F32),
            jax.ShapeDtypeStruct((8, ROWS), F32),
        ),
        in_specs=[hbm] * 10 + [vmem] * 4,
        out_specs=(hbm, vmem),
        scratch_shapes=scratch,
        compiler_params=pltpu.CompilerParams(
            collective_id=0, has_side_effects=True, vmem_limit_bytes=63 * 1024 * 1024
        ),
        cost_estimate=pl.CostEstimate(
            flops=12_000_000_000, bytes_accessed=25_000_000, transcendentals=600_000
        ),
    )(
        exp_hidden, exp_pre_gain.reshape(1, KDIM), exp_gate, exp_up, exp_down,
        exp_out_gain.reshape(1, KDIM), exp_head.reshape(16, KDIM, WIDE), ama_hidden, ama_out_gain.reshape(1, KAMA),
        ama_head, logit_scale.reshape(4, 128), prompt_of.reshape(1, ROWS), prior_picks,
        valid_mask.reshape(1, WIDE),
    )
    scores, best = pl.pallas_call(
        finish,
        out_shape=(
            jax.ShapeDtypeStruct((ROWS, WIDE), F32),
            jax.ShapeDtypeStruct((1, ROWS), F32),
        ),
        in_specs=[vmem] * 3,
        out_specs=(vmem, vmem),
    )(raw, stats, valid_mask.reshape(1, WIDE))
    return scores, best.reshape(ROWS)


def solution(mesh):
    torus = Mesh(mesh.devices.reshape(4, 2, 4, 2, 2), AXES)
    in_specs = (
        P(REP, TP), P(TP), P(TP, REP), P(TP, REP), P(REP, TP), P(TP), P(None, ALL),
        P(REP, TP), P(TP), P(None, ALL), P(), P(), P(), P(ALL),
    )
    out_specs = (P(None, ALL), P())
    return jax.shard_map(body, mesh=torus, in_specs=in_specs, out_specs=out_specs, check_vma=False)
```

```python
import functools

import jax
import jax.numpy as jnp
from jax import lax
from jax.experimental import pallas as pl
from jax.experimental.pallas import tpu as pltpu
from jax.sharding import Mesh
from jax.sharding import PartitionSpec as P

DE = 8192
DA = 4096
AXES = ("z", "l", "x", "h", "c")
REP = ("z", "l")
TP = ("x", "h", "c")
ALL = REP + TP

norm_epsilon = 1e-05
contrast_weight = 0.5
hamming_weight = 0.7
LOWEST = -3.0e38

ROWS = 512
BLOCK = 64
KDIM = 512
HALF = 1792
CHUNK = 256
CHUNKS = HALF // CHUNK
XFIRST = 4
YFIRST = CHUNKS - XFIRST
KAMA = 256
WIDE = 512
BF16 = jnp.bfloat16
F32 = jnp.float32

XH = [(d // 2, d % 2) for d in range(1, 8)]
TPO = [(d // 4, (d // 2) % 2, d % 2) for d in range(1, 16)]
ZL = [(d // 2, d % 2) for d in range(1, 8)]


def dot(a, b):
    return jnp.dot(a, b, preferred_element_type=F32)


def eye128():
    return lax.broadcasted_iota(jnp.int32, (128, 128), 0) == lax.broadcasted_iota(
        jnp.int32, (128, 128), 1
    )


def to_row(column):
    return jnp.sum(jnp.where(eye128(), jnp.broadcast_to(column, (128, 128)), 0.0), 0, keepdims=True)


def to_column(row):
    return jnp.sum(jnp.where(eye128(), jnp.broadcast_to(row, (128, 128)), 0.0), 1, keepdims=True)


def aligned(v, m):
    return pl.multiple_of(v, m)


def kernel(
    hid_in, pre_gain, gate, up, down, out_gain, head, ama_in, ama_gain, ahead,
    lscale, prompt, picks, valid,
    raw_out, stats_out,
    XR, XG, W, DOWN, HEADA, HEADB, AHEAD, PB, M1, SR, T, HS, HR, YR, HID, ACC, OB, OR, FE, FA, AIN, LE, LA,
    STS, ST, FS, FR, SFS, SF, SGS, SG, RE, CNT, SBUF, PG, OG, AG,
    s_loc, s_wl, s_ws, s_wr, s_xs, s_xr, s_bs, s_br, s_sts, s_str, s_frs, s_frr,
    s_rs, s_rr, s_hs, s_hr, s_cs, s_cr, s_os, s_or, s_rings, s_ringr, s_fs, s_fr,
    s_sfs, s_sfr, s_sgs, s_sgr, s_qs, s_qr, s_out,
):
    z, l, x, h, c = (lax.axis_index(a) for a in AXES)
    sib = 1 - c
    r = z * 2 + l
    b = x * 2 + h
    t = x * 4 + h * 2 + c
    y = h * 2 + l
    xp, xn, xo = lax.rem(x + 3, 4), lax.rem(x + 1, 4), lax.rem(x + 2, 4)

    def remote(src, dst, ss, rs, **where):
        return pltpu.make_async_remote_copy(
            src_ref=src, dst_ref=dst, send_sem=ss, recv_sem=rs,
            device_id=where, device_id_type=pl.DeviceIdType.MESH,
        )

    sends = []

    def send(src, dst, ss, rs, **where):
        cp = remote(src, dst, ss, rs, **where)
        cp.start()
        sends.append(cp)

    later = []

    def send_set(region, ss, rs, where):
        remote(region(), region(), ss, rs, **where()).start()
        later.append(lambda: remote(region(), region(), ss, rs, **where()).wait_send())

    def go(src, dst, ss, rs, **where):
        remote(src, dst, ss, rs, **where).start()

    def recv(dst, rs):
        remote(dst, dst, rs, rs, c=sib).wait_recv()

    def local(src, dst, sem):
        return pltpu.make_async_copy(src, dst, sem)

    def zl(d, sign):
        dz, dl = ZL[d]
        return lax.rem(z + sign * dz + 4, 4), lax.rem(l + dl, 2)

    def xh(d, sign):
        dx, dh = XH[d]
        return lax.rem(x + sign * dx + 4, 4), lax.rem(h + dh, 2)

    def tp(d, sign):
        dx, dh, dc = TPO[d]
        return lax.rem(x + sign * dx + 4, 4), lax.rem(h + dh, 2), lax.rem(c + dc, 2)

    def wcols(half, j):
        return pl.ds(aligned(half * HALF + j * CHUNK, 128), CHUNK)

    def wpart(j, core, i):
        rows = pl.ds(aligned(core * KDIM, KDIM), KDIM)
        return W.at[j, rows, pl.ds(i * CHUNK, CHUNK)]

    def wlocal(j, i, ref):
        return local(ref.at[:, wcols(c, j)], wpart(j, c, i), s_wl.at[j, i])

    first = [
        local(hid_in, XR.at[r], s_loc.at[0]),
        local(pre_gain, PG, s_loc.at[1]),
        local(ama_in, AIN, s_loc.at[2]),
        local(ama_gain, AG, s_loc.at[3]),
        local(out_gain, OG, s_loc.at[4]),
    ]
    for cp in first:
        cp.start()
    for j in (0, 4, 1, 5, 2, 6, 3):
        wlocal(j, 0, gate).start()
        wlocal(j, 1, up).start()
    late = [
        local(down, DOWN, s_loc.at[5]),
        local(ahead, AHEAD, s_loc.at[6]),
        local(head.at[:, pl.ds(0, 256), :], HEADA, s_loc.at[7]),
        local(head.at[:, pl.ds(256, 256), :], HEADB, s_loc.at[8]),
    ]

    barrier = pltpu.get_barrier_semaphore()

    def greet(**where):
        pl.semaphore_signal(barrier, inc=1, device_id=where, device_id_type=pl.DeviceIdType.MESH)

    for d in range(7):
        pz, q = zl(d, 1)
        greet(z=pz, l=q)
    for d in range(15):
        px, ph, pc = tp(d, 1)
        greet(x=px, h=ph, c=pc)
    greet(h=1 - h, l=1 - l)
    pl.semaphore_wait(barrier, 23)

    for d in range(7):
        pz, q = zl(d, 1)
        send(hid_in, XR.at[r], s_xs.at[d], s_xr.at[d], z=pz, l=q)
    for j in (0, 4, 1, 5, 2, 6, 3):
        for i, ref in enumerate((gate, up)):
            send(
                ref.at[:, wcols(sib, j)], wpart(j, c, i),
                s_ws.at[j, i], s_wr.at[j, i], c=sib,
            )

    def ring(index, sets, places, me):
        prv, nxt = lax.rem(me + 3, 4), lax.rem(me + 1, 4)
        opp = lax.rem(me + 2, 4)
        lo, hi = pl.ds(0, 32), pl.ds(32, 32)
        full = pl.ds(0, 64)

        def pass_on(p, rows, q, n):
            send_set(
                lambda: sets(p, rows), s_rings.at[index, n], s_ringr.at[index, n], lambda: places(q)
            )

        def start():
            pass_on(me, full, nxt, 0)
            pass_on(me, full, prv, 1)

        def pass_next():
            recv(sets(prv, full), s_ringr.at[index, 0])
            pass_on(prv, lo, nxt, 2)

        def pass_prev():
            recv(sets(nxt, full), s_ringr.at[index, 1])
            pass_on(nxt, hi, prv, 3)

        def finish():
            recv(sets(opp, lo), s_ringr.at[index, 2])
            recv(sets(opp, hi), s_ringr.at[index, 3])

        return start, pass_next, pass_prev, finish, (me, prv, nxt, opp)

    def spread(index, sets, places, me):
        full = pl.ds(0, 64)

        def to(d):
            send_set(
                lambda: sets(me, full), s_rings.at[index, d], s_ringr.at[index, d],
                lambda: places(lax.rem(me + d, 4)),
            )

        def start():
            for d in (1, 3, 2):
                to(d)

        def finish():
            for d in (1, 3, 2):
                recv(sets(lax.rem(me + 4 - d, 4), full), s_ringr.at[index, d])

        return start, finish

    def y_place(p):
        return dict(h=lax.div(p, 2), l=lax.rem(p, 2))

    every4, every2 = pl.ds(0, 4), pl.ds(0, 2)

    def rings_x_y_z(ref, cols, first_index, split=False):
        a = ring(first_index, lambda p, k: ref.at[p, h, c, z, l, k, cols], lambda p: dict(x=p), x)
        bb = ring(
            first_index + 1,
            lambda p, k: ref.at[every4, lax.div(p, 2), c, z, lax.rem(p, 2), k, cols], y_place, y,
        )
        if split:
            def d(yy, n):
                return ring(
                    first_index + 6 + n,
                    lambda p, k: ref.at[every4, lax.div(yy, 2), c, p, lax.rem(yy, 2), k, cols],
                    lambda p: dict(z=p), z,
                )
        else:
            d = ring(
                first_index + 2,
                lambda p, k: ref.at[every4, every2, c, p, every2, k, cols], lambda p: dict(z=p), z,
            )
        return a, bb, d

    def rings_z_y_x(ref, cols, first_index):
        a = ring(first_index, lambda p, k: ref.at[x, h, c, p, l, k, cols], lambda p: dict(z=p), z)
        bb = ring(
            first_index + 1,
            lambda p, k: ref.at[x, lax.div(p, 2), c, every4, lax.rem(p, 2), k, cols], y_place, y,
        )

        def d(yy, n):
            return ring(
                first_index + 6 + n,
                lambda p, k: ref.at[p, lax.div(yy, 2), c, every4, lax.rem(yy, 2), k, cols],
                lambda p: dict(x=p), x,
            )

        return a, bb, d

    def a_set(ref, cc, p, cols):
        return ref.at[every4, every2, cc, p, every2, pl.ds(0, 64), cols]

    def b_set(ref, cc, p, cols):
        return ref.at[p, every2, cc, every4, every2, pl.ds(0, 64), cols]

    def to_core(ref, maker, p, cols, index, n):
        send_set(
            lambda: maker(ref, c, p, cols), s_fs.at[index, n], s_fr.at[index, n], lambda: dict(c=sib)
        )

    def from_other(ref, maker, p, cols, index, n):
        recv(maker(ref, sib, p, cols), s_fr.at[index, n])

    for cp in first:
        cp.wait()
    values_x = XR[r].astype(F32)
    values_a = AIN[...].astype(F32)
    squares = jnp.concatenate(
        [jnp.sum(v * v, axis=1, keepdims=True) for v in (values_x, values_a)], axis=0
    )
    STS[...] = jnp.broadcast_to(to_row(squares), (8, 128))
    for d in range(15):
        px, ph, pc = tp(d, 1)
        send(STS, ST.at[d], s_sts.at[d], s_str.at[0], x=px, h=ph, c=pc)
    recv(ST, s_str.at[0])
    total = STS[...]
    for d in range(15):
        total += ST[d]
    lane = lax.broadcasted_iota(jnp.int32, (8, 128), 1)
    means = jnp.where(lane < BLOCK, total / DE, total / DA)
    FS[...] = lax.rsqrt(means + norm_epsilon)
    for d in range(7):
        pz, q = zl(d, 1)
        send(FS, FR.at[d], s_frs.at[d], s_frr.at[0], z=pz, l=q)
    own_factors = to_column(FS[0:1, :])

    FA[x, h, c, z, l] = (values_a * own_factors[BLOCK:] * AG[...]).astype(BF16)
    ama_cols = pl.ds(0, KAMA)
    ama = rings_x_y_z(FA, ama_cols, 0)
    ama_x = spread(
        0, lambda p, k: FA.at[p, h, c, z, l, k, ama_cols], lambda p: dict(x=p), x
    )
    ama_y = spread(
        1, lambda p, k: FA.at[every4, lax.div(p, 2), c, z, lax.rem(p, 2), k, ama_cols], y_place, y
    )
    ama_x[0]()

    def take_rows(rr, d, factors):
        XG[c, rr] = (XR[rr].astype(F32) * factors[:BLOCK] * PG[...]).astype(BF16)
        send(XG.at[c, rr], XG.at[c, rr], s_bs.at[d], s_br.at[d], c=sib)

    take_rows(r, 7, own_factors)
    for cp in late:
        cp.start()
    recv(FR, s_frr.at[0])
    for d in range(7):
        pz, q = zl(d, -1)
        rr = pz * 2 + q
        recv(XR.at[rr], s_xr.at[d])
        take_rows(rr, d, to_column(FR[d, 0:1, :]))

    ama_x[1]()
    ama_y[0]()

    for d in range(7):
        pz, q = zl(d, -1)
        recv(XG.at[sib, pz * 2 + q], s_br.at[d])
    recv(XG.at[sib, r], s_br.at[7])

    gates, ups = pl.ds(0, CHUNK), pl.ds(CHUNK, CHUNK)

    def piece(j, p, cols, xfirst):
        return PB.at[j, p, :, :, cols] if xfirst else YR.at[j - XFIRST, p, :, cols]

    def slot(ref, j, n, xfirst):
        return ref.at[j, n] if xfirst else ref.at[j, n, 0]

    def slots(ref, j, xfirst):
        return ref.at[j] if xfirst else ref.at[j, :, 0]

    def first_sends(j, xfirst):
        for p, cols, ref, n, k, to in (
            (xo, gates, M1, 0, 0, xn), (xo, ups, M1, 1, 0, xp),
            (xn, ups, SR, 0, 1, xn), (xp, gates, SR, 1, 1, xp),
        ):
            go(piece(j, p, cols, xfirst), slot(ref, j, n, xfirst), s_rs.at[j, 0], s_rr.at[j, k], x=to)

    def product(j):
        for i, ref in enumerate((gate, up)):
            wlocal(j, i, ref).wait()
            recv(wpart(j, sib, i), s_wr.at[j, i])

        def block(q, _):
            quad = pl.ds(q * 4, 4)
            lhs = jnp.concatenate([XG[k, quad].reshape(256, KDIM) for k in range(2)], axis=1)
            PB[j, pl.ds(q * 2, 2)] = dot(lhs, W[j]).astype(BF16).reshape(2, 2, BLOCK, 2 * CHUNK)
            return 0

        lax.fori_loop(0, 2, block, 0)

    def products(i, _):
        product(i)
        first_sends(i, True)

        @pl.when(i < YFIRST)
        def _():
            j = i + XFIRST
            product(j)
            go(PB.at[j, :, 1 - h], YR.at[i], s_rs.at[j, 2], s_rr.at[j, 2], h=1 - h)

        return 0

    lax.fori_loop(0, XFIRST, products, 0)


    ids = t * WIDE + r * (16 * WIDE) + lax.broadcasted_iota(jnp.int32, (16, WIDE), 1)
    per_prompt = jnp.zeros((16, WIDE), F32)
    for k in range(24):
        per_prompt += (picks[:, k : k + 1] == ids).astype(F32)
    chosen = (lax.broadcasted_iota(jnp.int32, (16, ROWS), 0) == prompt[...]).astype(F32)
    CNT[...] = lax.dot_general(
        chosen.astype(BF16), per_prompt.astype(BF16), (((0,), (0,)), ((), ())),
        preferred_element_type=F32,
    )

    ama_y[1]()
    ama[2][0]()

    def add_and_pass(j, xfirst):
        recv(slots(M1, j, xfirst), s_rr.at[j, 0])
        for n, p, cols in ((0, xn, gates), (1, xp, ups)):
            ref = slot(M1, j, n, xfirst)
            ref[...] = (ref[...].astype(F32) + piece(j, p, cols, xfirst)[...].astype(F32)).astype(BF16)
            go(ref, slot(SR, j, n + 2, xfirst), s_rs.at[j, 1], s_rr.at[j, 1], x=p)

    def ring_sums(j, xfirst):
        recv(slots(SR, j, xfirst), s_rr.at[j, 1])
        terms = [slot(SR, j, n, xfirst)[...].astype(F32) for n in range(4)]
        g = piece(j, x, gates, xfirst)[...].astype(F32) + terms[1] + terms[2]
        u = piece(j, x, ups, xfirst)[...].astype(F32) + terms[0] + terms[3]
        return g, u

    def put_hidden(j, g, u):
        HID[c, j, x, h] = (g / (1.0 + jnp.exp(-g)) * u).astype(BF16)

    def around(j, own):
        go(own, own, s_hs.at[j, 1], s_hr.at[j, 1], x=xn)
        go(own, own, s_hs.at[j, 1], s_hr.at[j, 2], x=xp)

    def halves_on(j, blocks):
        for p, q, n, first_row in ((xp, xn, 1, 0), (xn, xp, 2, 32)):
            recv(blocks(p, pl.ds(0, BLOCK)), s_hr.at[j, n])
            part = blocks(p, pl.ds(first_row, 32))
            go(part, part, s_hs.at[j, 2], s_hr.at[j, 3], x=q)

    def core_copy(j):
        return remote(HID.at[c, j], HID.at[c, j], s_cs.at[j], s_cr.at[j], c=sib)

    def use_chunk(j):
        recv(HID.at[sib, j], s_cr.at[j])

        def block(q, _):
            rows = pl.ds(aligned(q * 256, 256), 256)
            pair = pl.ds(q * 2, 2)
            lhs = jnp.concatenate([HID[k, j, pair].reshape(256, CHUNK) for k in range(2)], axis=1)
            rhs = jnp.concatenate(
                [DOWN[pl.ds(aligned(k * HALF + j * CHUNK, CHUNK), CHUNK), :] for k in range(2)], axis=0
            )
            ACC[rows, :] += dot(lhs, rhs)
            return 0

        lax.fori_loop(0, 2, block, 0)

    def x0(j):
        add_and_pass(j, True)

    def x1(j):
        g, u = ring_sums(j, True)
        T[j, :, :, gates] = g
        T[j, :, :, ups] = u
        HS[j] = T[j, 1 - h].astype(BF16)
        go(HS.at[j], HR.at[j], s_rs.at[j, 2], s_rr.at[j, 2], h=1 - h)

    def x2(j):
        recv(HR.at[j], s_rr.at[j, 2])
        both = T[j, h] + HR[j].astype(F32)
        put_hidden(j, both[:, :CHUNK], both[:, CHUNK:])
        own = HID.at[c, j, x, h]
        go(own, own, s_hs.at[j, 0], s_hr.at[j, 0], h=1 - h)

    def x3(j):
        recv(HID.at[c, j, x, 1 - h], s_hr.at[j, 0])
        around(j, HID.at[c, j, x])

    def x4(j):
        halves_on(j, lambda p, rows: HID.at[c, j, p, :, rows])

    def x5(j):
        recv(HID.at[c, j, xo], s_hr.at[j, 3])
        core_copy(j).start()

    def y0(i):
        j = i + XFIRST
        recv(YR.at[i], s_rr.at[j, 2])
        YR[i] = (YR[i].astype(F32) + PB[j, :, h].astype(F32)).astype(BF16)
        first_sends(j, False)

    def y1(i):
        add_and_pass(i + XFIRST, False)

    def y2(i):
        j = i + XFIRST
        g, u = ring_sums(j, False)
        put_hidden(j, g, u)
        around(j, HID.at[c, j, x, h])

    def y3(i):
        j = i + XFIRST
        halves_on(j, lambda p, rows: HID.at[c, j, p, h, rows])

    def y4(i):
        j = i + XFIRST
        recv(HID.at[c, j, xo, h], s_hr.at[j, 3])
        got = HID.at[c, j, :, h]
        go(got, got, s_hs.at[j, 0], s_hr.at[j, 0], h=1 - h)

    def y5(i):
        j = i + XFIRST
        recv(HID.at[c, j, :, 1 - h], s_hr.at[j, 0])
        core_copy(j).start()

    def y6(i):
        use_chunk(i + XFIRST)

    xstages = (x0, x1, x2, x3, x4, x5, use_chunk)
    ystages = (y0, y1, y2, y3, y4, y5, y6)
    ACC[...] = jnp.zeros_like(ACC)
    late[0].wait()
    a_places = ama[2][4]

    def stages(n, _):
        for k in reversed(range(7)):
            for many, steps in ((YFIRST, ystages), (XFIRST, xstages)):
                pl.when((n - k >= 0) & (n - k < many))(functools.partial(steps[k], n - k))

        return 0

    lax.fori_loop(0, 5, stages, 0)
    ama[2][1]()
    ama[2][2]()
    lax.fori_loop(5, 8, stages, 0)
    ama[2][3]()
    for k in range(4):
        to_core(FA, a_set, a_places[k], ama_cols, 0, k)
    lax.fori_loop(8, XFIRST + 6, stages, 0)

    for q in range(8):
        OB[q] = ACC[q * BLOCK : (q + 1) * BLOCK, :].astype(BF16)
    for d in range(7):
        pz, q = zl(d, 1)
        send(OB.at[pz * 2 + q], OR.at[d], s_os.at[d], s_or.at[0], z=pz, l=q)

    late[1].wait()
    for n in range(4):
        from_other(FA, a_set, a_places[n], ama_cols, 0, n)

    def ama_block(q, _):
        rows = pl.ds(aligned(q * 256, 256), 256)
        LA[rows, :] = jnp.zeros((256, WIDE), F32)

        def part(k, _):
            lhs = jnp.concatenate(
                [FA[k, n // 2, n % 2, pl.ds(q * 2, 2)].reshape(256, KAMA) for n in range(4)], axis=1
            )
            LA[rows, :] += dot(lhs, AHEAD[pl.ds(aligned(k * 4 * KAMA, 4 * KAMA), 4 * KAMA), :])
            return 0

        lax.fori_loop(0, 4, part, 0)
        return 0

    lax.fori_loop(0, 2, ama_block, 0)

    layer = values_x + ACC[pl.ds(aligned(r * BLOCK, BLOCK), BLOCK), :]
    recv(OR, s_or.at[0])
    for d in range(7):
        layer += OR[d].astype(F32)
    FE[x, h, c, z, l] = (layer * OG[...]).astype(BF16)

    low, high = pl.ds(0, 256), pl.ds(256, 256)
    one = rings_x_y_z(FE, low, 3, split=True)
    two = rings_z_y_x(FE, high, 7)
    one[0][0]()
    two[0][0]()

    squares = jnp.sum(layer * layer, axis=1, keepdims=True)
    squares = jnp.concatenate([squares, squares], axis=0)
    SFS[...] = jnp.broadcast_to(to_row(squares), (8, 128))
    for d in range(15):
        px, ph, pc = tp(d, 1)
        send(SFS, SF.at[d], s_sfs.at[d], s_sfr.at[0], x=px, h=ph, c=pc)

    for g in (one[0], two[0]):
        g[1]()
        g[2]()
    y_order = one[1][4]
    last_one = [one[2](p, n) for n, p in enumerate(y_order)]
    last_two = [two[2](p, n) for n, p in enumerate(y_order)]
    for g, n, e in ((one[0], one[1], last_one), (two[0], two[1], last_two)):
        g[3]()
        n[0]()
        e[0][0]()
    for k in (1, 2):
        for n, e in ((one[1], last_one), (two[1], last_two)):
            n[k]()
            e[k][0]()

    recv(SF, s_sfr.at[0])
    total = SFS[...]
    for d in range(15):
        total += SF[d]
    SGS[...] = total
    for d in range(7):
        pz, q = zl(d, 1)
        send(SGS, SG.at[d], s_sgs.at[d], s_sgr.at[0], z=pz, l=q)

    for n, e in ((one[1], last_one), (two[1], last_two)):
        n[3]()
        e[3][0]()
    to_core(FE, a_set, z, low, 1, 0)
    to_core(FE, b_set, x, high, 2, 0)
    late[2].wait()
    late[3].wait()
    LE[...] = jnp.zeros_like(LE)

    def use_a(p):
        def part(k, _):
            lhs = jnp.concatenate(
                [FE[k, n // 2, n % 2, p, :, :, 0:256].reshape(128, 256) for n in range(4)], axis=1
            )
            rows = pl.ds(aligned(p * 128, 128), 128)
            LE[rows, :] += dot(lhs, HEADA[pl.ds(k * 4, 4)].reshape(1024, WIDE))
            return 0

        lax.fori_loop(0, 4, part, 0)

    def use_b(p):
        def part(q, _):
            pair = pl.ds(q * 2, 2)
            lhs = jnp.concatenate(
                [FE[p, n // 2, n % 2, pair, :, :, 256:512].reshape(256, 256) for n in range(4)], axis=1
            )
            rows = pl.ds(aligned(q * 256, 256), 256)
            LE[rows, :] += dot(lhs, HEADB[pl.ds(p * 4, 4)].reshape(1024, WIDE))
            return 0

        lax.fori_loop(0, 2, part, 0)

    za, xb = last_one[0][4], last_two[0][4]
    for n in range(4):
        for e in (last_one, last_two):
            e[n][1]()
            e[n][2]()
        if n == 1:
            from_other(FE, a_set, z, low, 1, 0)
            use_a(z)
            from_other(FE, b_set, x, high, 2, 0)
            use_b(x)
    for n in (1, 2):
        to_core(FE, a_set, za[n], low, 1, n)
        to_core(FE, b_set, xb[n], high, 2, n)
    for n in (1, 2):
        from_other(FE, a_set, za[n], low, 1, n)
        use_a(za[n])
        from_other(FE, b_set, xb[n], high, 2, n)
        use_b(xb[n])

    recv(SG, s_sgr.at[0])
    for q in range(4):
        ls = to_column(lscale[q : q + 1, :])
        RE[1, pl.ds(q * 128, 128), :] = jnp.broadcast_to(ls, (128, 128))

    def row_factors(rr, line):
        rows = pl.ds(aligned(rr * BLOCK, BLOCK), BLOCK)
        col = lax.rsqrt(to_column(line)[:BLOCK] / DE + norm_epsilon)
        RE[0, rows, :] = col * RE[1, rows, :]

    row_factors(r, SGS[0:1, :])
    for d in range(7):
        pz, q = zl(d, -1)
        row_factors(pz * 2 + q, SG[d, 0:1, :])

    for n in range(4):
        for e in (last_one, last_two):
            e[n][3]()
    to_core(FE, a_set, za[3], low, 1, 3)
    to_core(FE, b_set, xb[3], high, 2, 3)
    from_other(FE, a_set, za[3], low, 1, 3)
    use_a(za[3])
    from_other(FE, b_set, xb[3], high, 2, 3)
    use_b(xb[3])

    vmask = valid[...].astype(F32)
    half_valid = contrast_weight * vmask
    for q in range(4):
        rows = pl.ds(q * 128, 128)
        le = LE[rows, :] * RE[0, rows, 0:1]
        la = LA[rows, :] * RE[1, rows, 0:1]
        me = jnp.max(le, axis=1, keepdims=True)
        ma = jnp.max(la, axis=1, keepdims=True)
        se = jnp.sum(jnp.exp(le - me), axis=1, keepdims=True)
        sa = jnp.sum(jnp.exp(la - ma), axis=1, keepdims=True)
        raw = le - half_valid * la - hamming_weight * CNT[rows, :]
        LE[rows, :] = raw
        local(LE.at[rows], raw_out.at[rows], s_out.at[q]).start()
        used = jnp.broadcast_to(vmask, raw.shape) > 0.5
        m1 = jnp.max(jnp.where(used, raw, LOWEST), axis=1, keepdims=True)
        m0 = jnp.max(jnp.where(used, LOWEST, raw), axis=1, keepdims=True)
        lines = [to_row(v) for v in (me, se, ma, sa, m1, m0, me, me)]
        SBUF[0, c, :, rows] = jnp.concatenate(lines, axis=0)

    def merge(parts):
        me = functools.reduce(jnp.maximum, [p[0:1] for p in parts])
        ma = functools.reduce(jnp.maximum, [p[2:3] for p in parts])
        se = sum(p[1:2] * jnp.exp(p[0:1] - me) for p in parts)
        sa = sum(p[3:4] * jnp.exp(p[2:3] - ma) for p in parts)
        m1 = functools.reduce(jnp.maximum, [p[4:5] for p in parts])
        m0 = functools.reduce(jnp.maximum, [p[5:6] for p in parts])
        return jnp.concatenate([me, se, ma, sa, m1, m0, me, me], axis=0)

    mine = SBUF.at[0, c]
    send(mine, mine, s_qs.at[0, 0], s_qr.at[0, 0], c=sib)
    recv(SBUF.at[0, sib], s_qr.at[0, 0])
    merged = merge([SBUF[0, 0], SBUF[0, 1]])
    for phase, (me, place) in enumerate(
        ((x, lambda p: dict(x=p)), (y, y_place), (z, lambda p: dict(z=p))), start=1
    ):
        SBUF[phase, me] = merged
        mine = SBUF.at[phase, me]
        for d in range(1, 4):
            send(mine, mine, s_qs.at[phase, d], s_qr.at[phase, d], **place(lax.rem(me + d, 4)))
        for d in range(1, 4):
            recv(SBUF.at[phase, lax.rem(me + 4 - d, 4)], s_qr.at[phase, d])
        merged = merge([SBUF[phase, k] for k in range(4)])

    stats_out[...] = merged
    for q in range(4):
        rows = pl.ds(q * 128, 128)
        local(LE.at[rows], raw_out.at[rows], s_out.at[q]).wait()

    for cp in sends:
        cp.wait_send()
    for wait in later:
        wait()

    def drain(j, _):
        def sent(region, sem):
            remote(region, region, sem, sem, c=sib).wait_send()

        @pl.when(j < XFIRST)
        def _():
            sent(SR.at[j], s_rs.at[j, 0])
            sent(M1.at[j], s_rs.at[j, 1])
            sent(HR.at[j], s_rs.at[j, 2])
            sent(HID.at[c, j, x, h], s_hs.at[j, 0])
            sent(HID.at[c, j, pl.ds(0, 2)], s_hs.at[j, 1])
            sent(HID.at[c, j, x], s_hs.at[j, 2])

        @pl.when(j >= XFIRST)
        def _():
            sent(SR.at[j, :, 0], s_rs.at[j, 0])
            sent(M1.at[j, :, 0], s_rs.at[j, 1])
            sent(YR.at[j - XFIRST], s_rs.at[j, 2])
            sent(HID.at[c, j, :, h], s_hs.at[j, 0])
            sent(HID.at[c, j, x], s_hs.at[j, 1])
            sent(HID.at[c, j, x, h], s_hs.at[j, 2])

        core_copy(j).wait_send()
        return 0

    lax.fori_loop(0, CHUNKS, drain, 0)


def finish(raw, stats, valid, scores, best):
    shift_e = stats[0:1, :] + jnp.log(stats[1:2, :])
    shift_a = stats[2:3, :] + jnp.log(stats[3:4, :])
    best[...] = jnp.maximum(
        stats[4:5, :] - shift_e + contrast_weight * shift_a, stats[5:6, :] - shift_e
    )
    half_valid = contrast_weight * valid[...].astype(F32)
    for q in range(4):
        rows = slice(q * 128, (q + 1) * 128)
        back = half_valid * to_column(shift_a[:, rows]) - to_column(shift_e[:, rows])
        scores[rows, :] = raw[rows, :] + back


def body(
    exp_hidden, exp_pre_gain, exp_gate, exp_up, exp_down, exp_out_gain, exp_head,
    ama_hidden, ama_out_gain, ama_head, logit_scale, prompt_of, prior_picks, valid_mask,
):
    hbm = pl.BlockSpec(memory_space=pl.ANY)
    vmem = pl.BlockSpec(memory_space=pltpu.VMEM)
    dma = pltpu.SemaphoreType.DMA
    scratch = [
        pltpu.VMEM((8, BLOCK, KDIM), BF16),
        pltpu.VMEM((2, 8, BLOCK, KDIM), BF16),
        pltpu.VMEM((CHUNKS, 2 * KDIM, 2 * CHUNK), BF16),
        pltpu.VMEM((2 * HALF, KDIM), BF16),
        pltpu.VMEM((16, 256, WIDE), BF16),
        pltpu.VMEM((16, 256, WIDE), BF16),
        pltpu.VMEM((DA, WIDE), BF16),
        pltpu.VMEM((CHUNKS, 4, 2, BLOCK, 2 * CHUNK), BF16),
        pltpu.VMEM((CHUNKS, 2, 2, BLOCK, CHUNK), BF16),
        pltpu.VMEM((CHUNKS, 4, 2, BLOCK, CHUNK), BF16),
        pltpu.VMEM((XFIRST, 2, BLOCK, 2 * CHUNK), F32),
        pltpu.VMEM((XFIRST, BLOCK, 2 * CHUNK), BF16),
        pltpu.VMEM((XFIRST, BLOCK, 2 * CHUNK), BF16),
        pltpu.VMEM((YFIRST, 4, BLOCK, 2 * CHUNK), BF16),
        pltpu.VMEM((2, CHUNKS, 4, 2, BLOCK, CHUNK), BF16),
        pltpu.VMEM((ROWS, KDIM), F32),
        pltpu.VMEM((8, BLOCK, KDIM), BF16),
        pltpu.VMEM((7, BLOCK, KDIM), BF16),
        pltpu.VMEM((4, 2, 2, 4, 2, BLOCK, KDIM), BF16),
        pltpu.VMEM((4, 2, 2, 4, 2, BLOCK, KAMA), BF16),
        pltpu.VMEM((BLOCK, KAMA), BF16),
        pltpu.VMEM((ROWS, WIDE), F32),
        pltpu.VMEM((ROWS, WIDE), F32),
        pltpu.VMEM((8, 128), F32),
        pltpu.VMEM((15, 8, 128), F32),
        pltpu.VMEM((8, 128), F32),
        pltpu.VMEM((7, 8, 128), F32),
        pltpu.VMEM((8, 128), F32),
        pltpu.VMEM((15, 8, 128), F32),
        pltpu.VMEM((8, 128), F32),
        pltpu.VMEM((7, 8, 128), F32),
        pltpu.VMEM((2, ROWS, 128), F32),
        pltpu.VMEM((ROWS, WIDE), F32),
        pltpu.VMEM((4, 4, 8, ROWS), F32),
        pltpu.VMEM((1, KDIM), F32),
        pltpu.VMEM((1, KDIM), F32),
        pltpu.VMEM((1, KAMA), F32),
        dma((9,)), dma((CHUNKS, 2)), dma((CHUNKS, 2)), dma((CHUNKS, 2)),
        dma((7,)), dma((7,)), dma((8,)), dma((8,)), dma((15,)), dma((1,)), dma((7,)), dma((1,)),
        dma((CHUNKS, 3)), dma((CHUNKS, 3)), dma((CHUNKS, 3)), dma((CHUNKS, 4)),
        dma((CHUNKS,)), dma((CHUNKS,)), dma((7,)), dma((1,)),
        dma((17, 4)), dma((17, 4)), dma((3, 4)), dma((3, 4)),
        dma((15,)), dma((1,)), dma((7,)), dma((1,)), dma((4, 4)), dma((4, 4)), dma((4,)),
    ]
    raw, stats = pl.pallas_call(
        kernel,
        out_shape=(
            jax.ShapeDtypeStruct((ROWS, WIDE), F32),
            jax.ShapeDtypeStruct((8, ROWS), F32),
        ),
        in_specs=[hbm] * 10 + [vmem] * 4,
        out_specs=(hbm, vmem),
        scratch_shapes=scratch,
        compiler_params=pltpu.CompilerParams(
            collective_id=0, has_side_effects=True, vmem_limit_bytes=63 * 1024 * 1024
        ),
        cost_estimate=pl.CostEstimate(
            flops=12_000_000_000, bytes_accessed=25_000_000, transcendentals=600_000
        ),
    )(
        exp_hidden, exp_pre_gain.reshape(1, KDIM), exp_gate, exp_up, exp_down,
        exp_out_gain.reshape(1, KDIM), exp_head.reshape(16, KDIM, WIDE), ama_hidden, ama_out_gain.reshape(1, KAMA),
        ama_head, logit_scale.reshape(4, 128), prompt_of.reshape(1, ROWS), prior_picks,
        valid_mask.reshape(1, WIDE),
    )
    scores, best = pl.pallas_call(
        finish,
        out_shape=(
            jax.ShapeDtypeStruct((ROWS, WIDE), F32),
            jax.ShapeDtypeStruct((1, ROWS), F32),
        ),
        in_specs=[vmem] * 3,
        out_specs=(vmem, vmem),
    )(raw, stats, valid_mask.reshape(1, WIDE))
    return scores, best.reshape(ROWS)


def solution(mesh):
    torus = Mesh(mesh.devices.reshape(4, 2, 4, 2, 2), AXES)
    in_specs = (
        P(REP, TP), P(TP), P(TP, REP), P(TP, REP), P(REP, TP), P(TP), P(None, ALL),
        P(REP, TP), P(TP), P(None, ALL), P(), P(), P(), P(ALL),
    )
    out_specs = (P(None, ALL), P())
    return jax.shard_map(body, mesh=torus, in_specs=in_specs, out_specs=out_specs, check_vma=False)
```

```python
import functools

import jax
import jax.numpy as jnp
from jax import lax
from jax.experimental import pallas as pl
from jax.experimental.pallas import tpu as pltpu
from jax.sharding import Mesh
from jax.sharding import PartitionSpec as P

DE = 8192
DA = 4096
AXES = ("z", "l", "x", "h", "c")
REP = ("z", "l")
TP = ("x", "h", "c")
ALL = REP + TP

norm_epsilon = 1e-05
contrast_weight = 0.5
hamming_weight = 0.7
LOWEST = -3.0e38

ROWS = 512
BLOCK = 64
KDIM = 512
HALF = 1792
CHUNK = 256
CHUNKS = HALF // CHUNK
XFIRST = 4
YFIRST = CHUNKS - XFIRST
KAMA = 256
WIDE = 512
BF16 = jnp.bfloat16
F32 = jnp.float32

XH = [(d // 2, d % 2) for d in range(1, 8)]
TPO = [(d // 4, (d // 2) % 2, d % 2) for d in range(1, 16)]
ZL = [(d // 2, d % 2) for d in range(1, 8)]


def dot(a, b):
    return jnp.dot(a, b, preferred_element_type=F32)


def eye128():
    return lax.broadcasted_iota(jnp.int32, (128, 128), 0) == lax.broadcasted_iota(
        jnp.int32, (128, 128), 1
    )


def to_row(column):
    return jnp.sum(jnp.where(eye128(), jnp.broadcast_to(column, (128, 128)), 0.0), 0, keepdims=True)


def to_column(row):
    return jnp.sum(jnp.where(eye128(), jnp.broadcast_to(row, (128, 128)), 0.0), 1, keepdims=True)


def aligned(v, m):
    return pl.multiple_of(v, m)


def kernel(
    hid_in, pre_gain, gate, up, down, out_gain, head, ama_in, ama_gain, ahead,
    lscale, prompt, picks, valid,
    raw_out, stats_out,
    XR, XG, W, DOWN, HEADA, HEADB, AHEAD, PB, M1, SR, T, HS, HR, YR, HID, ACC, OB, OR, FE, FA, AIN, LE, LA,
    STS, ST, FS, FR, SFS, SF, SGS, SG, RE, CNT, SBUF, AST, PG, OG, AG,
    s_loc, s_wl, s_ws, s_wr, s_xs, s_xr, s_bs, s_br, s_sts, s_str, s_frs, s_frr,
    s_rs, s_rr, s_hs, s_hr, s_cs, s_cr, s_os, s_or, s_rings, s_ringr, s_fs, s_fr,
    s_sfs, s_sfr, s_sgs, s_sgr, s_qs, s_qr, s_out,
):
    z, l, x, h, c = (lax.axis_index(a) for a in AXES)
    sib = 1 - c
    r = z * 2 + l
    b = x * 2 + h
    t = x * 4 + h * 2 + c
    y = h * 2 + l
    xp, xn, xo = lax.rem(x + 3, 4), lax.rem(x + 1, 4), lax.rem(x + 2, 4)

    def remote(src, dst, ss, rs, **where):
        return pltpu.make_async_remote_copy(
            src_ref=src, dst_ref=dst, send_sem=ss, recv_sem=rs,
            device_id=where, device_id_type=pl.DeviceIdType.MESH,
        )

    sends = []

    def send(src, dst, ss, rs, **where):
        cp = remote(src, dst, ss, rs, **where)
        cp.start()
        sends.append(cp)

    later = []

    def send_set(region, ss, rs, where):
        remote(region(), region(), ss, rs, **where()).start()
        later.append(lambda: remote(region(), region(), ss, rs, **where()).wait_send())

    def go(src, dst, ss, rs, **where):
        remote(src, dst, ss, rs, **where).start()

    def recv(dst, rs):
        remote(dst, dst, rs, rs, c=sib).wait_recv()

    def local(src, dst, sem):
        return pltpu.make_async_copy(src, dst, sem)

    def zl(d, sign):
        dz, dl = ZL[d]
        return lax.rem(z + sign * dz + 4, 4), lax.rem(l + dl, 2)

    def xh(d, sign):
        dx, dh = XH[d]
        return lax.rem(x + sign * dx + 4, 4), lax.rem(h + dh, 2)

    def tp(d, sign):
        dx, dh, dc = TPO[d]
        return lax.rem(x + sign * dx + 4, 4), lax.rem(h + dh, 2), lax.rem(c + dc, 2)

    def wcols(half, j):
        return pl.ds(aligned(half * HALF + j * CHUNK, 128), CHUNK)

    def wpart(j, core, i):
        rows = pl.ds(aligned(core * KDIM, KDIM), KDIM)
        return W.at[j, rows, pl.ds(i * CHUNK, CHUNK)]

    def wlocal(j, i, ref):
        return local(ref.at[:, wcols(c, j)], wpart(j, c, i), s_wl.at[j, i])

    first = [
        local(hid_in, XR.at[r], s_loc.at[0]),
        local(pre_gain, PG, s_loc.at[1]),
        local(ama_in, AIN, s_loc.at[2]),
        local(ama_gain, AG, s_loc.at[3]),
        local(out_gain, OG, s_loc.at[4]),
    ]
    for cp in first:
        cp.start()
    for j in (0, 4, 1, 5, 2, 6, 3):
        wlocal(j, 0, gate).start()
        wlocal(j, 1, up).start()
    late = [
        local(down, DOWN, s_loc.at[5]),
        local(ahead, AHEAD, s_loc.at[6]),
        local(head.at[:, pl.ds(0, 256), :], HEADA, s_loc.at[7]),
        local(head.at[:, pl.ds(256, 256), :], HEADB, s_loc.at[8]),
    ]

    barrier = pltpu.get_barrier_semaphore()

    def greet(**where):
        pl.semaphore_signal(barrier, inc=1, device_id=where, device_id_type=pl.DeviceIdType.MESH)

    for d in range(7):
        pz, q = zl(d, 1)
        greet(z=pz, l=q)
    for d in range(15):
        px, ph, pc = tp(d, 1)
        greet(x=px, h=ph, c=pc)
    greet(h=1 - h, l=1 - l)
    for cp in first:
        cp.wait()
    values_x = XR[r].astype(F32)
    values_a = AIN[...].astype(F32)
    squares = jnp.concatenate(
        [jnp.sum(v * v, axis=1, keepdims=True) for v in (values_x, values_a)], axis=0
    )
    STS[...] = jnp.broadcast_to(to_row(squares), (8, 128))
    pl.semaphore_wait(barrier, 23)
    for d in range(15):
        px, ph, pc = tp(d, 1)
        send(STS, ST.at[d], s_sts.at[d], s_str.at[0], x=px, h=ph, c=pc)

    for d in range(7):
        pz, q = zl(d, 1)
        send(hid_in, XR.at[r], s_xs.at[d], s_xr.at[d], z=pz, l=q)
    for j in (0, 4, 1, 5, 2, 6, 3):
        for i, ref in enumerate((gate, up)):
            send(
                ref.at[:, wcols(sib, j)], wpart(j, c, i),
                s_ws.at[j, i], s_wr.at[j, i], c=sib,
            )

    def ring(index, sets, places, me):
        prv, nxt = lax.rem(me + 3, 4), lax.rem(me + 1, 4)
        opp = lax.rem(me + 2, 4)
        lo, hi = pl.ds(0, 32), pl.ds(32, 32)
        full = pl.ds(0, 64)

        def pass_on(p, rows, q, n):
            send_set(
                lambda: sets(p, rows), s_rings.at[index, n], s_ringr.at[index, n], lambda: places(q)
            )

        def start():
            pass_on(me, full, nxt, 0)
            pass_on(me, full, prv, 1)

        def pass_next():
            recv(sets(prv, full), s_ringr.at[index, 0])
            pass_on(prv, lo, nxt, 2)

        def pass_prev():
            recv(sets(nxt, full), s_ringr.at[index, 1])
            pass_on(nxt, hi, prv, 3)

        def finish():
            recv(sets(opp, lo), s_ringr.at[index, 2])
            recv(sets(opp, hi), s_ringr.at[index, 3])

        return start, pass_next, pass_prev, finish, (me, prv, nxt, opp)

    def spread(index, sets, places, me):
        full = pl.ds(0, 64)

        def to(d):
            send_set(
                lambda: sets(me, full), s_rings.at[index, d], s_ringr.at[index, d],
                lambda: places(lax.rem(me + d, 4)),
            )

        def start():
            for d in (1, 3, 2):
                to(d)

        def finish():
            for d in (1, 3, 2):
                recv(sets(lax.rem(me + 4 - d, 4), full), s_ringr.at[index, d])

        return start, finish

    def y_place(p):
        return dict(h=lax.div(p, 2), l=lax.rem(p, 2))

    every4, every2 = pl.ds(0, 4), pl.ds(0, 2)

    def rings_x_y_z(ref, cols, first_index, split=False):
        a = ring(first_index, lambda p, k: ref.at[p, h, c, z, l, k, cols], lambda p: dict(x=p), x)
        bb = ring(
            first_index + 1,
            lambda p, k: ref.at[every4, lax.div(p, 2), c, z, lax.rem(p, 2), k, cols], y_place, y,
        )
        if split:
            def d(yy, n):
                return ring(
                    first_index + 6 + n,
                    lambda p, k: ref.at[every4, lax.div(yy, 2), c, p, lax.rem(yy, 2), k, cols],
                    lambda p: dict(z=p), z,
                )
        else:
            d = ring(
                first_index + 2,
                lambda p, k: ref.at[every4, every2, c, p, every2, k, cols], lambda p: dict(z=p), z,
            )
        return a, bb, d

    def rings_z_y_x(ref, cols, first_index):
        a = ring(first_index, lambda p, k: ref.at[x, h, c, p, l, k, cols], lambda p: dict(z=p), z)
        bb = ring(
            first_index + 1,
            lambda p, k: ref.at[x, lax.div(p, 2), c, every4, lax.rem(p, 2), k, cols], y_place, y,
        )

        def d(yy, n):
            return ring(
                first_index + 6 + n,
                lambda p, k: ref.at[p, lax.div(yy, 2), c, every4, lax.rem(yy, 2), k, cols],
                lambda p: dict(x=p), x,
            )

        return a, bb, d

    def a_set(ref, cc, p, cols):
        return ref.at[every4, every2, cc, p, every2, pl.ds(0, 64), cols]

    def b_set(ref, cc, p, cols):
        return ref.at[p, every2, cc, every4, every2, pl.ds(0, 64), cols]

    def to_core(ref, maker, p, cols, index, n):
        send_set(
            lambda: maker(ref, c, p, cols), s_fs.at[index, n], s_fr.at[index, n], lambda: dict(c=sib)
        )

    def from_other(ref, maker, p, cols, index, n):
        recv(maker(ref, sib, p, cols), s_fr.at[index, n])

    recv(ST, s_str.at[0])
    total = STS[...]
    for d in range(15):
        total += ST[d]
    lane = lax.broadcasted_iota(jnp.int32, (8, 128), 1)
    means = jnp.where(lane < BLOCK, total / DE, total / DA)
    FS[...] = lax.rsqrt(means + norm_epsilon)
    for d in range(7):
        pz, q = zl(d, 1)
        send(FS, FR.at[d], s_frs.at[d], s_frr.at[0], z=pz, l=q)
    own_factors = to_column(FS[0:1, :])

    FA[x, h, c, z, l] = (values_a * own_factors[BLOCK:] * AG[...]).astype(BF16)
    ama_cols = pl.ds(0, KAMA)
    ama = rings_x_y_z(FA, ama_cols, 0)
    ama_x = spread(
        0, lambda p, k: FA.at[p, h, c, z, l, k, ama_cols], lambda p: dict(x=p), x
    )
    ama_y = spread(
        1, lambda p, k: FA.at[every4, lax.div(p, 2), c, z, lax.rem(p, 2), k, ama_cols], y_place, y
    )
    ama_x[0]()

    def take_rows(rr, d, factors):
        XG[c, rr] = (XR[rr].astype(F32) * factors[:BLOCK] * PG[...]).astype(BF16)
        send(XG.at[c, rr], XG.at[c, rr], s_bs.at[d], s_br.at[d], c=sib)

    take_rows(r, 7, own_factors)
    for cp in late:
        cp.start()
    recv(FR, s_frr.at[0])
    for d in range(7):
        pz, q = zl(d, -1)
        rr = pz * 2 + q
        recv(XR.at[rr], s_xr.at[d])
        take_rows(rr, d, to_column(FR[d, 0:1, :]))

    ama_x[1]()
    ama_y[0]()

    for d in range(7):
        pz, q = zl(d, -1)
        recv(XG.at[sib, pz * 2 + q], s_br.at[d])
    recv(XG.at[sib, r], s_br.at[7])

    gates, ups = pl.ds(0, CHUNK), pl.ds(CHUNK, CHUNK)

    def piece(j, p, cols, xfirst):
        return PB.at[j, p, :, :, cols] if xfirst else YR.at[j - XFIRST, p, :, cols]

    def slot(ref, j, n, xfirst):
        return ref.at[j, n] if xfirst else ref.at[j, n, 0]

    def slots(ref, j, xfirst):
        return ref.at[j] if xfirst else ref.at[j, :, 0]

    def first_sends(j, xfirst):
        for p, cols, ref, n, k, to in (
            (xo, gates, M1, 0, 0, xn), (xo, ups, M1, 1, 0, xp),
            (xn, ups, SR, 0, 1, xn), (xp, gates, SR, 1, 1, xp),
        ):
            go(piece(j, p, cols, xfirst), slot(ref, j, n, xfirst), s_rs.at[j, 0], s_rr.at[j, k], x=to)

    def product(j):
        for i, ref in enumerate((gate, up)):
            wlocal(j, i, ref).wait()
            recv(wpart(j, sib, i), s_wr.at[j, i])

        def block(q, _):
            quad = pl.ds(q * 4, 4)
            lhs = jnp.concatenate([XG[k, quad].reshape(256, KDIM) for k in range(2)], axis=1)
            PB[j, pl.ds(q * 2, 2)] = dot(lhs, W[j]).astype(BF16).reshape(2, 2, BLOCK, 2 * CHUNK)
            return 0

        lax.fori_loop(0, 2, block, 0)

    def products(i, _):
        product(i)
        first_sends(i, True)

        @pl.when(i < YFIRST)
        def _():
            j = i + XFIRST
            product(j)
            go(PB.at[j, :, 1 - h], YR.at[i], s_rs.at[j, 2], s_rr.at[j, 2], h=1 - h)

        return 0

    lax.fori_loop(0, XFIRST, products, 0)


    ids = t * WIDE + r * (16 * WIDE) + lax.broadcasted_iota(jnp.int32, (16, WIDE), 1)
    per_prompt = jnp.zeros((16, WIDE), F32)
    for k in range(24):
        per_prompt += (picks[:, k : k + 1] == ids).astype(F32)
    chosen = (lax.broadcasted_iota(jnp.int32, (16, ROWS), 0) == prompt[...]).astype(F32)
    CNT[...] = lax.dot_general(
        chosen.astype(BF16), per_prompt.astype(BF16), (((0,), (0,)), ((), ())),
        preferred_element_type=F32,
    )

    ama_y[1]()
    ama[2][0]()

    def add_and_pass(j, xfirst):
        recv(slots(M1, j, xfirst), s_rr.at[j, 0])
        for n, p, cols in ((0, xn, gates), (1, xp, ups)):
            ref = slot(M1, j, n, xfirst)
            ref[...] = (ref[...].astype(F32) + piece(j, p, cols, xfirst)[...].astype(F32)).astype(BF16)
            go(ref, slot(SR, j, n + 2, xfirst), s_rs.at[j, 1], s_rr.at[j, 1], x=p)

    def ring_sums(j, xfirst):
        recv(slots(SR, j, xfirst), s_rr.at[j, 1])
        terms = [slot(SR, j, n, xfirst)[...].astype(F32) for n in range(4)]
        g = piece(j, x, gates, xfirst)[...].astype(F32) + terms[1] + terms[2]
        u = piece(j, x, ups, xfirst)[...].astype(F32) + terms[0] + terms[3]
        return g, u

    def put_hidden(j, g, u):
        HID[c, j, x, h] = (g / (1.0 + jnp.exp(-g)) * u).astype(BF16)

    def around(j, own):
        go(own, own, s_hs.at[j, 1], s_hr.at[j, 1], x=xn)
        go(own, own, s_hs.at[j, 1], s_hr.at[j, 2], x=xp)

    def halves_on(j, blocks):
        for p, q, n, first_row in ((xp, xn, 1, 0), (xn, xp, 2, 32)):
            recv(blocks(p, pl.ds(0, BLOCK)), s_hr.at[j, n])
            part = blocks(p, pl.ds(first_row, 32))
            go(part, part, s_hs.at[j, 2], s_hr.at[j, 3], x=q)

    def core_copy(j):
        return remote(HID.at[c, j], HID.at[c, j], s_cs.at[j], s_cr.at[j], c=sib)

    def use_chunk(j):
        recv(HID.at[sib, j], s_cr.at[j])

        def block(q, _):
            rows = pl.ds(aligned(q * 256, 256), 256)
            pair = pl.ds(q * 2, 2)
            lhs = jnp.concatenate([HID[k, j, pair].reshape(256, CHUNK) for k in range(2)], axis=1)
            rhs = jnp.concatenate(
                [DOWN[pl.ds(aligned(k * HALF + j * CHUNK, CHUNK), CHUNK), :] for k in range(2)], axis=0
            )
            ACC[rows, :] += dot(lhs, rhs)
            return 0

        lax.fori_loop(0, 2, block, 0)

    def x0(j):
        add_and_pass(j, True)

    def x1(j):
        g, u = ring_sums(j, True)
        T[j, :, :, gates] = g
        T[j, :, :, ups] = u
        HS[j] = T[j, 1 - h].astype(BF16)
        go(HS.at[j], HR.at[j], s_rs.at[j, 2], s_rr.at[j, 2], h=1 - h)

    def x2(j):
        recv(HR.at[j], s_rr.at[j, 2])
        both = T[j, h] + HR[j].astype(F32)
        put_hidden(j, both[:, :CHUNK], both[:, CHUNK:])
        own = HID.at[c, j, x, h]
        go(own, own, s_hs.at[j, 0], s_hr.at[j, 0], h=1 - h)

    def x3(j):
        recv(HID.at[c, j, x, 1 - h], s_hr.at[j, 0])
        around(j, HID.at[c, j, x])

    def x4(j):
        halves_on(j, lambda p, rows: HID.at[c, j, p, :, rows])

    def x5(j):
        recv(HID.at[c, j, xo], s_hr.at[j, 3])
        core_copy(j).start()

    def y0(i):
        j = i + XFIRST
        recv(YR.at[i], s_rr.at[j, 2])
        YR[i] = (YR[i].astype(F32) + PB[j, :, h].astype(F32)).astype(BF16)
        first_sends(j, False)

    def y1(i):
        add_and_pass(i + XFIRST, False)

    def y2(i):
        j = i + XFIRST
        g, u = ring_sums(j, False)
        put_hidden(j, g, u)
        around(j, HID.at[c, j, x, h])

    def y3(i):
        j = i + XFIRST
        halves_on(j, lambda p, rows: HID.at[c, j, p, h, rows])

    def y4(i):
        j = i + XFIRST
        recv(HID.at[c, j, xo, h], s_hr.at[j, 3])
        got = HID.at[c, j, :, h]
        go(got, got, s_hs.at[j, 0], s_hr.at[j, 0], h=1 - h)

    def y5(i):
        j = i + XFIRST
        recv(HID.at[c, j, :, 1 - h], s_hr.at[j, 0])
        core_copy(j).start()

    def y6(i):
        use_chunk(i + XFIRST)

    xstages = (x0, x1, x2, x3, x4, x5, use_chunk)
    ystages = (y0, y1, y2, y3, y4, y5, y6)
    ACC[...] = jnp.zeros_like(ACC)
    late[0].wait()
    a_places = ama[2][4]

    def stages(n, _):
        for k in reversed(range(7)):
            for many, steps in ((YFIRST, ystages), (XFIRST, xstages)):
                pl.when((n - k >= 0) & (n - k < many))(functools.partial(steps[k], n - k))

        return 0

    lax.fori_loop(0, 5, stages, 0)
    ama[2][1]()
    ama[2][2]()
    lax.fori_loop(5, 8, stages, 0)
    ama[2][3]()
    for k in range(4):
        to_core(FA, a_set, a_places[k], ama_cols, 0, k)
    lax.fori_loop(8, XFIRST + 6, stages, 0)

    for q in range(8):
        OB[q] = ACC[q * BLOCK : (q + 1) * BLOCK, :].astype(BF16)
    for d in range(7):
        pz, q = zl(d, 1)
        send(OB.at[pz * 2 + q], OR.at[d], s_os.at[d], s_or.at[0], z=pz, l=q)

    late[1].wait()
    for n in range(4):
        from_other(FA, a_set, a_places[n], ama_cols, 0, n)

    def ama_block(q, _):
        rows = pl.ds(aligned(q * 256, 256), 256)
        LA[rows, :] = jnp.zeros((256, WIDE), F32)

        def part(k, _):
            lhs = jnp.concatenate(
                [FA[k, n // 2, n % 2, pl.ds(q * 2, 2)].reshape(256, KAMA) for n in range(4)], axis=1
            )
            LA[rows, :] += dot(lhs, AHEAD[pl.ds(aligned(k * 4 * KAMA, 4 * KAMA), 4 * KAMA), :])
            return 0

        lax.fori_loop(0, 4, part, 0)
        return 0

    lax.fori_loop(0, 2, ama_block, 0)

    vmask = valid[...].astype(F32)
    half_valid = contrast_weight * vmask
    for q in range(4):
        rows = pl.ds(q * 128, 128)
        ls = to_column(lscale[q : q + 1, :])
        RE[1, rows, :] = jnp.broadcast_to(ls, (128, 128))
        la = LA[rows, :] * ls
        ma = jnp.max(la, axis=1, keepdims=True)
        sa = jnp.sum(jnp.exp(la - ma), axis=1, keepdims=True)
        AST[0:1, rows] = to_row(ma)
        AST[1:2, rows] = to_row(sa)
        LA[rows, :] = half_valid * la + hamming_weight * CNT[rows, :]


    layer = values_x + ACC[pl.ds(aligned(r * BLOCK, BLOCK), BLOCK), :]
    recv(OR, s_or.at[0])
    for d in range(7):
        layer += OR[d].astype(F32)
    FE[x, h, c, z, l] = (layer * OG[...]).astype(BF16)

    low, high = pl.ds(0, 256), pl.ds(256, 256)
    one = rings_x_y_z(FE, low, 3, split=True)
    two = rings_z_y_x(FE, high, 7)
    one_first = spread(3, lambda p, k: FE.at[p, h, c, z, l, k, low], lambda p: dict(x=p), x)
    two_first = spread(7, lambda p, k: FE.at[x, h, c, p, l, k, high], lambda p: dict(z=p), z)
    one_first[0]()
    two_first[0]()

    squares = jnp.sum(layer * layer, axis=1, keepdims=True)
    squares = jnp.concatenate([squares, squares], axis=0)
    SFS[...] = jnp.broadcast_to(to_row(squares), (8, 128))
    for d in range(15):
        px, ph, pc = tp(d, 1)
        send(SFS, SF.at[d], s_sfs.at[d], s_sfr.at[0], x=px, h=ph, c=pc)

    y_order = one[1][4]
    last_one = [one[2](p, n) for n, p in enumerate(y_order)]
    last_two = [two[2](p, n) for n, p in enumerate(y_order)]
    for g, n, e in ((one_first, one[1], last_one), (two_first, two[1], last_two)):
        g[1]()
        n[0]()
        e[0][0]()
    for k in (1, 2):
        for n, e in ((one[1], last_one), (two[1], last_two)):
            n[k]()
            e[k][0]()

    recv(SF, s_sfr.at[0])
    total = SFS[...]
    for d in range(15):
        total += SF[d]
    SGS[...] = total
    for d in range(7):
        pz, q = zl(d, 1)
        send(SGS, SG.at[d], s_sgs.at[d], s_sgr.at[0], z=pz, l=q)

    for n, e in ((one[1], last_one), (two[1], last_two)):
        n[3]()
        e[3][0]()
    to_core(FE, a_set, z, low, 1, 0)
    to_core(FE, b_set, x, high, 2, 0)
    late[2].wait()
    late[3].wait()
    LE[...] = jnp.zeros_like(LE)

    def use_a(p):
        def part(k, _):
            lhs = jnp.concatenate(
                [FE[k, n // 2, n % 2, p, :, :, 0:256].reshape(128, 256) for n in range(4)], axis=1
            )
            rows = pl.ds(aligned(p * 128, 128), 128)
            LE[rows, :] += dot(lhs, HEADA[pl.ds(k * 4, 4)].reshape(1024, WIDE))
            return 0

        lax.fori_loop(0, 4, part, 0)

    def use_b(p):
        def part(q, _):
            pair = pl.ds(q * 2, 2)
            lhs = jnp.concatenate(
                [FE[p, n // 2, n % 2, pair, :, :, 256:512].reshape(256, 256) for n in range(4)], axis=1
            )
            rows = pl.ds(aligned(q * 256, 256), 256)
            LE[rows, :] += dot(lhs, HEADB[pl.ds(p * 4, 4)].reshape(1024, WIDE))
            return 0

        lax.fori_loop(0, 2, part, 0)

    za, xb = last_one[0][4], last_two[0][4]
    for n in range(4):
        for e in (last_one, last_two):
            e[n][1]()
            e[n][2]()
        if n == 1:
            from_other(FE, a_set, z, low, 1, 0)
            use_a(z)
            from_other(FE, b_set, x, high, 2, 0)
            use_b(x)
    for n in (1, 2):
        to_core(FE, a_set, za[n], low, 1, n)
        to_core(FE, b_set, xb[n], high, 2, n)
    for n in (1, 2):
        from_other(FE, a_set, za[n], low, 1, n)
        use_a(za[n])
        from_other(FE, b_set, xb[n], high, 2, n)
        use_b(xb[n])

    recv(SG, s_sgr.at[0])

    def row_factors(rr, line):
        rows = pl.ds(aligned(rr * BLOCK, BLOCK), BLOCK)
        col = lax.rsqrt(to_column(line)[:BLOCK] / DE + norm_epsilon)
        RE[0, rows, :] = col * RE[1, rows, :]

    row_factors(r, SGS[0:1, :])
    for d in range(7):
        pz, q = zl(d, -1)
        row_factors(pz * 2 + q, SG[d, 0:1, :])

    def a_group(n):
        return lambda ref, cc, p, cols: ref.at[
            every4, lax.div(y_order[n], 2), cc, p, lax.rem(y_order[n], 2), pl.ds(0, 64), cols
        ]

    def b_group(n):
        return lambda ref, cc, p, cols: ref.at[
            p, lax.div(y_order[n], 2), cc, every4, lax.rem(y_order[n], 2), pl.ds(0, 64), cols
        ]

    for n in range(4):
        last_one[n][3]()
        to_core(FE, a_group(n), za[3], low, 3, n)
        last_two[n][3]()
        to_core(FE, b_group(n), xb[3], high, 4, n)
    for n in range(4):
        from_other(FE, a_group(n), za[3], low, 3, n)
        from_other(FE, b_group(n), xb[3], high, 4, n)
    use_a(za[3])
    use_b(xb[3])

    for q in range(4):
        rows = pl.ds(q * 128, 128)
        le = LE[rows, :] * RE[0, rows, 0:1]
        me = jnp.max(le, axis=1, keepdims=True)
        se = jnp.sum(jnp.exp(le - me), axis=1, keepdims=True)
        raw = le - LA[rows, :]
        LE[rows, :] = raw
        local(LE.at[rows], raw_out.at[rows], s_out.at[q]).start()
        used = jnp.broadcast_to(vmask, raw.shape) > 0.5
        m1 = jnp.max(jnp.where(used, raw, LOWEST), axis=1, keepdims=True)
        m0 = jnp.max(jnp.where(used, LOWEST, raw), axis=1, keepdims=True)
        line_e, line_s, line_1, line_0 = (to_row(v) for v in (me, se, m1, m0))
        lines = [line_e, line_s, AST[0:1, rows], AST[1:2, rows], line_1, line_0, line_e, line_e]
        SBUF[0, x * 2 + c, :, rows] = jnp.concatenate(lines, axis=0)

    def merge(parts):
        me = functools.reduce(jnp.maximum, [p[0:1] for p in parts])
        ma = functools.reduce(jnp.maximum, [p[2:3] for p in parts])
        se = sum(p[1:2] * jnp.exp(p[0:1] - me) for p in parts)
        sa = sum(p[3:4] * jnp.exp(p[2:3] - ma) for p in parts)
        m1 = functools.reduce(jnp.maximum, [p[4:5] for p in parts])
        m0 = functools.reduce(jnp.maximum, [p[5:6] for p in parts])
        return jnp.concatenate([me, se, ma, sa, m1, m0, me, me], axis=0)

    mine = SBUF.at[0, x * 2 + c]
    for d in range(1, 8):
        send(
            mine, mine, s_qs.at[0, d], s_qr.at[0, d],
            x=lax.rem(x + d // 2, 4), c=lax.rem(c + d % 2, 2),
        )
    for d in range(1, 8):
        px, pc = lax.rem(x + 4 - d // 2, 4), lax.rem(c + d % 2, 2)
        recv(SBUF.at[0, px * 2 + pc], s_qr.at[0, d])
    merged = merge([SBUF[0, k] for k in range(8)])
    for phase, (me, place) in enumerate(
        ((y, y_place), (z, lambda p: dict(z=p))), start=1
    ):
        SBUF[phase, me] = merged
        mine = SBUF.at[phase, me]
        for d in range(1, 4):
            send(mine, mine, s_qs.at[phase, d], s_qr.at[phase, d], **place(lax.rem(me + d, 4)))
        for d in range(1, 4):
            recv(SBUF.at[phase, lax.rem(me + 4 - d, 4)], s_qr.at[phase, d])
        merged = merge([SBUF[phase, k] for k in range(4)])

    stats_out[...] = merged
    for q in range(4):
        rows = pl.ds(q * 128, 128)
        local(LE.at[rows], raw_out.at[rows], s_out.at[q]).wait()

    for cp in sends:
        cp.wait_send()
    for wait in later:
        wait()

    def drain(j, _):
        def sent(region, sem):
            remote(region, region, sem, sem, c=sib).wait_send()

        @pl.when(j < XFIRST)
        def _():
            sent(SR.at[j], s_rs.at[j, 0])
            sent(M1.at[j], s_rs.at[j, 1])
            sent(HR.at[j], s_rs.at[j, 2])
            sent(HID.at[c, j, x, h], s_hs.at[j, 0])
            sent(HID.at[c, j, pl.ds(0, 2)], s_hs.at[j, 1])
            sent(HID.at[c, j, x], s_hs.at[j, 2])

        @pl.when(j >= XFIRST)
        def _():
            sent(SR.at[j, :, 0], s_rs.at[j, 0])
            sent(M1.at[j, :, 0], s_rs.at[j, 1])
            sent(YR.at[j - XFIRST], s_rs.at[j, 2])
            sent(HID.at[c, j, :, h], s_hs.at[j, 0])
            sent(HID.at[c, j, x], s_hs.at[j, 1])
            sent(HID.at[c, j, x, h], s_hs.at[j, 2])

        core_copy(j).wait_send()
        return 0

    lax.fori_loop(0, CHUNKS, drain, 0)


def finish(raw, stats, valid, scores, best):
    shift_e = stats[0:1, :] + jnp.log(stats[1:2, :])
    shift_a = stats[2:3, :] + jnp.log(stats[3:4, :])
    best[...] = jnp.maximum(
        stats[4:5, :] - shift_e + contrast_weight * shift_a, stats[5:6, :] - shift_e
    )
    half_valid = contrast_weight * valid[...].astype(F32)
    for q in range(4):
        rows = slice(q * 128, (q + 1) * 128)
        back = half_valid * to_column(shift_a[:, rows]) - to_column(shift_e[:, rows])
        scores[rows, :] = raw[rows, :] + back


def body(
    exp_hidden, exp_pre_gain, exp_gate, exp_up, exp_down, exp_out_gain, exp_head,
    ama_hidden, ama_out_gain, ama_head, logit_scale, prompt_of, prior_picks, valid_mask,
):
    hbm = pl.BlockSpec(memory_space=pl.ANY)
    vmem = pl.BlockSpec(memory_space=pltpu.VMEM)
    dma = pltpu.SemaphoreType.DMA
    scratch = [
        pltpu.VMEM((8, BLOCK, KDIM), BF16),
        pltpu.VMEM((2, 8, BLOCK, KDIM), BF16),
        pltpu.VMEM((CHUNKS, 2 * KDIM, 2 * CHUNK), BF16),
        pltpu.VMEM((2 * HALF, KDIM), BF16),
        pltpu.VMEM((16, 256, WIDE), BF16),
        pltpu.VMEM((16, 256, WIDE), BF16),
        pltpu.VMEM((DA, WIDE), BF16),
        pltpu.VMEM((CHUNKS, 4, 2, BLOCK, 2 * CHUNK), BF16),
        pltpu.VMEM((CHUNKS, 2, 2, BLOCK, CHUNK), BF16),
        pltpu.VMEM((CHUNKS, 4, 2, BLOCK, CHUNK), BF16),
        pltpu.VMEM((XFIRST, 2, BLOCK, 2 * CHUNK), F32),
        pltpu.VMEM((XFIRST, BLOCK, 2 * CHUNK), BF16),
        pltpu.VMEM((XFIRST, BLOCK, 2 * CHUNK), BF16),
        pltpu.VMEM((YFIRST, 4, BLOCK, 2 * CHUNK), BF16),
        pltpu.VMEM((2, CHUNKS, 4, 2, BLOCK, CHUNK), BF16),
        pltpu.VMEM((ROWS, KDIM), F32),
        pltpu.VMEM((8, BLOCK, KDIM), BF16),
        pltpu.VMEM((7, BLOCK, KDIM), BF16),
        pltpu.VMEM((4, 2, 2, 4, 2, BLOCK, KDIM), BF16),
        pltpu.VMEM((4, 2, 2, 4, 2, BLOCK, KAMA), BF16),
        pltpu.VMEM((BLOCK, KAMA), BF16),
        pltpu.VMEM((ROWS, WIDE), F32),
        pltpu.VMEM((ROWS, WIDE), F32),
        pltpu.VMEM((8, 128), F32),
        pltpu.VMEM((15, 8, 128), F32),
        pltpu.VMEM((8, 128), F32),
        pltpu.VMEM((7, 8, 128), F32),
        pltpu.VMEM((8, 128), F32),
        pltpu.VMEM((15, 8, 128), F32),
        pltpu.VMEM((8, 128), F32),
        pltpu.VMEM((7, 8, 128), F32),
        pltpu.VMEM((2, ROWS, 128), F32),
        pltpu.VMEM((ROWS, WIDE), F32),
        pltpu.VMEM((3, 8, 8, ROWS), F32),
        pltpu.VMEM((8, ROWS), F32),
        pltpu.VMEM((1, KDIM), F32),
        pltpu.VMEM((1, KDIM), F32),
        pltpu.VMEM((1, KAMA), F32),
        dma((9,)), dma((CHUNKS, 2)), dma((CHUNKS, 2)), dma((CHUNKS, 2)),
        dma((7,)), dma((7,)), dma((8,)), dma((8,)), dma((15,)), dma((1,)), dma((7,)), dma((1,)),
        dma((CHUNKS, 3)), dma((CHUNKS, 3)), dma((CHUNKS, 3)), dma((CHUNKS, 4)),
        dma((CHUNKS,)), dma((CHUNKS,)), dma((7,)), dma((1,)),
        dma((17, 4)), dma((17, 4)), dma((5, 4)), dma((5, 4)),
        dma((15,)), dma((1,)), dma((7,)), dma((1,)), dma((3, 8)), dma((3, 8)), dma((4,)),
    ]
    raw, stats = pl.pallas_call(
        kernel,
        out_shape=(
            jax.ShapeDtypeStruct((ROWS, WIDE), F32),
            jax.ShapeDtypeStruct((8, ROWS), F32),
        ),
        in_specs=[hbm] * 10 + [vmem] * 4,
        out_specs=(hbm, vmem),
        scratch_shapes=scratch,
        compiler_params=pltpu.CompilerParams(
            collective_id=0, has_side_effects=True, vmem_limit_bytes=63 * 1024 * 1024
        ),
        cost_estimate=pl.CostEstimate(
            flops=12_000_000_000, bytes_accessed=25_000_000, transcendentals=600_000
        ),
    )(
        exp_hidden, exp_pre_gain.reshape(1, KDIM), exp_gate, exp_up, exp_down,
        exp_out_gain.reshape(1, KDIM), exp_head.reshape(16, KDIM, WIDE), ama_hidden, ama_out_gain.reshape(1, KAMA),
        ama_head, logit_scale.reshape(4, 128), prompt_of.reshape(1, ROWS), prior_picks,
        valid_mask.reshape(1, WIDE),
    )
    scores, best = pl.pallas_call(
        finish,
        out_shape=(
            jax.ShapeDtypeStruct((ROWS, WIDE), F32),
            jax.ShapeDtypeStruct((1, ROWS), F32),
        ),
        in_specs=[vmem] * 3,
        out_specs=(vmem, vmem),
    )(raw, stats, valid_mask.reshape(1, WIDE))
    return scores, best.reshape(ROWS)


def solution(mesh):
    torus = Mesh(mesh.devices.reshape(4, 2, 4, 2, 2), AXES)
    in_specs = (
        P(REP, TP), P(TP), P(TP, REP), P(TP, REP), P(REP, TP), P(TP), P(None, ALL),
        P(REP, TP), P(TP), P(None, ALL), P(), P(), P(), P(ALL),
    )
    out_specs = (P(None, ALL), P())
    return jax.shard_map(body, mesh=torus, in_specs=in_specs, out_specs=out_specs, check_vma=False)
```

```python
import functools

import jax
import jax.numpy as jnp
from jax import lax
from jax.experimental import pallas as pl
from jax.experimental.pallas import tpu as pltpu
from jax.sharding import Mesh
from jax.sharding import PartitionSpec as P

DE = 8192
DA = 4096
AXES = ("z", "l", "x", "h", "c")
REP = ("z", "l")
TP = ("x", "h", "c")
ALL = REP + TP

norm_epsilon = 1e-05
contrast_weight = 0.5
hamming_weight = 0.7
LOWEST = -3.0e38

ROWS = 512
BLOCK = 64
KDIM = 512
HALF = 1792
CHUNK = 256
CHUNKS = HALF // CHUNK
XFIRST = 4
YFIRST = CHUNKS - XFIRST
KAMA = 256
WIDE = 512
BF16 = jnp.bfloat16
F32 = jnp.float32

XH = [(d // 2, d % 2) for d in range(1, 8)]
TPO = [(d // 4, (d // 2) % 2, d % 2) for d in range(1, 16)]
ZL = [(d // 2, d % 2) for d in range(1, 8)]


def dot(a, b):
    return jnp.dot(a, b, preferred_element_type=F32)


def eye128():
    return lax.broadcasted_iota(jnp.int32, (128, 128), 0) == lax.broadcasted_iota(
        jnp.int32, (128, 128), 1
    )


def to_row(column):
    return jnp.sum(jnp.where(eye128(), jnp.broadcast_to(column, (128, 128)), 0.0), 0, keepdims=True)


def to_column(row):
    return jnp.sum(jnp.where(eye128(), jnp.broadcast_to(row, (128, 128)), 0.0), 1, keepdims=True)


def aligned(v, m):
    return pl.multiple_of(v, m)


def kernel(
    hid_in, pre_gain, gate, up, down, out_gain, head, ama_in, ama_gain, ahead,
    lscale, prompt, picks, valid,
    raw_out, stats_out,
    XR, XG, W, DOWN, HEADA, HEADB, AHEAD, PB, M1, SR, T, HS, HR, YR, HID, ACC, OB, OR, FE, FA, AIN, LE, LA,
    STS, ST, FS, FR, SFS, SF, SGS, SG, RE, CNT, SBUF, AST, PG, OG, AG,
    s_loc, s_wl, s_ws, s_wr, s_xs, s_xr, s_bs, s_br, s_sts, s_str, s_frs, s_frr,
    s_rs, s_rr, s_hs, s_hr, s_cs, s_cr, s_os, s_or, s_rings, s_ringr, s_fs, s_fr,
    s_sfs, s_sfr, s_sgs, s_sgr, s_qs, s_qr, s_out,
):
    z, l, x, h, c = (lax.axis_index(a) for a in AXES)
    sib = 1 - c
    r = z * 2 + l
    b = x * 2 + h
    t = x * 4 + h * 2 + c
    y = h * 2 + l
    xp, xn, xo = lax.rem(x + 3, 4), lax.rem(x + 1, 4), lax.rem(x + 2, 4)

    def remote(src, dst, ss, rs, **where):
        return pltpu.make_async_remote_copy(
            src_ref=src, dst_ref=dst, send_sem=ss, recv_sem=rs,
            device_id=where, device_id_type=pl.DeviceIdType.MESH,
        )

    sends = []

    def send(src, dst, ss, rs, **where):
        cp = remote(src, dst, ss, rs, **where)
        cp.start()
        sends.append(cp.wait_send)

    later = []

    def send_set(region, ss, rs, where):
        remote(region(), region(), ss, rs, **where()).start()
        later.append(lambda: remote(region(), region(), ss, rs, **where()).wait_send())

    def settle(*lists):
        for waits in lists:
            for wait in waits:
                wait()
            waits.clear()

    def go(src, dst, ss, rs, **where):
        remote(src, dst, ss, rs, **where).start()

    def recv(dst, rs):
        remote(dst, dst, rs, rs, c=sib).wait_recv()

    def local(src, dst, sem):
        return pltpu.make_async_copy(src, dst, sem)

    def zl(d, sign):
        dz, dl = ZL[d]
        return lax.rem(z + sign * dz + 4, 4), lax.rem(l + dl, 2)

    def xh(d, sign):
        dx, dh = XH[d]
        return lax.rem(x + sign * dx + 4, 4), lax.rem(h + dh, 2)

    def tp(d, sign):
        dx, dh, dc = TPO[d]
        return lax.rem(x + sign * dx + 4, 4), lax.rem(h + dh, 2), lax.rem(c + dc, 2)

    def wcols(half, j):
        return pl.ds(aligned(half * HALF + j * CHUNK, 128), CHUNK)

    def wpart(j, core, i):
        rows = pl.ds(aligned(core * KDIM, KDIM), KDIM)
        return W.at[j, rows, pl.ds(i * CHUNK, CHUNK)]

    def wlocal(j, i, ref):
        return local(ref.at[:, wcols(c, j)], wpart(j, c, i), s_wl.at[j, i])

    first = [
        local(hid_in, XR.at[r], s_loc.at[0]),
        local(pre_gain, PG, s_loc.at[1]),
        local(ama_in, AIN, s_loc.at[2]),
        local(ama_gain, AG, s_loc.at[3]),
        local(out_gain, OG, s_loc.at[4]),
    ]
    for cp in first:
        cp.start()
    for j in (0, 4, 1, 5, 2, 6, 3):
        wlocal(j, 0, gate).start()
        wlocal(j, 1, up).start()
    late = [
        local(down, DOWN, s_loc.at[5]),
        local(ahead, AHEAD, s_loc.at[6]),
        local(head.at[:, pl.ds(0, 256), :], HEADA, s_loc.at[7]),
        local(head.at[:, pl.ds(256, 256), :], HEADB, s_loc.at[8]),
    ]

    barrier = pltpu.get_barrier_semaphore()

    def greet(**where):
        pl.semaphore_signal(barrier, inc=1, device_id=where, device_id_type=pl.DeviceIdType.MESH)

    for d in range(7):
        pz, q = zl(d, 1)
        greet(z=pz, l=q)
    for d in range(15):
        px, ph, pc = tp(d, 1)
        greet(x=px, h=ph, c=pc)
    greet(h=1 - h, l=1 - l)
    for cp in first:
        cp.wait()
    values_x = XR[r].astype(F32)
    values_a = AIN[...].astype(F32)
    squares = jnp.concatenate(
        [jnp.sum(v * v, axis=1, keepdims=True) for v in (values_x, values_a)], axis=0
    )
    STS[...] = jnp.broadcast_to(to_row(squares), (8, 128))
    pl.semaphore_wait(barrier, 23)
    for d in range(15):
        px, ph, pc = tp(d, 1)
        send(STS, ST.at[d], s_sts.at[d], s_str.at[0], x=px, h=ph, c=pc)

    for d in range(7):
        pz, q = zl(d, 1)
        send(hid_in, XR.at[r], s_xs.at[d], s_xr.at[d], z=pz, l=q)

    def ring(index, sets, places, me):
        prv, nxt = lax.rem(me + 3, 4), lax.rem(me + 1, 4)
        opp = lax.rem(me + 2, 4)
        lo, hi = pl.ds(0, 32), pl.ds(32, 32)
        full = pl.ds(0, 64)

        def pass_on(p, rows, q, n):
            send_set(
                lambda: sets(p, rows), s_rings.at[index, n], s_ringr.at[index, n], lambda: places(q)
            )

        def start():
            pass_on(me, full, nxt, 0)
            pass_on(me, full, prv, 1)

        def pass_next():
            recv(sets(prv, full), s_ringr.at[index, 0])
            pass_on(prv, lo, nxt, 2)

        def pass_prev():
            recv(sets(nxt, full), s_ringr.at[index, 1])
            pass_on(nxt, hi, prv, 3)

        def finish():
            recv(sets(opp, lo), s_ringr.at[index, 2])
            recv(sets(opp, hi), s_ringr.at[index, 3])

        return start, pass_next, pass_prev, finish, (me, prv, nxt, opp)

    def spread(index, sets, places, me):
        full = pl.ds(0, 64)

        def to(d):
            send_set(
                lambda: sets(me, full), s_rings.at[index, d], s_ringr.at[index, d],
                lambda: places(lax.rem(me + d, 4)),
            )

        def start():
            for d in (1, 3, 2):
                to(d)

        def finish():
            for d in (1, 3, 2):
                recv(sets(lax.rem(me + 4 - d, 4), full), s_ringr.at[index, d])

        return start, finish

    def y_place(p):
        return dict(h=lax.div(p, 2), l=lax.rem(p, 2))

    every4, every2 = pl.ds(0, 4), pl.ds(0, 2)

    def rings_x_y_z(ref, cols, first_index, split=False):
        a = ring(first_index, lambda p, k: ref.at[p, h, c, z, l, k, cols], lambda p: dict(x=p), x)
        bb = ring(
            first_index + 1,
            lambda p, k: ref.at[every4, lax.div(p, 2), c, z, lax.rem(p, 2), k, cols], y_place, y,
        )
        if split:
            def d(yy, n):
                return ring(
                    first_index + 6 + n,
                    lambda p, k: ref.at[every4, lax.div(yy, 2), c, p, lax.rem(yy, 2), k, cols],
                    lambda p: dict(z=p), z,
                )
        else:
            d = ring(
                first_index + 2,
                lambda p, k: ref.at[every4, every2, c, p, every2, k, cols], lambda p: dict(z=p), z,
            )
        return a, bb, d

    def rings_z_y_x(ref, cols, first_index):
        a = ring(first_index, lambda p, k: ref.at[x, h, c, p, l, k, cols], lambda p: dict(z=p), z)
        bb = ring(
            first_index + 1,
            lambda p, k: ref.at[x, lax.div(p, 2), c, every4, lax.rem(p, 2), k, cols], y_place, y,
        )

        def d(yy, n):
            return ring(
                first_index + 6 + n,
                lambda p, k: ref.at[p, lax.div(yy, 2), c, every4, lax.rem(yy, 2), k, cols],
                lambda p: dict(x=p), x,
            )

        return a, bb, d

    def a_set(ref, cc, p, cols):
        return ref.at[every4, every2, cc, p, every2, pl.ds(0, 64), cols]

    def b_set(ref, cc, p, cols):
        return ref.at[p, every2, cc, every4, every2, pl.ds(0, 64), cols]

    def to_core(ref, maker, p, cols, index, n):
        send_set(
            lambda: maker(ref, c, p, cols), s_fs.at[index, n], s_fr.at[index, n], lambda: dict(c=sib)
        )

    def from_other(ref, maker, p, cols, index, n):
        recv(maker(ref, sib, p, cols), s_fr.at[index, n])

    recv(ST, s_str.at[0])
    total = STS[...]
    for d in range(15):
        total += ST[d]
    lane = lax.broadcasted_iota(jnp.int32, (8, 128), 1)
    means = jnp.where(lane < BLOCK, total / DE, total / DA)
    FS[...] = lax.rsqrt(means + norm_epsilon)
    for d in range(7):
        pz, q = zl(d, 1)
        send(FS, FR.at[d], s_frs.at[d], s_frr.at[0], z=pz, l=q)
    for j in (0, 4, 1, 5, 2, 6, 3):
        for i, ref in enumerate((gate, up)):
            send(
                ref.at[:, wcols(sib, j)], wpart(j, c, i),
                s_ws.at[j, i], s_wr.at[j, i], c=sib,
            )
    own_factors = to_column(FS[0:1, :])

    FA[x, h, c, z, l] = (values_a * own_factors[BLOCK:] * AG[...]).astype(BF16)
    ama_cols = pl.ds(0, KAMA)
    ama = rings_x_y_z(FA, ama_cols, 0)
    ama_x = spread(
        0, lambda p, k: FA.at[p, h, c, z, l, k, ama_cols], lambda p: dict(x=p), x
    )
    ama_y = spread(
        1, lambda p, k: FA.at[every4, lax.div(p, 2), c, z, lax.rem(p, 2), k, ama_cols], y_place, y
    )
    ama_x[0]()

    def take_rows(rr, d, factors):
        XG[c, rr] = (XR[rr].astype(F32) * factors[:BLOCK] * PG[...]).astype(BF16)
        send(XG.at[c, rr], XG.at[c, rr], s_bs.at[d], s_br.at[d], c=sib)

    take_rows(r, 7, own_factors)
    for cp in late:
        cp.start()
    recv(FR, s_frr.at[0])
    for d in range(7):
        pz, q = zl(d, -1)
        rr = pz * 2 + q
        recv(XR.at[rr], s_xr.at[d])
        take_rows(rr, d, to_column(FR[d, 0:1, :]))

    ama_x[1]()
    ama_y[0]()

    for d in range(7):
        pz, q = zl(d, -1)
        recv(XG.at[sib, pz * 2 + q], s_br.at[d])
    recv(XG.at[sib, r], s_br.at[7])

    gates, ups = pl.ds(0, CHUNK), pl.ds(CHUNK, CHUNK)

    def piece(j, p, cols, xfirst):
        return PB.at[j, p, :, :, cols] if xfirst else YR.at[j - XFIRST, p, :, cols]

    def slot(ref, j, n, xfirst):
        return ref.at[j, n] if xfirst else ref.at[j, n, 0]

    def slots(ref, j, xfirst):
        return ref.at[j] if xfirst else ref.at[j, :, 0]

    def first_sends(j, xfirst):
        for p, cols, ref, n, k, to in (
            (xo, gates, M1, 0, 0, xn), (xo, ups, M1, 1, 0, xp),
            (xn, ups, SR, 0, 1, xn), (xp, gates, SR, 1, 1, xp),
        ):
            go(piece(j, p, cols, xfirst), slot(ref, j, n, xfirst), s_rs.at[j, 0], s_rr.at[j, k], x=to)

    def product(j):
        for i, ref in enumerate((gate, up)):
            wlocal(j, i, ref).wait()
            recv(wpart(j, sib, i), s_wr.at[j, i])

        def block(q, _):
            quad = pl.ds(q * 4, 4)
            lhs = jnp.concatenate([XG[k, quad].reshape(256, KDIM) for k in range(2)], axis=1)
            PB[j, pl.ds(q * 2, 2)] = dot(lhs, W[j]).astype(BF16).reshape(2, 2, BLOCK, 2 * CHUNK)
            return 0

        lax.fori_loop(0, 2, block, 0)

    def products(i, _):
        product(i)
        first_sends(i, True)

        @pl.when(i < YFIRST)
        def _():
            j = i + XFIRST
            product(j)
            go(PB.at[j, :, 1 - h], YR.at[i], s_rs.at[j, 2], s_rr.at[j, 2], h=1 - h)

        return 0

    lax.fori_loop(0, XFIRST, products, 0)


    ids = t * WIDE + r * (16 * WIDE) + lax.broadcasted_iota(jnp.int32, (16, WIDE), 1)
    per_prompt = jnp.zeros((16, WIDE), F32)
    for k in range(24):
        per_prompt += (picks[:, k : k + 1] == ids).astype(F32)
    chosen = (lax.broadcasted_iota(jnp.int32, (16, ROWS), 0) == prompt[...]).astype(F32)
    CNT[...] = lax.dot_general(
        chosen.astype(BF16), per_prompt.astype(BF16), (((0,), (0,)), ((), ())),
        preferred_element_type=F32,
    )

    ama_y[1]()
    ama[2][0]()

    def add_and_pass(j, xfirst):
        recv(slots(M1, j, xfirst), s_rr.at[j, 0])
        for n, p, cols in ((0, xn, gates), (1, xp, ups)):
            ref = slot(M1, j, n, xfirst)
            ref[...] = (ref[...].astype(F32) + piece(j, p, cols, xfirst)[...].astype(F32)).astype(BF16)
            go(ref, slot(SR, j, n + 2, xfirst), s_rs.at[j, 1], s_rr.at[j, 1], x=p)

    def ring_sums(j, xfirst):
        recv(slots(SR, j, xfirst), s_rr.at[j, 1])
        terms = [slot(SR, j, n, xfirst)[...].astype(F32) for n in range(4)]
        g = piece(j, x, gates, xfirst)[...].astype(F32) + terms[1] + terms[2]
        u = piece(j, x, ups, xfirst)[...].astype(F32) + terms[0] + terms[3]
        return g, u

    def put_hidden(j, g, u):
        HID[c, j, x, h] = (g / (1.0 + jnp.exp(-g)) * u).astype(BF16)

    def around(j, own):
        go(own, own, s_hs.at[j, 1], s_hr.at[j, 1], x=xn)
        go(own, own, s_hs.at[j, 1], s_hr.at[j, 2], x=xp)

    def halves_on(j, blocks):
        for p, q, n, first_row in ((xp, xn, 1, 0), (xn, xp, 2, 32)):
            recv(blocks(p, pl.ds(0, BLOCK)), s_hr.at[j, n])
            part = blocks(p, pl.ds(first_row, 32))
            go(part, part, s_hs.at[j, 2], s_hr.at[j, 3], x=q)

    def core_copy(j):
        return remote(HID.at[c, j], HID.at[c, j], s_cs.at[j], s_cr.at[j], c=sib)

    def use_chunk(j):
        recv(HID.at[sib, j], s_cr.at[j])

        def block(q, _):
            rows = pl.ds(aligned(q * 256, 256), 256)
            pair = pl.ds(q * 2, 2)
            lhs = jnp.concatenate([HID[k, j, pair].reshape(256, CHUNK) for k in range(2)], axis=1)
            rhs = jnp.concatenate(
                [DOWN[pl.ds(aligned(k * HALF + j * CHUNK, CHUNK), CHUNK), :] for k in range(2)], axis=0
            )
            ACC[rows, :] += dot(lhs, rhs)
            return 0

        lax.fori_loop(0, 2, block, 0)

    def x0(j):
        add_and_pass(j, True)

    def x1(j):
        g, u = ring_sums(j, True)
        T[j, :, :, gates] = g
        T[j, :, :, ups] = u
        HS[j] = T[j, 1 - h].astype(BF16)
        go(HS.at[j], HR.at[j], s_rs.at[j, 2], s_rr.at[j, 2], h=1 - h)

    def x2(j):
        recv(HR.at[j], s_rr.at[j, 2])
        both = T[j, h] + HR[j].astype(F32)
        put_hidden(j, both[:, :CHUNK], both[:, CHUNK:])
        own = HID.at[c, j, x, h]
        go(own, own, s_hs.at[j, 0], s_hr.at[j, 0], h=1 - h)

    def x3(j):
        recv(HID.at[c, j, x, 1 - h], s_hr.at[j, 0])
        around(j, HID.at[c, j, x])

    def x4(j):
        halves_on(j, lambda p, rows: HID.at[c, j, p, :, rows])

    def x5(j):
        recv(HID.at[c, j, xo], s_hr.at[j, 3])
        core_copy(j).start()

    def y0(i):
        j = i + XFIRST
        recv(YR.at[i], s_rr.at[j, 2])
        YR[i] = (YR[i].astype(F32) + PB[j, :, h].astype(F32)).astype(BF16)
        first_sends(j, False)

    def y1(i):
        add_and_pass(i + XFIRST, False)

    def y2(i):
        j = i + XFIRST
        g, u = ring_sums(j, False)
        put_hidden(j, g, u)
        around(j, HID.at[c, j, x, h])

    def y3(i):
        j = i + XFIRST
        halves_on(j, lambda p, rows: HID.at[c, j, p, h, rows])

    def y4(i):
        j = i + XFIRST
        recv(HID.at[c, j, xo, h], s_hr.at[j, 3])
        got = HID.at[c, j, :, h]
        go(got, got, s_hs.at[j, 0], s_hr.at[j, 0], h=1 - h)

    def y5(i):
        j = i + XFIRST
        recv(HID.at[c, j, :, 1 - h], s_hr.at[j, 0])
        core_copy(j).start()

    def y6(i):
        use_chunk(i + XFIRST)

    xstages = (x0, x1, x2, x3, x4, x5, use_chunk)
    ystages = (y0, y1, y2, y3, y4, y5, y6)
    ACC[...] = jnp.zeros_like(ACC)
    late[0].wait()
    a_places = ama[2][4]

    def stages(n, _):
        for k in reversed(range(7)):
            for many, steps in ((YFIRST, ystages), (XFIRST, xstages)):
                pl.when((n - k >= 0) & (n - k < many))(functools.partial(steps[k], n - k))

        return 0

    lax.fori_loop(0, 5, stages, 0)
    ama[2][1]()
    ama[2][2]()
    lax.fori_loop(5, 8, stages, 0)
    ama[2][3]()
    for k in range(4):
        to_core(FA, a_set, a_places[k], ama_cols, 0, k)
    lax.fori_loop(8, XFIRST + 6, stages, 0)

    for q in range(8):
        OB[q] = ACC[q * BLOCK : (q + 1) * BLOCK, :].astype(BF16)
    early = sends + later
    sends.clear()
    later.clear()
    for d in range(7):
        pz, q = zl(d, 1)
        send(OB.at[pz * 2 + q], OR.at[d], s_os.at[d], s_or.at[0], z=pz, l=q)

    settle(early)

    def drain(j, _):
        def sent(region, sem):
            remote(region, region, sem, sem, c=sib).wait_send()

        @pl.when(j < XFIRST)
        def _():
            sent(SR.at[j], s_rs.at[j, 0])
            sent(M1.at[j], s_rs.at[j, 1])
            sent(HR.at[j], s_rs.at[j, 2])
            sent(HID.at[c, j, x, h], s_hs.at[j, 0])
            sent(HID.at[c, j, pl.ds(0, 2)], s_hs.at[j, 1])
            sent(HID.at[c, j, x], s_hs.at[j, 2])

        @pl.when(j >= XFIRST)
        def _():
            sent(SR.at[j, :, 0], s_rs.at[j, 0])
            sent(M1.at[j, :, 0], s_rs.at[j, 1])
            sent(YR.at[j - XFIRST], s_rs.at[j, 2])
            sent(HID.at[c, j, :, h], s_hs.at[j, 0])
            sent(HID.at[c, j, x], s_hs.at[j, 1])
            sent(HID.at[c, j, x, h], s_hs.at[j, 2])

        core_copy(j).wait_send()
        return 0

    lax.fori_loop(0, CHUNKS, drain, 0)

    late[1].wait()
    for n in range(4):
        from_other(FA, a_set, a_places[n], ama_cols, 0, n)

    def ama_block(q, _):
        rows = pl.ds(aligned(q * 256, 256), 256)
        LA[rows, :] = jnp.zeros((256, WIDE), F32)

        def part(k, _):
            lhs = jnp.concatenate(
                [FA[k, n // 2, n % 2, pl.ds(q * 2, 2)].reshape(256, KAMA) for n in range(4)], axis=1
            )
            LA[rows, :] += dot(lhs, AHEAD[pl.ds(aligned(k * 4 * KAMA, 4 * KAMA), 4 * KAMA), :])
            return 0

        lax.fori_loop(0, 4, part, 0)
        return 0

    lax.fori_loop(0, 2, ama_block, 0)

    vmask = valid[...].astype(F32)
    half_valid = contrast_weight * vmask
    for q in range(4):
        rows = pl.ds(q * 128, 128)
        ls = to_column(lscale[q : q + 1, :])
        RE[1, rows, :] = jnp.broadcast_to(ls, (128, 128))
        la = LA[rows, :] * ls
        ma = jnp.max(la, axis=1, keepdims=True)
        sa = jnp.sum(jnp.exp(la - ma), axis=1, keepdims=True)
        AST[0:1, rows] = to_row(ma)
        AST[1:2, rows] = to_row(sa)
        LA[rows, :] = half_valid * la + hamming_weight * CNT[rows, :]


    layer = values_x + ACC[pl.ds(aligned(r * BLOCK, BLOCK), BLOCK), :]
    recv(OR, s_or.at[0])
    for d in range(7):
        layer += OR[d].astype(F32)
    FE[x, h, c, z, l] = (layer * OG[...]).astype(BF16)

    low, high = pl.ds(0, 256), pl.ds(256, 256)
    one = rings_x_y_z(FE, low, 3, split=True)
    two = rings_z_y_x(FE, high, 7)
    one_first = spread(3, lambda p, k: FE.at[p, h, c, z, l, k, low], lambda p: dict(x=p), x)
    two_first = spread(7, lambda p, k: FE.at[x, h, c, p, l, k, high], lambda p: dict(z=p), z)
    one_first[0]()
    two_first[0]()

    squares = jnp.sum(layer * layer, axis=1, keepdims=True)
    squares = jnp.concatenate([squares, squares], axis=0)
    SFS[...] = jnp.broadcast_to(to_row(squares), (8, 128))
    for d in range(15):
        px, ph, pc = tp(d, 1)
        send(SFS, SF.at[d], s_sfs.at[d], s_sfr.at[0], x=px, h=ph, c=pc)

    y_order = one[1][4]
    last_one = [one[2](p, n) for n, p in enumerate(y_order)]
    last_two = [two[2](p, n) for n, p in enumerate(y_order)]
    for g, n, e in ((one_first, one[1], last_one), (two_first, two[1], last_two)):
        g[1]()
        n[0]()
        e[0][0]()
    for k in (1, 2):
        for n, e in ((one[1], last_one), (two[1], last_two)):
            n[k]()
            e[k][0]()

    recv(SF, s_sfr.at[0])
    total = SFS[...]
    for d in range(15):
        total += SF[d]
    SGS[...] = total
    for d in range(7):
        pz, q = zl(d, 1)
        send(SGS, SG.at[d], s_sgs.at[d], s_sgr.at[0], z=pz, l=q)

    for n, e in ((one[1], last_one), (two[1], last_two)):
        n[3]()
        e[3][0]()
    to_core(FE, a_set, z, low, 1, 0)
    to_core(FE, b_set, x, high, 2, 0)
    late[2].wait()
    late[3].wait()
    LE[...] = jnp.zeros_like(LE)

    def use_a(p):
        def part(k, _):
            lhs = jnp.concatenate(
                [FE[k, n // 2, n % 2, p, :, :, 0:256].reshape(128, 256) for n in range(4)], axis=1
            )
            rows = pl.ds(aligned(p * 128, 128), 128)
            LE[rows, :] += dot(lhs, HEADA[pl.ds(k * 4, 4)].reshape(1024, WIDE))
            return 0

        lax.fori_loop(0, 4, part, 0)

    def use_b(p):
        def part(q, _):
            pair = pl.ds(q * 2, 2)
            lhs = jnp.concatenate(
                [FE[p, n // 2, n % 2, pair, :, :, 256:512].reshape(256, 256) for n in range(4)], axis=1
            )
            rows = pl.ds(aligned(q * 256, 256), 256)
            LE[rows, :] += dot(lhs, HEADB[pl.ds(p * 4, 4)].reshape(1024, WIDE))
            return 0

        lax.fori_loop(0, 2, part, 0)

    za, xb = last_one[0][4], last_two[0][4]
    for n in range(4):
        for e in (last_one, last_two):
            e[n][1]()
            e[n][2]()
        if n == 1:
            from_other(FE, a_set, z, low, 1, 0)
            use_a(z)
            from_other(FE, b_set, x, high, 2, 0)
            use_b(x)
    for n in (1, 2):
        to_core(FE, a_set, za[n], low, 1, n)
        to_core(FE, b_set, xb[n], high, 2, n)
    for n in (1, 2):
        from_other(FE, a_set, za[n], low, 1, n)
        use_a(za[n])
        from_other(FE, b_set, xb[n], high, 2, n)
        use_b(xb[n])

    recv(SG, s_sgr.at[0])

    def row_factors(rr, line):
        rows = pl.ds(aligned(rr * BLOCK, BLOCK), BLOCK)
        col = lax.rsqrt(to_column(line)[:BLOCK] / DE + norm_epsilon)
        RE[0, rows, :] = col * RE[1, rows, :]

    row_factors(r, SGS[0:1, :])
    for d in range(7):
        pz, q = zl(d, -1)
        row_factors(pz * 2 + q, SG[d, 0:1, :])

    def a_group(n):
        return lambda ref, cc, p, cols: ref.at[
            every4, lax.div(y_order[n], 2), cc, p, lax.rem(y_order[n], 2), pl.ds(0, 64), cols
        ]

    def b_group(n):
        return lambda ref, cc, p, cols: ref.at[
            p, lax.div(y_order[n], 2), cc, every4, lax.rem(y_order[n], 2), pl.ds(0, 64), cols
        ]

    settle(sends)
    for n in range(4):
        last_one[n][3]()
        to_core(FE, a_group(n), za[3], low, 3, n)
        last_two[n][3]()
        to_core(FE, b_group(n), xb[3], high, 4, n)
    for n in range(4):
        from_other(FE, a_group(n), za[3], low, 3, n)
        from_other(FE, b_group(n), xb[3], high, 4, n)
    use_a(za[3])
    use_b(xb[3])

    for q in range(4):
        rows = pl.ds(q * 128, 128)
        le = LE[rows, :] * RE[0, rows, 0:1]
        me = jnp.max(le, axis=1, keepdims=True)
        se = jnp.sum(jnp.exp(le - me), axis=1, keepdims=True)
        raw = le - LA[rows, :]
        LE[rows, :] = raw
        local(LE.at[rows], raw_out.at[rows], s_out.at[q]).start()
        used = jnp.broadcast_to(vmask, raw.shape) > 0.5
        m1 = jnp.max(jnp.where(used, raw, LOWEST), axis=1, keepdims=True)
        m0 = jnp.max(jnp.where(used, LOWEST, raw), axis=1, keepdims=True)
        line_e, line_s, line_1, line_0 = (to_row(v) for v in (me, se, m1, m0))
        lines = [line_e, line_s, AST[0:1, rows], AST[1:2, rows], line_1, line_0, line_e, line_e]
        SBUF[0, x * 2 + c, :, rows] = jnp.concatenate(lines, axis=0)

    def merge(parts):
        me = functools.reduce(jnp.maximum, [p[0:1] for p in parts])
        ma = functools.reduce(jnp.maximum, [p[2:3] for p in parts])
        se = sum(p[1:2] * jnp.exp(p[0:1] - me) for p in parts)
        sa = sum(p[3:4] * jnp.exp(p[2:3] - ma) for p in parts)
        m1 = functools.reduce(jnp.maximum, [p[4:5] for p in parts])
        m0 = functools.reduce(jnp.maximum, [p[5:6] for p in parts])
        return jnp.concatenate([me, se, ma, sa, m1, m0, me, me], axis=0)

    mine = SBUF.at[0, x * 2 + c]
    for d in range(1, 8):
        send(
            mine, mine, s_qs.at[0, d], s_qr.at[0, d],
            x=lax.rem(x + d // 2, 4), c=lax.rem(c + d % 2, 2),
        )
    settle(later)
    for d in range(1, 8):
        px, pc = lax.rem(x + 4 - d // 2, 4), lax.rem(c + d % 2, 2)
        recv(SBUF.at[0, px * 2 + pc], s_qr.at[0, d])
    merged = merge([SBUF[0, k] for k in range(8)])
    for phase, (me, place) in enumerate(
        ((y, y_place), (z, lambda p: dict(z=p))), start=1
    ):
        SBUF[phase, me] = merged
        mine = SBUF.at[phase, me]
        for d in range(1, 4):
            send(mine, mine, s_qs.at[phase, d], s_qr.at[phase, d], **place(lax.rem(me + d, 4)))
        for d in range(1, 4):
            recv(SBUF.at[phase, lax.rem(me + 4 - d, 4)], s_qr.at[phase, d])
        merged = merge([SBUF[phase, k] for k in range(4)])

    stats_out[...] = merged
    for q in range(4):
        rows = pl.ds(q * 128, 128)
        local(LE.at[rows], raw_out.at[rows], s_out.at[q]).wait()

    settle(sends, later)


def finish(raw, stats, valid, scores, best):
    shift_e = stats[0:1, :] + jnp.log(stats[1:2, :])
    shift_a = stats[2:3, :] + jnp.log(stats[3:4, :])
    best[...] = jnp.maximum(
        stats[4:5, :] - shift_e + contrast_weight * shift_a, stats[5:6, :] - shift_e
    )
    half_valid = contrast_weight * valid[...].astype(F32)
    for q in range(4):
        rows = slice(q * 128, (q + 1) * 128)
        back = half_valid * to_column(shift_a[:, rows]) - to_column(shift_e[:, rows])
        scores[rows, :] = raw[rows, :] + back


def body(
    exp_hidden, exp_pre_gain, exp_gate, exp_up, exp_down, exp_out_gain, exp_head,
    ama_hidden, ama_out_gain, ama_head, logit_scale, prompt_of, prior_picks, valid_mask,
):
    hbm = pl.BlockSpec(memory_space=pl.ANY)
    vmem = pl.BlockSpec(memory_space=pltpu.VMEM)
    dma = pltpu.SemaphoreType.DMA
    scratch = [
        pltpu.VMEM((8, BLOCK, KDIM), BF16),
        pltpu.VMEM((2, 8, BLOCK, KDIM), BF16),
        pltpu.VMEM((CHUNKS, 2 * KDIM, 2 * CHUNK), BF16),
        pltpu.VMEM((2 * HALF, KDIM), BF16),
        pltpu.VMEM((16, 256, WIDE), BF16),
        pltpu.VMEM((16, 256, WIDE), BF16),
        pltpu.VMEM((DA, WIDE), BF16),
        pltpu.VMEM((CHUNKS, 4, 2, BLOCK, 2 * CHUNK), BF16),
        pltpu.VMEM((CHUNKS, 2, 2, BLOCK, CHUNK), BF16),
        pltpu.VMEM((CHUNKS, 4, 2, BLOCK, CHUNK), BF16),
        pltpu.VMEM((XFIRST, 2, BLOCK, 2 * CHUNK), F32),
        pltpu.VMEM((XFIRST, BLOCK, 2 * CHUNK), BF16),
        pltpu.VMEM((XFIRST, BLOCK, 2 * CHUNK), BF16),
        pltpu.VMEM((YFIRST, 4, BLOCK, 2 * CHUNK), BF16),
        pltpu.VMEM((2, CHUNKS, 4, 2, BLOCK, CHUNK), BF16),
        pltpu.VMEM((ROWS, KDIM), F32),
        pltpu.VMEM((8, BLOCK, KDIM), BF16),
        pltpu.VMEM((7, BLOCK, KDIM), BF16),
        pltpu.VMEM((4, 2, 2, 4, 2, BLOCK, KDIM), BF16),
        pltpu.VMEM((4, 2, 2, 4, 2, BLOCK, KAMA), BF16),
        pltpu.VMEM((BLOCK, KAMA), BF16),
        pltpu.VMEM((ROWS, WIDE), F32),
        pltpu.VMEM((ROWS, WIDE), F32),
        pltpu.VMEM((8, 128), F32),
        pltpu.VMEM((15, 8, 128), F32),
        pltpu.VMEM((8, 128), F32),
        pltpu.VMEM((7, 8, 128), F32),
        pltpu.VMEM((8, 128), F32),
        pltpu.VMEM((15, 8, 128), F32),
        pltpu.VMEM((8, 128), F32),
        pltpu.VMEM((7, 8, 128), F32),
        pltpu.VMEM((2, ROWS, 128), F32),
        pltpu.VMEM((ROWS, WIDE), F32),
        pltpu.VMEM((3, 8, 8, ROWS), F32),
        pltpu.VMEM((8, ROWS), F32),
        pltpu.VMEM((1, KDIM), F32),
        pltpu.VMEM((1, KDIM), F32),
        pltpu.VMEM((1, KAMA), F32),
        dma((9,)), dma((CHUNKS, 2)), dma((CHUNKS, 2)), dma((CHUNKS, 2)),
        dma((7,)), dma((7,)), dma((8,)), dma((8,)), dma((15,)), dma((1,)), dma((7,)), dma((1,)),
        dma((CHUNKS, 3)), dma((CHUNKS, 3)), dma((CHUNKS, 3)), dma((CHUNKS, 4)),
        dma((CHUNKS,)), dma((CHUNKS,)), dma((7,)), dma((1,)),
        dma((17, 4)), dma((17, 4)), dma((5, 4)), dma((5, 4)),
        dma((15,)), dma((1,)), dma((7,)), dma((1,)), dma((3, 8)), dma((3, 8)), dma((4,)),
    ]
    raw, stats = pl.pallas_call(
        kernel,
        out_shape=(
            jax.ShapeDtypeStruct((ROWS, WIDE), F32),
            jax.ShapeDtypeStruct((8, ROWS), F32),
        ),
        in_specs=[hbm] * 10 + [vmem] * 4,
        out_specs=(hbm, vmem),
        scratch_shapes=scratch,
        compiler_params=pltpu.CompilerParams(
            collective_id=0, has_side_effects=True, vmem_limit_bytes=63 * 1024 * 1024
        ),
        cost_estimate=pl.CostEstimate(
            flops=12_000_000_000, bytes_accessed=25_000_000, transcendentals=600_000
        ),
    )(
        exp_hidden, exp_pre_gain.reshape(1, KDIM), exp_gate, exp_up, exp_down,
        exp_out_gain.reshape(1, KDIM), exp_head.reshape(16, KDIM, WIDE), ama_hidden, ama_out_gain.reshape(1, KAMA),
        ama_head, logit_scale.reshape(4, 128), prompt_of.reshape(1, ROWS), prior_picks,
        valid_mask.reshape(1, WIDE),
    )
    scores, best = pl.pallas_call(
        finish,
        out_shape=(
            jax.ShapeDtypeStruct((ROWS, WIDE), F32),
            jax.ShapeDtypeStruct((1, ROWS), F32),
        ),
        in_specs=[vmem] * 3,
        out_specs=(vmem, vmem),
    )(raw, stats, valid_mask.reshape(1, WIDE))
    return scores, best.reshape(ROWS)


def solution(mesh):
    torus = Mesh(mesh.devices.reshape(4, 2, 4, 2, 2), AXES)
    in_specs = (
        P(REP, TP), P(TP), P(TP, REP), P(TP, REP), P(REP, TP), P(TP), P(None, ALL),
        P(REP, TP), P(TP), P(None, ALL), P(), P(), P(), P(ALL),
    )
    out_specs = (P(None, ALL), P())
    return jax.shard_map(body, mesh=torus, in_specs=in_specs, out_specs=out_specs, check_vma=False)
```
